32 devices in a mesh: row: 4 (over y, core), col: 8 (over z, x).
Axes of the slice: x: 2, y: 2, z: 4, core: 2. Of those that a mesh axis runs over, the one named last changes fastest.
Arguments:
- features: bfloat16 [262144, 400], P(('row', 'col')), may hold values from -110 to 110
- labels: int32 [262144], P(('row', 'col')), may hold values from 0 to 46
- counts: int32 [4, 8], replicated, may hold values from 1 to 8192, as said below
- w_branch: float32 [4, 100, 512], replicated, may hold values from -0.625 to 0.625
- w_mid: float32 [2048, 512], P(('row', 'col')), may hold values from -0.125 to 0.125
- w_out: float32 [512, 47], replicated, may hold values from -0.25 to 0.25
- left_branch: float32 [4, 100, 100], replicated, may hold values from -5.9604645e-08 to 5.9604645e-08
- right_branch: float32 [4, 512, 512], replicated, may hold values from -1.1175871e-08 to 1.1175871e-08
- basis_left_branch: float32 [4, 100, 100], replicated, may hold values from -1 to 1, as said below
- basis_right_branch: float32 [4, 512, 512], replicated, may hold values from -1 to 1, as said below
- first_branch: float32 [4, 100, 512], replicated, may hold values from -0.00012207031 to 0.00012207031
- second_branch: float32 [4, 100, 512], replicated, may hold values from 2.0599366e-11 to 3.3569336e-10
- right_mid: float32 [512, 512], replicated, may hold values from -4.7683716e-06 to 4.7683716e-06
- basis_right_mid: float32 [512, 512], replicated, may hold values from -1 to 1, as said below
- first_mid: float32 [2048, 512], P(('row', 'col')), may hold values from -0.00048828125 to 0.00048828125
- second_mid: float32 [2048, 512], P(('row', 'col')), may hold values from 3.8146972e-10 to 6.1035155e-09
- left_out: float32 [512, 512], replicated, may hold values from -9.536743e-07 to 9.536743e-07
- right_out: float32 [47, 47], replicated, may hold values from -9.536743e-06 to 9.536743e-06
- basis_left_out: float32 [512, 512], replicated, may hold values from -1 to 1, as said below
- basis_right_out: float32 [47, 47], replicated, may hold values from -1 to 1, as said below
- first_out: float32 [512, 47], replicated, may hold values from -0.0014648438 to 0.0014648438
- second_out: float32 [512, 47], replicated, may hold values from 3.4332275e-09 to 5.493164e-08
Outputs:
- logits: float32 [131072, 47], P(('row', 'col'))
- grad_features: bfloat16 [262144, 400], P(('row', 'col'))
- new_left_branch: float32 [4, 100, 100], replicated
- new_right_branch: float32 [4, 512, 512], replicated
- new_first_branch: float32 [4, 100, 512], replicated
- new_second_branch: float32 [4, 100, 512], replicated
- new_w_branch: float32 [4, 100, 512], replicated
- low_w_branch: bfloat16 [4, 100, 512], replicated
- new_right_mid: float32 [512, 512], replicated
- new_first_mid: float32 [2048, 512], P(('row', 'col'))
- new_second_mid: float32 [2048, 512], P(('row', 'col'))
- new_w_mid: float32 [2048, 512], P(('row', 'col'))
- low_w_mid: bfloat16 [2048, 512], P(('row', 'col'))
- new_left_out: float32 [512, 512], replicated
- new_right_out: float32 [47, 47], replicated
- new_first_out: float32 [512, 47], replicated
- new_second_out: float32 [512, 47], replicated
- new_w_out: float32 [512, 47], replicated
- low_w_out: bfloat16 [512, 47], replicated
The draws below stay inside these ranges and needn't reach their ends.
Inputs may be any that keep to these rules, and one draw needn't show every extreme that they name: `counts`: each row sums to 32768; exactly one entry of each row equals 8192. `basis_left_branch`: each matrix is orthogonal. `basis_right_branch`: each matrix is orthogonal. `basis_right_mid`: orthogonal. `basis_left_out`: orthogonal. `basis_right_out`: orthogonal.
All inputs are finite; a program needn't handle non-finite values.
Results may differ from the reference program's by a relative error of at most 0.0089.
Values may be sent and summed in bfloat16 or wider, within the bound.
No kernel may reach another device: no remote copies, remote signals or barrier semaphores. Data moves between devices by JAX's collectives and lax.ppermute only.
A program may use at most 320 MiB of HBM per device.

```python
import math
import jax
import jax.numpy as jnp
from jax import lax

OPS = 4
DIN = 100
HID = 512
CLS = 47
AVG = 4096
STEP = 5
CAT = 2048
CAP = 8192
GROUPS = 4
PEERS = 8
DEVICES = 32


def signed_cosines(key, stacked, length):
    sign_key, perm_key = jax.random.split(key)
    sign_values = jnp.where(jax.random.bernoulli(sign_key, 0.5, (stacked, length, 1)), 1.0, -1.0)
    frequency = jax.vmap(lambda perm_seed: jax.random.permutation(perm_seed, length))(jax.random.split(perm_key, stacked))
    frequency = frequency.astype(jnp.float32)[:, None, :]
    row_index = jnp.arange(length, dtype=jnp.float32)[None, :, None] + 0.5
    norm_value = jnp.where(frequency == 0.0, jnp.sqrt(1.0 / length), jnp.sqrt(2.0 / length))
    cosine_table = jnp.cos(jnp.pi * row_index * frequency / length) * norm_value
    return (sign_values * cosine_table).astype(jnp.float32)


def draw_features(key, part):
    key = jax.random.fold_in(key, 11)
    base_key, column_key, rough_key = jax.random.split(key, 3)
    all_slots = DEVICES * CAP
    position = jnp.arange(all_slots, dtype=jnp.float32) / (all_slots - 1)
    base_values = jnp.clip(jax.random.normal(base_key, (all_slots, OPS * DIN)), -6.0, 6.0)
    rise_scale = 1.0 + 2.0 * position
    column_scale = jnp.exp(jax.random.uniform(column_key, (OPS * DIN,), minval=0.0, maxval=1.3862944))
    rough_scale = jnp.exp(jax.random.uniform(rough_key, (all_slots, 1), minval=-0.35, maxval=0.35))
    return (base_values * rise_scale[:, None] * column_scale[None, :] * rough_scale).astype(jnp.bfloat16)


def draw_counts(key, part):
    key = jax.random.fold_in(key, 23)
    light_key, full_key, take_key, flip_key = jax.random.split(key, 4)
    half = PEERS // 2
    light = jax.random.randint(light_key, (GROUPS, half), 1, max(AVG // 4, 1) + 1)
    full_at = jax.random.randint(full_key, (GROUPS, 1), 0, half)
    take_at = (full_at + 1 + jax.random.randint(take_key, (GROUPS, 1), 0, half - 1)) % half
    index = jnp.arange(half, dtype=jnp.int32)[None, :]
    taken = jnp.sum(jnp.where(index == full_at, light, 0), axis=1, keepdims=True)
    heavy = 2 * AVG - light
    heavy = jnp.where(index == full_at, CAP, heavy)
    heavy = jnp.where(index == take_at, heavy - taken, heavy)
    flip = jax.random.randint(flip_key, (GROUPS, 1), 0, 2)
    light_first = jnp.concatenate([light, heavy], axis=1)
    heavy_first = jnp.concatenate([heavy, light], axis=1)
    return jnp.where(flip == 1, heavy_first, light_first).astype(jnp.int32)


def draw_basis_left_branch(key, part):
    key = jax.random.fold_in(key, 31)
    return signed_cosines(key, OPS, DIN)


def draw_basis_right_branch(key, part):
    key = jax.random.fold_in(key, 37)
    return signed_cosines(key, OPS, HID)


def draw_basis_right_mid(key, part):
    key = jax.random.fold_in(key, 41)
    return signed_cosines(key, 1, HID)[0]


def draw_basis_left_out(key, part):
    key = jax.random.fold_in(key, 43)
    return signed_cosines(key, 1, HID)[0]


def draw_basis_right_out(key, part):
    key = jax.random.fold_in(key, 47)
    return signed_cosines(key, 1, CLS)[0]


def plant(drawn, key, smallest, high):
    place = [jax.random.randint(jax.random.fold_in(key, axis), (), 0, length) for axis, length in enumerate(drawn.shape)]
    main_axis = drawn.shape.index(max(drawn.shape))
    neighbour = place[:main_axis] + [(place[main_axis] + 1) % drawn.shape[main_axis]] + place[main_axis + 1:]
    return drawn.at[tuple(place)].set(smallest).at[tuple(neighbour)].set(high)


def shard_levels(own_key, dims, cuts, smallest, top_value):
    def one(dim, parts):
        steps = jax.random.uniform(jax.random.fold_in(jax.random.fold_in(own_key, 6), dim), (parts,), jnp.float32, smallest / len(cuts), top_value / len(cuts))
        return jnp.repeat(jnp.exp(steps), dims[dim] // parts).reshape((-1,) + (1,) * (len(dims) - dim - 1))

    gain = one(*cuts[0])
    for cut in cuts[1:]:
        gain = gain * one(*cut)
    return gain


def noise(own_key, dims, deviation, most, cuts=(), kind=jnp.bfloat16):
    gain = shard_levels(own_key, dims, cuts, -0.22, 0.18) if cuts else 1.0
    values = jax.random.normal(own_key, dims, jnp.float32) * deviation * gain
    return jnp.minimum(jnp.maximum(values, -most), most).astype(kind)


def setup_inputs(seed: int = 0) -> dict:
    arg_keys = jax.random.split(jax.random.key(seed), 23)
    features = draw_features(jax.random.fold_in(arg_keys[22], 71), 0)
    labels = plant(jax.random.randint(arg_keys[1], (DEVICES * CAP,), 0, CLS), jax.random.fold_in(arg_keys[1], 1), 0, CLS - 1).astype(jnp.int32)
    counts = draw_counts(jax.random.fold_in(arg_keys[22], 71), 0)
    w_branch = noise(arg_keys[3], (OPS, DIN, HID), DIN ** -0.5, 0.625, (), jnp.float32)
    w_mid = noise(arg_keys[4], (CAT, HID), CAT ** -0.5, 0.125, ((0, 32),), jnp.float32)
    w_out = noise(arg_keys[5], (HID, CLS), HID ** -0.5, 0.25, (), jnp.float32)
    left_branch = noise(arg_keys[6], (OPS, DIN, DIN), (0.0013 * (AVG * DEVICES) ** -1), 5.960464477539063e-08, (), jnp.float32)
    right_branch = noise(arg_keys[7], (OPS, HID, HID), (0.00026 * (AVG * DEVICES) ** -1), 1.1175870895385742e-08, (), jnp.float32)
    basis_left_branch = draw_basis_left_branch(jax.random.fold_in(arg_keys[22], 71), 0)
    basis_right_branch = draw_basis_right_branch(jax.random.fold_in(arg_keys[22], 71), 0)
    first_branch = noise(arg_keys[10], (OPS, DIN, HID), (0.007 * (AVG * DEVICES) ** -0.5), 0.00012207031, (), jnp.float32)
    second_branch = jnp.clip(jnp.exp(jax.random.uniform(arg_keys[11], (OPS, DIN, HID), jnp.float32, math.log(2.0599365962992167e-11), math.log(3.356933619969027e-10))), 2.0599365962992167e-11, 3.356933619969027e-10)
    right_mid = noise(arg_keys[12], (HID, HID), (0.098 * (AVG * DEVICES) ** -1), 4.76837158203125e-06, (), jnp.float32)
    basis_right_mid = draw_basis_right_mid(jax.random.fold_in(arg_keys[22], 71), 0)
    first_mid = noise(arg_keys[14], (CAT, HID), (0.03 * (AVG * DEVICES) ** -0.5), 0.00048828125, ((0, 32),), jnp.float32)
    second_mid = jnp.clip(jnp.exp(math.log(6.103515470812226e-09) - 2.7725887 * jax.random.uniform(arg_keys[15], (CAT, HID), jnp.float32) ** shard_levels(arg_keys[15], (CAT, HID), ((0, 32),), -0.2, 0.2)), 3.8146971692576415e-10, 6.103515470812226e-09)
    left_out = noise(arg_keys[16], (HID, HID), (0.02 * (AVG * DEVICES) ** -1), 9.5367431640625e-07, (), jnp.float32)
    right_out = noise(arg_keys[17], (CLS, CLS), (0.22 * (AVG * DEVICES) ** -1), 9.5367431640625e-06, (), jnp.float32)
    basis_left_out = draw_basis_left_out(jax.random.fold_in(arg_keys[22], 71), 0)
    basis_right_out = draw_basis_right_out(jax.random.fold_in(arg_keys[22], 71), 0)
    first_out = noise(arg_keys[20], (HID, CLS), (0.09 * (AVG * DEVICES) ** -0.5), 0.0014648438, (), jnp.float32)
    second_out = jnp.clip(jnp.exp(jax.random.uniform(arg_keys[21], (HID, CLS), jnp.float32, math.log(3.433227480087453e-09), math.log(5.493163968139925e-08))), 3.433227480087453e-09, 5.493163968139925e-08)
    return {"features": features, "labels": labels, "counts": counts, "w_branch": w_branch, "w_mid": w_mid, "w_out": w_out, "left_branch": left_branch, "right_branch": right_branch, "basis_left_branch": basis_left_branch, "basis_right_branch": basis_right_branch, "first_branch": first_branch, "second_branch": second_branch, "right_mid": right_mid, "basis_right_mid": basis_right_mid, "first_mid": first_mid, "second_mid": second_mid, "left_out": left_out, "right_out": right_out, "basis_left_out": basis_left_out, "basis_right_out": basis_right_out, "first_out": first_out, "second_out": second_out}


beta_first = 0.5
beta_second = 0.9
beta_factor = 0.95
adam_eps = 1e-08
norm_eps = 1e-05
rate_branch = 0.1
rate_mid = 0.02
rate_out = 0.04
highest = lax.Precision.HIGHEST

@jax.custom_vjp
def low(v):
    return lax.optimization_barrier(v.astype(jnp.bfloat16)).astype(jnp.float32)

@jax.custom_vjp
def low_back(v):
    return v

def low_keep(v):
    return (low(v), None)

def low_pass(kept, grad):
    return (grad,)

def back_keep(v):
    return (v, None)

def back_low(kept, grad):
    return (low(grad),)
low.defvjp(low_keep, low_pass)
low_back.defvjp(back_keep, back_low)

def precondition(gradient, left_factor, right_factor, basis_left, basis_right, first_moment, second_moment, weight, rate):
    new_left = beta_factor * left_factor + (1.0 - beta_factor) * jnp.einsum('kij,klj->kil', gradient, gradient, precision=highest)
    new_right = beta_factor * right_factor + (1.0 - beta_factor) * jnp.einsum('kji,kjl->kil', gradient, gradient, precision=highest)
    turned = jnp.einsum('kai,kaj->kij', basis_left, gradient, precision=highest)
    turned = jnp.einsum('kij,kjl->kil', turned, basis_right, precision=highest)
    new_first = beta_first * first_moment + (1.0 - beta_first) * turned
    new_second = beta_second * second_moment + (1.0 - beta_second) * turned * turned
    direction = new_first / (1.0 - beta_first ** STEP) / (jnp.sqrt(new_second / (1.0 - beta_second ** STEP)) + adam_eps)
    turned_back = jnp.einsum('kia,kab->kib', basis_left, direction, precision=highest)
    turned_back = jnp.einsum('kib,klb->kil', turned_back, basis_right, precision=highest)
    return (new_left, new_right, new_first, new_second, weight - rate * turned_back)

def balanced_rows(counts):
    group_ends = jnp.cumsum(counts, axis=1).astype(jnp.int32)
    group_starts = (group_ends - counts).astype(jnp.int32)
    positions = jnp.arange(PEERS * AVG, dtype=jnp.int32)
    source = lax.optimization_barrier(jnp.sum((group_ends[:, None, :] <= positions[None, :, None]).astype(jnp.int32), axis=2)).astype(jnp.int32)
    offset = positions[None, :] - jnp.take_along_axis(group_starts, source, axis=1)
    groups = jnp.arange(GROUPS, dtype=jnp.int32)[:, None]
    return ((groups * PEERS + source) * CAP + offset).reshape(-1).astype(jnp.int32)

def column_norm(values):
    mean_value = lax.optimization_barrier(jnp.mean(values, axis=(0, 1)))
    scale_value = lax.rsqrt(lax.optimization_barrier(jnp.mean(values * values, axis=(0, 1))) - mean_value * mean_value + norm_eps)
    return (mean_value, scale_value)

def forward(weight_branch, weight_mid, weight_out, moved_rows, targets):
    branch_low = low(weight_branch)
    mid_low = low(weight_mid)
    out_low = low(weight_out)
    tiles = moved_rows.reshape(-1, AVG, OPS, DIN)

    def first_block(tile_rows):
        return low_back(jnp.einsum('rkd,kdh->rkh', tile_rows, branch_low, precision=highest).reshape(AVG, CAT))
    branch_pre = lax.map(jax.checkpoint(first_block), tiles)
    mean_branch, scale_branch = column_norm(branch_pre)

    def second_block(tile_rows):
        branch_norm = (tile_rows - mean_branch) * scale_branch
        joined = low(jax.nn.silu(jax.nn.silu(branch_norm)))
        return low_back(jnp.dot(joined, mid_low, precision=highest))
    mid_pre = lax.map(jax.checkpoint(second_block), branch_pre)
    mean_mid, scale_mid = column_norm(mid_pre)

    def third_block(block_pair):
        tile_rows, tile_labels = block_pair
        hidden_out = low(jax.nn.silu((tile_rows - mean_mid) * scale_mid))
        scores = low_back(jnp.dot(hidden_out, out_low, precision=highest))
        picked = jnp.take_along_axis(scores, tile_labels[:, None], axis=1)[:, 0]
        return (scores, jnp.sum(jax.nn.logsumexp(scores, axis=1) - picked))
    scores, losses = lax.map(jax.checkpoint(third_block), (mid_pre, targets.reshape(-1, AVG)))
    return (jnp.sum(losses) / (AVG * DEVICES), scores.reshape(-1, CLS))

def reference(features, labels, counts, w_branch, w_mid, w_out, left_branch, right_branch, basis_left_branch, basis_right_branch, first_branch, second_branch, right_mid, basis_right_mid, first_mid, second_mid, left_out, right_out, basis_left_out, basis_right_out, first_out, second_out):
    pick_rows = balanced_rows(counts)
    moved_rows = features[pick_rows].astype(jnp.float32)
    targets = labels[pick_rows]
    loss_value, pullback, logits = jax.vjp(lambda wb_arg, wm_arg, wo_arg, rows_arg: forward(wb_arg, wm_arg, wo_arg, rows_arg, targets), w_branch, w_mid, w_out, moved_rows, has_aux=True)
    grad_branch, grad_mid, grad_out, grad_rows = pullback(jnp.ones_like(loss_value))
    grad_features = jnp.zeros(features.shape, jnp.float32).at[pick_rows].set(grad_rows).astype(jnp.bfloat16)
    new_left_branch, new_right_branch, new_first_branch, new_second_branch, new_w_branch = precondition(grad_branch, left_branch, right_branch, basis_left_branch, basis_right_branch, first_branch, second_branch, w_branch, rate_branch)
    out_parts = precondition(grad_out[None], left_out[None], right_out[None], basis_left_out[None], basis_right_out[None], first_out[None], second_out[None], w_out[None], rate_out)
    new_left_out, new_right_out, new_first_out, new_second_out, new_w_out = [piece[0] for piece in out_parts]
    new_right_mid = beta_factor * right_mid + (1.0 - beta_factor) * jnp.dot(grad_mid.T, grad_mid, precision=highest)
    turned = jnp.dot(grad_mid, basis_right_mid, precision=highest)
    new_first_mid = beta_first * first_mid + (1.0 - beta_first) * turned
    new_second_mid = beta_second * second_mid + (1.0 - beta_second) * turned * turned
    direction = new_first_mid / (1.0 - beta_first ** STEP) / (jnp.sqrt(new_second_mid / (1.0 - beta_second ** STEP)) + adam_eps)
    new_w_mid = w_mid - rate_mid * jnp.dot(direction, basis_right_mid.T, precision=highest)
    return (logits, grad_features, new_left_branch, new_right_branch, new_first_branch, new_second_branch, new_w_branch, new_w_branch.astype(jnp.bfloat16), new_right_mid, new_first_mid, new_second_mid, new_w_mid, new_w_mid.astype(jnp.bfloat16), new_left_out, new_right_out, new_first_out, new_second_out, new_w_out, new_w_out.astype(jnp.bfloat16))
```

```python
import functools

import jax
import jax.numpy as jnp
from jax import lax
from jax.experimental import pallas as pl
from jax.experimental.pallas import tpu as pltpu
from jax.sharding import PartitionSpec as P

OPS = 4
DIN = 100
HID = 512
CLS = 47
AVG = 4096
STEP = 5
CAT = 2048
LANE = 128
CPAD = 48
STRIDE = 96
WINDOW = 112
VALID = 400
WIDE = 416
SHARE = 12
BOTH = ("row", "col")

beta_first = 0.5
beta_second = 0.9
beta_factor = 0.95
adam_eps = 1e-08
norm_eps = 1e-05
rate_branch = 0.1
rate_mid = 0.02
rate_out = 0.04
highest = lax.Precision.HIGHEST
f32 = jnp.float32
bf16 = jnp.bfloat16
VMEM_LIMIT = 60 * 2**20


def dot_on(first_arg, second_arg, first_dim, second_dim, precision=None):
    return lax.dot_general(
        first_arg,
        second_arg,
        (((first_dim,), (second_dim,)), ((), ())),
        precision=precision,
        preferred_element_type=f32,
    )


def params():
    return pltpu.CompilerParams(vmem_limit_bytes=VMEM_LIMIT)


def cost(microseconds):
    return pl.CostEstimate(
        flops=int(microseconds * 1e9), bytes_accessed=1, transcendentals=0
    )


def shape(dims, dtype):
    return jax.ShapeDtypeStruct(dims, dtype)


def fixed(dims):
    return pl.BlockSpec(dims, lambda *_: (0,) * len(dims))


def rows_of(block, width):
    return pl.BlockSpec((block, width), lambda i, *_: (i, 0))


def columns_of(height, block):
    return pl.BlockSpec((height, block), lambda i, *_: (0, i))


def low_f32(values):
    return values.astype(bf16).astype(f32)


def split_low(values):
    high = values.astype(bf16)
    return high, (values - high.astype(f32)).astype(bf16)


def fold_rows(values):
    return jnp.sum(values.reshape(values.shape[0] // 8, 8, values.shape[1]), axis=0)


def add_up(ref):
    value = ref[0]
    for index in range(1, ref.shape[0]):
        value = value + ref[index]
    return value


def own_count(counts):
    return counts[lax.axis_index("row"), lax.axis_index("col")]


def branch_scale(stats, op, all_rows):
    mean = stats[op : op + 1, :] / all_rows
    square = stats[OPS + op : OPS + op + 1, :] / all_rows
    return mean, lax.rsqrt(square - mean * mean + norm_eps)


def unpack_pair(packed):
    parts = HID // LANE
    return [
        jnp.concatenate(
            [packed[index * parts + part : index * parts + part + 1, :] for part in range(parts)],
            axis=1,
        )
        for index in range(2)
    ]


def pack_pair(first, second):
    parts = HID // LANE
    return jnp.concatenate(
        [
            value[:, part * LANE : (part + 1) * LANE]
            for value in (first, second)
            for part in range(parts)
        ],
        axis=0,
    )


def mid_scale(stats_ref, all_rows):
    total, square = unpack_pair(add_up(stats_ref))
    mean = total / all_rows
    return mean, lax.rsqrt(square / all_rows - mean * mean + norm_eps)


def window_rows(x_ref, op):
    return jnp.concatenate(
        [x_ref[op * STRIDE : op * STRIDE + WINDOW, :], x_ref[VALID:WIDE, :]], axis=0
    )


def padded(window):
    return jnp.concatenate([window, jnp.zeros((LANE - WINDOW, HID), bf16)], axis=0)


def gram_product(gram, window):
    high, low = split_low(gram)
    weight = padded(window)
    return jnp.dot(high, weight, preferred_element_type=f32) + jnp.dot(
        low, weight, preferred_element_type=f32
    )


def gather_pieces(refs, held):
    row = lax.axis_index("row")
    size = held.shape[0] // len(refs)
    for index, ref in enumerate(refs):
        at = pl.multiple_of((row ^ index) * size, size)
        held[pl.ds(at, size), :] = ref[...].reshape(size, held.shape[1]).astype(held.dtype)


def gram_body(counts, x_ref, w_ref, xa_ref, window_ref, gram_ref, stats_ref):
    step = pl.program_id(0)
    block = x_ref.shape[1]

    @pl.when(step == 0)
    def _():
        gram_ref[...] = jnp.zeros_like(gram_ref)
        for op in range(OPS):
            shift = op * (DIN - STRIDE)
            parts = [low_f32(w_ref[:, op, :])]
            if shift:
                parts.insert(0, jnp.zeros((shift, HID), f32))
            if WINDOW - DIN - shift:
                parts.append(jnp.zeros((WINDOW - DIN - shift, HID), f32))
            window_ref[op] = jnp.concatenate(parts, axis=0).astype(bf16)

    column = step * block + lax.broadcasted_iota(jnp.int32, (16, block), 1)
    valid = jnp.where(column < own_count(counts), 1.0, 0.0)
    xa_ref[:VALID, :] = x_ref[...] * valid[0:1, :].astype(bf16)
    line = lax.broadcasted_iota(jnp.int32, (16, block), 0)
    xa_ref[VALID:, :] = jnp.where(line < 2, valid, 0.0).astype(bf16)
    for op in range(OPS):
        rows = window_rows(xa_ref, op)
        gram_ref[op] += dot_on(rows, rows, 1, 1)

    @pl.when(step == pl.num_programs(0) - 1)
    def _():
        for op in range(OPS):
            turned = gram_product(gram_ref[op], window_ref[op])
            stats_ref[op : op + 1, :] = turned[WINDOW : WINDOW + 1, :]
            stats_ref[OPS + op : OPS + op + 1, :] = jnp.sum(
                window_ref[op].astype(f32) * turned[:WINDOW, :], axis=0, keepdims=True
            )


def gram_call(counts, features, w_branch, block):
    total = features.shape[1]
    return pl.pallas_call(
        gram_body,
        grid_spec=pltpu.PrefetchScalarGridSpec(
            num_scalar_prefetch=1,
            grid=(total // block,),
            in_specs=[columns_of(VALID, block), fixed((DIN, OPS, HID))],
            out_specs=[
                columns_of(WIDE, block),
                fixed((OPS, WINDOW, HID)),
                fixed((OPS, LANE, LANE)),
                fixed((2 * OPS, HID)),
            ],
        ),
        out_shape=[
            shape((WIDE, total), bf16),
            shape((OPS, WINDOW, HID), bf16),
            shape((OPS, LANE, LANE), f32),
            shape((2 * OPS, HID), f32),
        ],
        compiler_params=params(),
        cost_estimate=cost(6),
        name="row_moments",
    )(counts, features, w_branch)


def forward_body(all_rows, count, *refs):
    xa_ref, stats_ref, window_ref = refs[:3]
    pieces = refs[3 : 3 + count]
    pre_ref, joined_ref, slope_ref, wm_ref, out_ref, wide, total = refs[3 + count :]
    step = pl.program_id(0)

    @pl.when(step == 0)
    def _():
        total[...] = jnp.zeros_like(total)
        gather_pieces(pieces, wm_ref)
        stats = add_up(stats_ref)
        line = lax.broadcasted_iota(jnp.int32, (LANE - WINDOW, HID), 0)
        for op in range(OPS):
            mean, scale = branch_scale(stats, op, all_rows)
            half = 0.5 * scale
            high, low = split_low(window_ref[op].astype(f32) * half)
            base = -mean * half
            base_high = low_f32(base)
            wide[op, :WINDOW, :] = high
            wide[op, WINDOW:LANE, :] = jnp.where(
                line == 0, base_high, jnp.where(line == 1, base - base_high, 0.0)
            ).astype(bf16)
            wide[op, LANE : LANE + WINDOW, :] = low
            wide[op, LANE + WINDOW :, :] = jnp.zeros((LANE - WINDOW, HID), bf16)

    pre = None
    for op in range(OPS):
        rows = window_rows(xa_ref, op).T
        half = jnp.dot(
            jnp.concatenate([rows, rows], axis=1), wide[op], preferred_element_type=f32
        ).astype(bf16)
        first = jnp.tanh(half) + 1.0
        act = half * first
        half_act = act * 0.5
        second = jnp.tanh(half_act) + 1.0
        joined = half_act * second
        slope = (first * ((half - half_act) + 0.5)) * (second * ((act - joined) + 1.0))
        joined_ref[:, op * HID : (op + 1) * HID] = joined
        slope_ref[:, op * HID : (op + 1) * HID] = slope
        term = jnp.dot(
            joined, wm_ref[op * HID : (op + 1) * HID, :], preferred_element_type=f32
        )
        pre = term if pre is None else pre + term
    pre_ref[...] = pre
    total[0] += fold_rows(pre)
    total[1] += fold_rows(pre * pre)

    @pl.when(step == pl.num_programs(0) - 1)
    def _():
        packed = pack_pair(
            jnp.sum(total[0], axis=0, keepdims=True), jnp.sum(total[1], axis=0, keepdims=True)
        )
        for index in range(out_ref.shape[0]):
            out_ref[index] = packed


def forward_call(all_rows, devices, spread, stats, window, pieces, block):
    total = spread.shape[1]
    count = len(pieces)
    return pl.pallas_call(
        functools.partial(forward_body, all_rows, count),
        grid=(total // block,),
        in_specs=[
            columns_of(WIDE, block),
            fixed(stats.shape),
            fixed((OPS, WINDOW, HID)),
        ]
        + [fixed(piece.shape) for piece in pieces],
        out_specs=[
            rows_of(block, HID),
            rows_of(block, CAT),
            rows_of(block, CAT),
            fixed((CAT, HID)),
            fixed((devices, 8, LANE)),
        ],
        out_shape=[
            shape((total, HID), f32),
            shape((total, CAT), bf16),
            shape((total, CAT), bf16),
            shape((CAT, HID), bf16),
            shape((devices, 8, LANE), f32),
        ],
        scratch_shapes=[pltpu.VMEM((OPS, 2 * LANE, HID), bf16), pltpu.VMEM((2, 8, HID), f32)],
        compiler_params=params(),
        cost_estimate=cost(44),
        name="forward_layers",
    )(spread, stats, window, *pieces)


def head_body(
    all_rows,
    counts,
    pre_ref,
    stats_ref,
    wo_ref,
    labels_ref,
    half_ref,
    back_ref,
    logits_ref,
    grad_ref,
    sums_ref,
    wo_low,
    norm,
    total,
):
    step = pl.program_id(0)
    block = pre_ref.shape[0]

    @pl.when(step == 0)
    def _():
        total[...] = jnp.zeros_like(total)
        grad_ref[...] = jnp.zeros_like(grad_ref)
        wo_low[...] = jnp.concatenate(
            [wo_ref[...], jnp.zeros((CPAD - CLS, HID), f32)], axis=0
        ).astype(bf16)
        mean, scale = mid_scale(stats_ref, all_rows)
        norm[0:1, :] = 0.5 * scale
        norm[1:2, :] = -0.5 * scale * mean

    half = pre_ref[...] * norm[0:1, :] + norm[1:2, :]
    tanh = jnp.tanh(half)
    part = half * tanh
    hidden = (half + part).astype(bf16)
    slope = (0.5 * (1.0 + tanh)) * (1.0 + (half - part))
    logits = dot_on(wo_low[...], hidden, 1, 1)
    logits_ref[...] = logits
    kind = lax.broadcasted_iota(jnp.int32, (CPAD, block), 0)
    column = step * block + lax.broadcasted_iota(jnp.int32, (CPAD, block), 1)
    real = kind < CLS
    top = jnp.max(jnp.where(real, logits, -jnp.inf), axis=0, keepdims=True)
    raised = jnp.where(real, jnp.exp(logits - top), 0.0)
    probs = raised / jnp.sum(raised, axis=0, keepdims=True)
    score = (probs - jnp.where(kind == labels_ref[...], 1.0, 0.0)) / all_rows
    score = jnp.where(column < own_count(counts), score, 0.0).astype(bf16)
    grad_ref[...] += dot_on(score, hidden, 1, 0)
    back = dot_on(score, wo_low[...], 0, 0) * slope
    total[0] += fold_rows(back)
    total[1] += fold_rows(back * half)
    half_ref[...] = half.astype(bf16)
    back_ref[...] = back.astype(bf16)

    @pl.when(step == pl.num_programs(0) - 1)
    def _():
        packed = pack_pair(
            jnp.sum(total[0], axis=0, keepdims=True),
            2.0 * jnp.sum(total[1], axis=0, keepdims=True),
        )
        for index in range(sums_ref.shape[0]):
            sums_ref[index] = packed


def head_call(all_rows, counts, pre, stats, w_out, labels, block):
    total = pre.shape[0]
    return pl.pallas_call(
        functools.partial(head_body, all_rows),
        grid_spec=pltpu.PrefetchScalarGridSpec(
            num_scalar_prefetch=1,
            grid=(total // block,),
            in_specs=[
                rows_of(block, HID),
                fixed(stats.shape),
                fixed((CLS, HID)),
                columns_of(1, block),
            ],
            out_specs=[
                rows_of(block, HID),
                rows_of(block, HID),
                columns_of(CPAD, block),
                fixed((CPAD, HID)),
                fixed(stats.shape),
            ],
            scratch_shapes=[
                pltpu.VMEM((CPAD, HID), bf16),
                pltpu.VMEM((8, HID), f32),
                pltpu.VMEM((2, 8, HID), f32),
            ],
        ),
        out_shape=[
            shape((total, HID), bf16),
            shape((total, HID), bf16),
            shape((CPAD, total), f32),
            shape((CPAD, HID), f32),
            shape(stats.shape, f32),
        ],
        compiler_params=params(),
        cost_estimate=cost(18),
        name="head",
    )(counts, pre, stats, w_out, labels)


def mid_grad_body(
    all_rows,
    half_ref,
    back_ref,
    joined_ref,
    stats_ref,
    sums_ref,
    mid_ref,
    kept_ref,
    sent_ref,
    norm,
    grad,
):
    step = pl.program_id(0)

    @pl.when(step == 0)
    def _():
        grad[...] = jnp.zeros_like(grad)
        scale = mid_scale(stats_ref, all_rows)[1]
        level, slant = unpack_pair(add_up(sums_ref))
        norm[0:1, :] = scale
        norm[1:2, :] = scale * (level / all_rows)
        norm[2:3, :] = 2.0 * scale * (slant / all_rows)

    mid = (
        back_ref[...].astype(f32) * norm[0:1, :]
        - norm[1:2, :]
        - half_ref[...].astype(f32) * norm[2:3, :]
    ).astype(bf16)
    mid_ref[...] = mid
    for op in range(OPS):
        span = slice(op * HID, (op + 1) * HID)
        grad[span, :] += dot_on(joined_ref[:, span], mid, 0, 0)

    @pl.when(step == pl.num_programs(0) - 1)
    def _():
        core = lax.rem(lax.axis_index("row"), 2)
        pairs, size = kept_ref.shape[0], kept_ref.shape[1]
        for pair in range(pairs):
            kept = pl.multiple_of((2 * pair + core) * size, size)
            sent = pl.multiple_of((2 * pair + 1 - core) * size, size)
            kept_ref[pair] = grad[pl.ds(kept, size), :]
            sent_ref[pair] = grad[pl.ds(sent, size), :]


def mid_grad_call(all_rows, groups, half, back, joined, stats, sums, block):
    total = half.shape[0]
    parted = (groups // 2, CAT // groups, HID)
    return pl.pallas_call(
        functools.partial(mid_grad_body, all_rows),
        grid=(total // block,),
        in_specs=[
            rows_of(block, HID),
            rows_of(block, HID),
            rows_of(block, CAT),
            fixed(stats.shape),
            fixed(sums.shape),
        ],
        out_specs=[rows_of(block, HID), fixed(parted), fixed(parted)],
        out_shape=[shape((total, HID), bf16), shape(parted, f32), shape(parted, f32)],
        scratch_shapes=[pltpu.VMEM((8, HID), f32), pltpu.VMEM((CAT, HID), f32)],
        compiler_params=params(),
        cost_estimate=cost(27),
        name="mid_grad",
    )(half, back, joined, stats, sums)


def branch_back_body(all_rows, ops, parted, *refs):
    mid_ref, slope_ref, xa_ref, wm_ref, stats_ref, grad_out_ref, gram_ref = refs[:7]
    refs = refs[7:]
    if parted:
        early_ref, back_ref, kept_ref, sent_refs = refs[0], refs[1], refs[2], refs[3:-2]
    else:
        back_ref, late_ref = refs[:2]
    halved, grad = refs[-2:]
    step = pl.program_id(0)

    @pl.when(step == 0)
    def _():
        grad[...] = jnp.zeros_like(grad)
        stats = add_up(stats_ref)
        for index, op in enumerate(ops):
            halved[index : index + 1, :] = 0.5 * branch_scale(stats, op, all_rows)[1]

    for index, op in enumerate(ops):
        span = slice(index * HID, (index + 1) * HID)
        joined_back = dot_on(mid_ref[...], wm_ref[span, :], 1, 1)
        back = (
            (joined_back * halved[index : index + 1, :]) * slope_ref[:, span].astype(f32)
        ).astype(bf16)
        back_ref[:, span] = back
        line = slice(op * LANE, (op + 1) * LANE) if parted else slice(index * LANE, (index + 1) * LANE)
        grad[line, :HID] += dot_on(window_rows(xa_ref, op), back, 1, 0)

    @pl.when(step == pl.num_programs(0) - 1)
    def _():
        for index, op in enumerate(ops):
            start = (op if parted else index) * LANE
            grad[start : start + LANE, HID:] = gram_ref[op]
            grad[start : start + LANE, :HID] = jnp.concatenate(
                [
                    grad[start : start + WINDOW + 1, :HID],
                    grad_out_ref[op * SHARE : (op + 1) * SHARE, :],
                    jnp.zeros((LANE - WINDOW - 1 - SHARE, HID), f32),
                ],
                axis=0,
            )
        if parted:
            grad[: ops[0] * LANE, :] = early_ref[...]
            size = kept_ref.shape[0]
            row = lax.axis_index("row")
            kept_ref[...] = grad[pl.ds(pl.multiple_of(row * size, size), size), :]
            for distance, sent_ref in enumerate(sent_refs, 1):
                at = pl.multiple_of((row ^ distance) * size, size)
                sent_ref[...] = grad[pl.ds(at, size), :].astype(bf16)
        else:
            late_ref[...] = grad[...]


def branch_back_call(
    all_rows, groups, ops, mid, slope, spread, mid_low, stats, grad_out, gram, early, block
):
    total = mid.shape[0]
    count = len(ops)
    offset = ops[0] // count
    wide = HID + LANE
    parted = early is not None
    if parted:
        size = OPS * LANE // groups
        parts = [shape((size, wide), f32)] + [shape((size, wide), bf16)] * (groups - 1)
    else:
        parts = [shape((count * LANE, wide), f32)]
    return pl.pallas_call(
        functools.partial(branch_back_body, all_rows, ops, parted),
        grid=(total // block,),
        in_specs=[
            rows_of(block, HID),
            pl.BlockSpec((block, count * HID), lambda i: (i, offset)),
            columns_of(WIDE, block),
            pl.BlockSpec((count * HID, HID), lambda i: (offset, 0)),
            fixed(stats.shape),
            fixed((CPAD, HID)),
            fixed((OPS, LANE, LANE)),
        ]
        + ([fixed(early.shape)] if parted else []),
        out_specs=[rows_of(block, count * HID)] + [fixed(part.shape) for part in parts],
        out_shape=[shape((total, count * HID), bf16)] + parts,
        scratch_shapes=[
            pltpu.VMEM((8, HID), f32),
            pltpu.VMEM(((OPS if parted else count) * LANE, wide), f32),
        ],
        compiler_params=params(),
        cost_estimate=cost(23),
        name="branch_back",
    )(mid, slope, spread, mid_low, stats, grad_out, gram, *([early] if parted else []))


def add_windows(pieces, write):
    for index, piece in enumerate(pieces):
        start = index * STRIDE
        skip = WINDOW - STRIDE if index else 0
        stop = WINDOW if index == len(pieces) - 1 else STRIDE
        if index:
            write(start, pieces[index - 1][STRIDE:WINDOW, :] + piece[:skip, :])
        write(start + skip, piece[skip:stop, :])


def rows_part_body(ops, window_ref, back_ref, out_ref):
    pieces = [
        dot_on(window_ref[op], back_ref[:, index * HID : (index + 1) * HID], 1, 1)
        for index, op in enumerate(ops)
    ]

    def write(at, value):
        out_ref[at : at + value.shape[0], :] = value.astype(bf16)

    add_windows(pieces, write)


def rows_part_call(ops, window, back, block):
    total, width = back.shape
    height = (len(ops) - 1) * STRIDE + WINDOW
    return pl.pallas_call(
        functools.partial(rows_part_body, ops),
        grid=(total // block,),
        in_specs=[fixed((OPS, WINDOW, HID)), rows_of(block, width)],
        out_specs=columns_of(height, block),
        out_shape=shape((height, total), bf16),
        compiler_params=params(),
        cost_estimate=cost(9),
        name="rows_part",
    )(window, back)


def branch_terms(all_rows, mean, scale, window, raw):
    level = raw[WINDOW : WINDOW + 1, :]
    inner = scale * (
        jnp.sum(window.astype(f32) * raw[:WINDOW, :], axis=0, keepdims=True) - mean * level
    )
    return level / all_rows, scale * (inner / all_rows)


def rows_back_body(all_rows, count, counts, *refs):
    xa_ref, low_ref, high_ref, stats_ref, window_ref = refs[:5]
    pieces = refs[5 : 5 + count]
    out_ref, inner, grads = refs[5 + count :]
    step = pl.program_id(0)
    block = xa_ref.shape[1]

    @pl.when(step == 0)
    def _():
        gather_pieces(pieces, grads)
        stats = add_up(stats_ref)
        lane = lax.broadcasted_iota(jnp.int32, (WINDOW, LANE), 1)
        for op in range(OPS):
            mean, scale = branch_scale(stats, op, all_rows)
            window = window_ref[op]
            level, slant = branch_terms(
                all_rows, mean, scale, window, grads[op * LANE : (op + 1) * LANE, :HID]
            )
            wide = window.astype(f32)
            turned = dot_on(
                (wide * slant).astype(bf16),
                padded(window),
                1,
                1,
            )
            base = jnp.sum(wide * (mean * slant - level), axis=1, keepdims=True)
            high = low_f32(base)
            inner[op] = jnp.where(
                lane == WINDOW, high, jnp.where(lane == WINDOW + 1, base - high, -turned)
            ).astype(bf16)

    moved = [
        jnp.dot(inner[op], window_rows(xa_ref, op), preferred_element_type=f32)
        for op in range(OPS)
    ]
    column = step * block + lax.broadcasted_iota(jnp.int32, (1, block), 1)
    valid = column < own_count(counts)

    split = OPS // 2 * STRIDE

    def write(at, value):
        stop = at + value.shape[0]
        if at < low_ref.shape[0]:
            value = value + low_ref[at:stop, :].astype(f32)
        if at >= split:
            value = value + high_ref[at - split : stop - split, :].astype(f32)
        out_ref[at:stop, :] = jnp.where(valid, value, 0.0).astype(bf16)

    add_windows(moved, write)


def rows_back_call(all_rows, counts, spread, parts, stats, window, pieces, block):
    total = spread.shape[1]
    count = len(pieces)
    return pl.pallas_call(
        functools.partial(rows_back_body, all_rows, count),
        grid_spec=pltpu.PrefetchScalarGridSpec(
            num_scalar_prefetch=1,
            grid=(total // block,),
            in_specs=[
                columns_of(WIDE, block),
                columns_of(parts[0].shape[0], block),
                columns_of(parts[1].shape[0], block),
                fixed(stats.shape),
                fixed((OPS, WINDOW, HID)),
            ]
            + [fixed(piece.shape) for piece in pieces],
            out_specs=columns_of(VALID, block),
            scratch_shapes=[
                pltpu.VMEM((OPS, WINDOW, LANE), bf16),
                pltpu.VMEM((OPS * LANE, HID + LANE), f32),
            ],
        ),
        out_shape=shape((VALID, total), bf16),
        compiler_params=params(),
        cost_estimate=cost(8),
        name="rows_back",
    )(counts, spread, *parts, stats, window, *pieces)


def distances(peers):
    found = []
    for gap in range(-peers, peers + 1):
        pairs = [
            (source, source + gap)
            for source in range(peers)
            if max(0, 2 * source - peers) <= source + gap <= min(2 * source + 1, peers - 1)
        ]
        if pairs:
            found.append((gap, pairs))
    return found


def cut_body(gaps, counts, logits_ref, *refs):
    outs, held = refs[:-1], refs[-1]
    total = logits_ref.shape[1]
    row, member = lax.axis_index("row"), lax.axis_index("col")
    count = counts[row, member]
    begin = jnp.int32(0)
    for peer in range(counts.shape[1]):
        begin += jnp.where(peer < member, counts[row, peer], 0)
    front = AVG + LANE
    rest = lax.rem(LANE - lax.rem(begin, LANE), LANE)
    lane = lax.broadcasted_iota(jnp.int32, (CPAD, LANE), 1)
    empty = jnp.zeros((CPAD, LANE), f32)
    turn = LANE - rest

    def turned(tile):
        if tile < 0 or tile >= total // LANE:
            return empty
        piece = logits_ref[:, tile * LANE : (tile + 1) * LANE]
        piece = jnp.where(tile * LANE + lane < count, piece, 0.0)
        return pltpu.roll(piece, turn, 1)

    held[:, : front - LANE] = jnp.zeros((CPAD, front - LANE), bf16)
    held[:, front + total :] = jnp.zeros((CPAD, AVG + LANE), bf16)
    left = turned(-1)
    for tile in range(-1, total // LANE):
        right = turned(tile + 1)
        at = front + tile * LANE
        held[:, at : at + LANE] = jnp.where(lane < turn, left, right).astype(bf16)
        left = right
    for out, gap in zip(outs, gaps):
        at = jnp.maximum(front + (member + gap) * AVG - begin, 0)
        at = jnp.minimum(at // LANE, (front + total) // LANE) * LANE
        out[...] = held[:, pl.ds(pl.multiple_of(at, LANE), AVG)]


def cut_call(counts, logits, gaps):
    total = logits.shape[1]
    return pl.pallas_call(
        functools.partial(cut_body, gaps),
        grid_spec=pltpu.PrefetchScalarGridSpec(
            num_scalar_prefetch=1,
            grid=(1,),
            in_specs=[fixed((CPAD, total))],
            out_specs=[fixed((CPAD, AVG))] * len(gaps),
            scratch_shapes=[pltpu.VMEM((CPAD, 2 * AVG + 2 * LANE + total), bf16)],
        ),
        out_shape=[shape((CPAD, AVG), bf16)] * len(gaps),
        compiler_params=params(),
        cost_estimate=cost(4),
        name="cut_logits",
    )(counts, logits)


def join_body(*refs):
    out = refs[-1]
    value = refs[0][...].astype(f32)
    for ref in refs[1:-1]:
        value = value + ref[...].astype(f32)
    out[...] = value[:CLS, :]


def join_call(pieces, block):
    return pl.pallas_call(
        join_body,
        grid=(AVG // block,),
        in_specs=[pl.BlockSpec((CPAD, block), lambda i: (0, i))] * len(pieces),
        out_specs=columns_of(CLS, block),
        out_shape=shape((CLS, AVG), f32),
        compiler_params=params(),
        cost_estimate=cost(3),
        name="join_logits",
    )(*pieces)


def moments(turned, first, second):
    new_first = beta_first * first + (1.0 - beta_first) * turned
    new_second = beta_second * second + (1.0 - beta_second) * turned * turned
    direction = (
        new_first
        / (1.0 - beta_first**STEP)
        / (jnp.sqrt(new_second / (1.0 - beta_second**STEP)) + adam_eps)
    )
    return new_first, new_second, direction


def factor(old, grad, dim):
    return beta_factor * old + (1.0 - beta_factor) * dot_on(grad, grad, dim, dim, highest)


def branch_update_body(all_rows, count, *refs):
    stats_ref, window_ref = refs[:2]
    pieces = refs[2 : 2 + count]
    (
        w_ref,
        left_ref,
        right_ref,
        basis_left_ref,
        basis_right_ref,
        first_ref,
        second_ref,
        new_left_ref,
        new_right_ref,
        new_first_ref,
        new_second_ref,
        new_w_ref,
        low_w_ref,
        grad_out_ref,
        grads,
    ) = refs[2 + count :]

    step = pl.program_id(0)

    @pl.when(step == 0)
    def _():
        gather_pieces(pieces, grads)
        for op in range(OPS):
            at = op * LANE + WINDOW + 1
            grad_out_ref[op * SHARE : (op + 1) * SHARE, :] = grads[at : at + SHARE, :HID]

    for op in range(OPS):

        @pl.when(step == op)
        def _(op=op):
            mean, scale = branch_scale(add_up(stats_ref), op, all_rows)
            window = window_ref[op]
            raw = grads[op * LANE : (op + 1) * LANE, :HID]
            gram = grads[op * LANE : (op + 1) * LANE, HID:]
            level, slant = branch_terms(all_rows, mean, scale, window, raw)
            column = gram[:WINDOW, WINDOW : WINDOW + 1]
            normed = gram_product(gram, window)[:WINDOW, :] - column * mean
            grad = raw[:WINDOW, :] - column * level - normed * slant
            shift = op * (DIN - STRIDE)
            grad = grad[shift : shift + DIN, :]
            new_left_ref[:, op, :] = factor(left_ref[:, op, :], grad, 1)
            new_right_ref[0] = factor(right_ref[0], grad, 0)
            basis_left, basis_right = basis_left_ref[:, op, :], basis_right_ref[0]
            turned = dot_on(basis_left, grad, 0, 0, highest)
            turned = dot_on(turned, basis_right, 1, 0, highest)
            new_first, new_second, direction = moments(
                turned, first_ref[:, op, :], second_ref[:, op, :]
            )
            new_first_ref[:, op, :] = new_first
            new_second_ref[:, op, :] = new_second
            back = dot_on(basis_left, direction, 1, 0, highest)
            back = dot_on(back, basis_right, 1, 1, highest)
            new_w = w_ref[:, op, :] - rate_branch * back
            new_w_ref[:, op, :] = new_w
            low_w_ref[:, op, :] = new_w.astype(bf16)


def branch_update_call(
    all_rows, stats, window, pieces, w, left, right, basis_left, basis_right, first, second
):
    small, wide = fixed((DIN, OPS, DIN)), fixed((DIN, OPS, HID))
    square = pl.BlockSpec((1, HID, HID), lambda k: (k, 0, 0))
    count = len(pieces)
    return pl.pallas_call(
        functools.partial(branch_update_body, all_rows, count),
        grid=(OPS,),
        in_specs=[fixed(stats.shape), fixed((OPS, WINDOW, HID))]
        + [fixed(piece.shape) for piece in pieces]
        + [wide, small, square, small, square, wide, wide],
        out_specs=[small, square, wide, wide, wide, wide, fixed((CPAD, HID))],
        out_shape=[
            shape((DIN, OPS, DIN), f32),
            shape((OPS, HID, HID), f32),
            shape((DIN, OPS, HID), f32),
            shape((DIN, OPS, HID), f32),
            shape((DIN, OPS, HID), f32),
            shape((DIN, OPS, HID), bf16),
            shape((CPAD, HID), f32),
        ],
        scratch_shapes=[pltpu.VMEM((OPS * LANE, HID + LANE), f32)],
        compiler_params=params(),
        cost_estimate=cost(12),
        name="branch_update",
    )(stats, window, *pieces, w, left, right, basis_left, basis_right, first, second)


def out_update_body(
    grad_ref,
    w_ref,
    left_ref,
    right_ref,
    basis_left_ref,
    basis_right_ref,
    first_ref,
    second_ref,
    new_left_ref,
    new_right_ref,
    new_first_ref,
    new_second_ref,
    new_w_ref,
    low_w_ref,
):
    grad = grad_ref[:CLS, :]
    new_left_ref[...] = factor(left_ref[...], grad, 0)
    new_right_ref[...] = factor(right_ref[...], grad, 1)
    turned = jnp.dot(grad, basis_left_ref[...], precision=highest, preferred_element_type=f32)
    turned = dot_on(basis_right_ref[...], turned, 0, 0, highest)
    new_first, new_second, direction = moments(turned, first_ref[...], second_ref[...])
    new_first_ref[...] = new_first
    new_second_ref[...] = new_second
    back = dot_on(direction, basis_left_ref[...], 1, 1, highest)
    back = dot_on(basis_right_ref[...], back, 1, 0, highest)
    new_w = w_ref[...] - rate_out * back
    new_w_ref[...] = new_w
    low_w_ref[...] = new_w.astype(bf16)


def out_update_call(grad, w, left, right, basis_left, basis_right, first, second):
    return pl.pallas_call(
        out_update_body,
        out_shape=[
            shape((HID, HID), f32),
            shape((CLS, CLS), f32),
            shape((CLS, HID), f32),
            shape((CLS, HID), f32),
            shape((CLS, HID), f32),
            shape((CLS, HID), bf16),
        ],
        compiler_params=params(),
        cost_estimate=cost(4),
        name="out_update",
    )(grad, w, left, right, basis_left, basis_right, first, second)


def mid_update_body(
    grad_ref, w_ref, basis_ref, first_ref, second_ref, new_first_ref, new_second_ref, new_w_ref, low_w_ref
):
    turned = dot_on(grad_ref[...], basis_ref[...], 1, 0, highest)
    new_first, new_second, direction = moments(turned, first_ref[...], second_ref[...])
    new_first_ref[...] = new_first
    new_second_ref[...] = new_second
    new_w = w_ref[...] - rate_mid * dot_on(direction, basis_ref[...], 1, 1, highest)
    new_w_ref[...] = new_w
    low_w_ref[...] = new_w.astype(bf16)


def mid_update_call(grad, w, basis, first, second):
    rows = grad.shape[0]
    return pl.pallas_call(
        mid_update_body,
        out_shape=[shape((rows, HID), f32)] * 3 + [shape((rows, HID), bf16)],
        compiler_params=params(),
        cost_estimate=cost(3),
        name="mid_update",
    )(grad, w, basis, first, second)


def mid_factor_body(right_ref, *refs):
    out_ref, held = refs[-2:]
    gather_pieces(refs[:-2], held)
    out_ref[...] = beta_factor * right_ref[...] + (1.0 - beta_factor) * dot_on(
        held[...], held[...], 0, 0
    )


def mid_factor_call(right, pieces):
    return pl.pallas_call(
        mid_factor_body,
        out_shape=shape((HID, HID), f32),
        scratch_shapes=[pltpu.VMEM((CAT, HID), bf16)],
        compiler_params=params(),
        cost_estimate=cost(3),
        name="mid_factor",
    )(right, *pieces)


def after(values, *others):
    return lax.optimization_barrier((values,) + others)[0]


def swap(values, axis, distance):
    peers = lax.axis_size(axis)
    return lax.ppermute(values, axis, [(peer, peer ^ distance) for peer in range(peers)])


def add_all(values):
    while len(values) > 1:
        values = [values[i] + values[i + 1] for i in range(0, len(values), 2)]
    return values[0]


def exchange(values):
    return lax.all_to_all(values, "col", 0, 0, tiled=True)


def spread_out(values):
    return exchange(jnp.broadcast_to(values[None], (lax.axis_size("col"),) + values.shape))


def row_copies(values):
    pieces = {0: values}
    distance = lax.axis_size("row") // 2
    while distance:
        pieces.update({d ^ distance: swap(v, "row", distance) for d, v in list(pieces.items())})
        distance //= 2
    return [pieces[d] for d in sorted(pieces)]


def sum_in_row(values):
    return add_all([values] + [swap(values, "row", d) for d in range(1, lax.axis_size("row"))])


def keep_bit(values, distance):
    bit = lax.rem(lax.axis_index("row") // distance, 2)
    pairs = values.reshape((-1, 2) + values.shape[1:])
    kept = lax.dynamic_index_in_dim(pairs, bit, 1, keepdims=False)
    sent = lax.dynamic_index_in_dim(pairs, 1 - bit, 1, keepdims=False)
    return kept, sent


def finish_scatter(values, distance):
    while distance < lax.axis_size("row"):
        kept, sent = keep_bit(values, distance)
        values = kept + swap(sent.astype(bf16), "row", distance).astype(f32)
        distance *= 2
    values = values.reshape((lax.axis_size("col"), -1) + values.shape[2:]).astype(bf16)
    return jnp.sum(exchange(values).astype(f32), axis=0)


def local(
    features,
    labels,
    counts,
    w_branch,
    w_mid,
    w_out,
    left_branch,
    right_branch,
    basis_left_branch,
    basis_right_branch,
    first_branch,
    second_branch,
    right_mid,
    basis_right_mid,
    first_mid,
    second_mid,
    left_out,
    right_out,
    basis_left_out,
    basis_right_out,
    first_out,
    second_out,
):
    groups, peers = lax.axis_size("row"), lax.axis_size("col")
    devices = groups * peers
    all_rows = float(AVG * devices)

    def by_input(values):
        return values.transpose(1, 0, 2)

    own_mid = spread_out(w_mid.astype(bf16)).reshape(-1, HID)
    spread, window, gram, branch_sums = gram_call(counts, features.T, by_input(w_branch), 2048)
    own_mid = after(own_mid, branch_sums)
    pieces = {0: own_mid}
    distance = groups // 2
    while distance > 1:
        pieces.update({d ^ distance: swap(v, "row", distance) for d, v in list(pieces.items())})
        distance //= 2
    branch_stats = spread_out(sum_in_row(branch_sums))
    held = lax.optimization_barrier((branch_stats, *[pieces[d] for d in sorted(pieces)]))
    branch_stats, pieces = held[0], dict(zip(sorted(pieces), held[1:]))
    pieces.update({d ^ 1: swap(v, "row", 1) for d, v in list(pieces.items())})
    pre, joined, slope, mid_low, mid_sums = forward_call(
        all_rows, devices, spread, branch_stats, window, [pieces[d] for d in sorted(pieces)], 1024
    )
    mid_stats = lax.all_to_all(mid_sums, BOTH, 0, 0, tiled=True)
    half, back, logits, grad_out, back_sums = head_call(
        all_rows, counts, pre, mid_stats, w_out.T, labels.reshape(1, -1), 1024
    )
    back_stats = lax.all_to_all(back_sums, BOTH, 0, 0, tiled=True)

    plan = distances(peers)
    cuts = cut_call(counts, after(logits, back_stats), [gap for gap, _ in plan])
    moved = [
        cut if gap == 0 else lax.ppermute(cut, "col", pairs)
        for cut, (gap, pairs) in zip(cuts, plan)
    ]
    mid, kept, sent = mid_grad_call(
        all_rows, groups, after(half, *cuts), back, joined, mid_stats, back_stats, 1024
    )
    near = swap(sent, "row", 1)
    early_back, early = branch_back_call(
        all_rows, groups, (0, 1), mid, slope, spread, mid_low, branch_stats, grad_out, gram, None, 1024
    )
    near = after(near, early)
    kept, sent = keep_bit(kept + near, 2)
    sent = sent.astype(bf16)
    far = swap(sent, "row", 2)
    late_back, own, *parts = branch_back_call(
        all_rows,
        groups,
        (2, 3),
        after(mid, sent),
        slope,
        spread,
        mid_low,
        branch_stats,
        grad_out,
        gram,
        early,
        1024,
    )
    held = lax.optimization_barrier((own, far, *moved))
    own, far, moved = held[0], held[1], held[2:]
    terms = [own] + [
        swap(part, "row", distance) for distance, part in enumerate(parts, 1)
    ]
    low_part = rows_part_call((0, 1), window, after(early_back, own), 1024)
    grad_mid = kept + far.astype(f32)
    grad_mid = finish_scatter(grad_mid, 4)
    held = lax.optimization_barrier((low_part, grad_mid, *terms))
    low_part, grad_mid, terms = held[0], held[1], held[2:]
    grad_branch = add_all([terms[0]] + [term.astype(f32) for term in terms[1:]])
    grad_branch = grad_branch.reshape(peers, -1, HID + LANE).astype(bf16)
    grad_branch = exchange(grad_branch)
    all_mid = spread_out(grad_mid.astype(bf16)).reshape(-1, HID)
    high_part = rows_part_call((2, 3), window, after(late_back, low_part), 1024)
    held = lax.optimization_barrier((high_part, grad_branch, all_mid))
    high_part, grad_branch, all_mid = held
    grad_branch = jnp.sum(grad_branch.astype(f32), axis=0)
    branch_pieces = row_copies(spread_out(grad_branch.astype(bf16)).reshape(-1, HID + LANE))
    mid_pieces = row_copies(all_mid)
    grad_features = rows_back_call(
        all_rows,
        counts,
        spread,
        (low_part, high_part),
        branch_stats,
        window,
        branch_pieces,
        2048,
    )
    new_logits = join_call(moved, 1024)
    mid_parts = mid_update_call(grad_mid, w_mid, basis_right_mid, first_mid, second_mid)
    new_right_mid = mid_factor_call(right_mid, mid_pieces)
    *branch_parts, grad_out = branch_update_call(
        all_rows,
        branch_stats,
        window,
        branch_pieces,
        by_input(w_branch),
        by_input(left_branch),
        right_branch,
        by_input(basis_left_branch),
        basis_right_branch,
        by_input(first_branch),
        by_input(second_branch),
    )
    branch_parts = [
        part if index == 1 else by_input(part) for index, part in enumerate(branch_parts)
    ]
    out_parts = out_update_call(
        grad_out,
        w_out.T,
        left_out,
        right_out,
        basis_left_out,
        basis_right_out,
        first_out.T,
        second_out.T,
    )
    out_parts = list(out_parts[:2]) + [part.T for part in out_parts[2:]]
    return (new_logits.T, grad_features.T, *branch_parts, new_right_mid, *mid_parts, *out_parts)


def solution(mesh):
    split, rows, whole = P(BOTH, None), P(BOTH), P()
    in_specs = (split, rows, whole, whole, split) + (whole,) * 9 + (split, split) + (whole,) * 6
    out_specs = (split, split) + (whole,) * 7 + (split,) * 4 + (whole,) * 6
    return jax.shard_map(local, mesh=mesh, in_specs=in_specs, out_specs=out_specs, check_vma=False)
```

```python
import functools

import jax
import jax.numpy as jnp
from jax import lax
from jax.experimental import pallas as pl
from jax.experimental.pallas import tpu as pltpu
from jax.sharding import PartitionSpec as P

OPS = 4
DIN = 100
HID = 512
CLS = 47
AVG = 4096
STEP = 5
CAT = 2048
LANE = 128
CPAD = 48
STRIDE = 96
WINDOW = 112
VALID = 400
HEAD = 512
WIDE = 416
SHARE = 12
BOTH = ("row", "col")

beta_first = 0.5
beta_second = 0.9
beta_factor = 0.95
adam_eps = 1e-08
norm_eps = 1e-05
rate_branch = 0.1
rate_mid = 0.02
rate_out = 0.04
f32 = jnp.float32
bf16 = jnp.bfloat16
VMEM_LIMIT = 60 * 2**20


def dot_on(first_arg, second_arg, first_dim, second_dim, precision=None):
    return lax.dot_general(
        first_arg,
        second_arg,
        (((first_dim,), (second_dim,)), ((), ())),
        precision=precision,
        preferred_element_type=f32,
    )


def params():
    return pltpu.CompilerParams(vmem_limit_bytes=VMEM_LIMIT)


def cost(microseconds):
    return pl.CostEstimate(
        flops=int(microseconds * 1e9), bytes_accessed=1, transcendentals=0
    )


def shape(dims, dtype):
    return jax.ShapeDtypeStruct(dims, dtype)


def fixed(dims):
    return pl.BlockSpec(dims, lambda *_: (0,) * len(dims))


def rows_of(block, width):
    return pl.BlockSpec((block, width), lambda i, *_: (i, 0))


def columns_of(height, block):
    return pl.BlockSpec((height, block), lambda i, *_: (0, i))


def low_f32(values):
    return values.astype(bf16).astype(f32)


def split_low(values):
    high = values.astype(bf16)
    return high, (values - high.astype(f32)).astype(bf16)


def fold_rows(values):
    return jnp.sum(values.reshape(values.shape[0] // 8, 8, values.shape[1]), axis=0)


def add_up(ref):
    value = ref[0]
    for index in range(1, ref.shape[0]):
        value = value + ref[index]
    return value


def own_count(counts):
    return counts[lax.axis_index("row"), lax.axis_index("col")]


def branch_scale(stats, op, all_rows):
    mean = stats[op : op + 1, :] / all_rows
    square = stats[OPS + op : OPS + op + 1, :] / all_rows
    return mean, lax.rsqrt(square - mean * mean + norm_eps)


def unpack_pair(packed):
    parts = HID // LANE
    return [
        jnp.concatenate(
            [packed[index * parts + part : index * parts + part + 1, :] for part in range(parts)],
            axis=1,
        )
        for index in range(2)
    ]


def pack_pair(first, second):
    parts = HID // LANE
    return jnp.concatenate(
        [
            value[:, part * LANE : (part + 1) * LANE]
            for value in (first, second)
            for part in range(parts)
        ],
        axis=0,
    )


def mid_scale(stats_ref, all_rows):
    total, square = unpack_pair(add_up(stats_ref))
    mean = total / all_rows
    return mean, lax.rsqrt(square / all_rows - mean * mean + norm_eps)


def window_rows(x_ref, op):
    return jnp.concatenate(
        [x_ref[op * STRIDE : op * STRIDE + WINDOW, :], x_ref[VALID:WIDE, :]], axis=0
    )


def padded(window):
    return jnp.concatenate([window, jnp.zeros((LANE - WINDOW, HID), bf16)], axis=0)


def gram_product(gram, window):
    high, low = split_low(gram)
    weight = padded(window)
    return jnp.dot(high, weight, preferred_element_type=f32) + jnp.dot(
        low, weight, preferred_element_type=f32
    )


def mask_rows(counts, x_ref, held):
    block = x_ref.shape[1]
    column = pl.program_id(0) * block + lax.broadcasted_iota(jnp.int32, (16, block), 1)
    valid = jnp.where(column < own_count(counts), 1.0, 0.0)
    line = lax.broadcasted_iota(jnp.int32, (16, block), 0)
    held[:VALID, :] = x_ref[...] * valid[0:1, :].astype(bf16)
    held[VALID:, :] = jnp.where(line < 2, valid, 0.0).astype(bf16)


def gather_pieces(refs, held):
    row = lax.axis_index("row")
    size = held.shape[0] // len(refs)
    for index, ref in enumerate(refs):
        at = pl.multiple_of((row ^ index) * size, size)
        held[pl.ds(at, size), :] = ref[...].reshape(size, held.shape[1]).astype(held.dtype)


def gram_body(counts, x_ref, w_ref, window_ref, gram_ref, stats_ref, xa_ref):
    step = pl.program_id(0)

    @pl.when(step == 0)
    def _():
        gram_ref[...] = jnp.zeros_like(gram_ref)
        for op in range(OPS):
            shift = op * (DIN - STRIDE)
            parts = [low_f32(w_ref[:, op, :])]
            if shift:
                parts.insert(0, jnp.zeros((shift, HID), f32))
            if WINDOW - DIN - shift:
                parts.append(jnp.zeros((WINDOW - DIN - shift, HID), f32))
            window_ref[op] = jnp.concatenate(parts, axis=0).astype(bf16)

    mask_rows(counts, x_ref, xa_ref)
    for op in range(0, OPS, 2):
        rows = jnp.concatenate([window_rows(xa_ref, op), window_rows(xa_ref, op + 1)], axis=0)
        both = dot_on(rows, rows, 1, 1)
        gram_ref[op] += both[:LANE, :LANE]
        gram_ref[op + 1] += both[LANE:, LANE:]

    @pl.when(step == pl.num_programs(0) - 1)
    def _():
        for op in range(OPS):
            turned = gram_product(gram_ref[op], window_ref[op])
            stats_ref[op : op + 1, :] = turned[WINDOW : WINDOW + 1, :]
            stats_ref[OPS + op : OPS + op + 1, :] = jnp.sum(
                window_ref[op].astype(f32) * turned[:WINDOW, :], axis=0, keepdims=True
            )


def gram_call(counts, features, w_branch, block):
    total = features.shape[1]
    return pl.pallas_call(
        gram_body,
        grid_spec=pltpu.PrefetchScalarGridSpec(
            num_scalar_prefetch=1,
            grid=(total // block,),
            in_specs=[columns_of(VALID, block), fixed((DIN, OPS, HID))],
            out_specs=[
                fixed((OPS, WINDOW, HID)),
                fixed((OPS, LANE, LANE)),
                fixed((2 * OPS, HID)),
            ],
            scratch_shapes=[pltpu.VMEM((WIDE, block), bf16)],
        ),
        out_shape=[
            shape((OPS, WINDOW, HID), bf16),
            shape((OPS, LANE, LANE), f32),
            shape((2 * OPS, HID), f32),
        ],
        compiler_params=params(),
        cost_estimate=cost(6),
        name="row_moments",
    )(counts, features, w_branch)


def forward_body(all_rows, count, counts, *refs):
    x_ref, stats_ref, window_ref = refs[:3]
    pieces = refs[3 : 3 + count]
    pre_ref, joined_ref, slope_ref, wm_ref, out_ref, wide, total, xa_ref = refs[3 + count :]
    step = pl.program_id(0)

    @pl.when(step == 0)
    def _():
        total[...] = jnp.zeros_like(total)
        gather_pieces(pieces, wm_ref)
        stats = add_up(stats_ref)
        line = lax.broadcasted_iota(jnp.int32, (LANE - WINDOW, HID), 0)
        for op in range(OPS):
            mean, scale = branch_scale(stats, op, all_rows)
            half = 0.5 * scale
            high, low = split_low(window_ref[op].astype(f32) * half)
            base = -mean * half
            base_high = low_f32(base)
            wide[op, :WINDOW, :] = high
            wide[op, WINDOW:LANE, :] = jnp.where(
                line == 0, base_high, jnp.where(line == 1, base - base_high, 0.0)
            ).astype(bf16)
            wide[op, LANE : LANE + WINDOW, :] = low
            wide[op, LANE + WINDOW :, :] = jnp.zeros((LANE - WINDOW, HID), bf16)

    mask_rows(counts, x_ref, xa_ref)
    pre = None
    for op in range(OPS):
        rows = window_rows(xa_ref, op).T
        half = jnp.dot(
            jnp.concatenate([rows, rows], axis=1), wide[op], preferred_element_type=f32
        ).astype(bf16)
        first = jnp.tanh(half) + 1.0
        act = half * first
        half_act = act * 0.5
        second = jnp.tanh(half_act) + 1.0
        joined = half_act * second
        slope = (first * ((half - half_act) + 0.5)) * (second * ((act - joined) + 1.0))
        joined_ref[:, op * HID : (op + 1) * HID] = joined
        slope_ref[:, op * HID : (op + 1) * HID] = slope
        term = jnp.dot(
            joined, wm_ref[op * HID : (op + 1) * HID, :], preferred_element_type=f32
        )
        pre = term if pre is None else pre + term
    pre_ref[...] = pre.astype(bf16)
    total[0] += fold_rows(pre)
    total[1] += fold_rows(pre * pre)

    @pl.when(step == pl.num_programs(0) - 1)
    def _():
        packed = pack_pair(
            jnp.sum(total[0], axis=0, keepdims=True), jnp.sum(total[1], axis=0, keepdims=True)
        )
        for index in range(out_ref.shape[0]):
            out_ref[index] = packed


def forward_call(all_rows, devices, counts, features, stats, window, pieces, block):
    total = features.shape[1]
    count = len(pieces)
    return pl.pallas_call(
        functools.partial(forward_body, all_rows, count),
        grid_spec=pltpu.PrefetchScalarGridSpec(
            num_scalar_prefetch=1,
            grid=(total // block,),
            in_specs=[
                columns_of(VALID, block),
                fixed(stats.shape),
                fixed((OPS, WINDOW, HID)),
            ]
            + [fixed(piece.shape) for piece in pieces],
            out_specs=[
                rows_of(block, HID),
                rows_of(block, CAT),
                rows_of(block, CAT),
                fixed((CAT, HID)),
                fixed((devices, 8, LANE)),
            ],
            scratch_shapes=[
                pltpu.VMEM((OPS, 2 * LANE, HID), bf16),
                pltpu.VMEM((2, 8, HID), f32),
                pltpu.VMEM((WIDE, block), bf16),
            ],
        ),
        out_shape=[
            shape((total, HID), bf16),
            shape((total, CAT), bf16),
            shape((total, CAT), bf16),
            shape((CAT, HID), bf16),
            shape((devices, 8, LANE), f32),
        ],
        compiler_params=params(),
        cost_estimate=cost(44),
        name="forward_layers",
    )(counts, features, stats, window, *pieces)


def head_body(
    all_rows,
    counts,
    pre_ref,
    stats_ref,
    wo_ref,
    labels_ref,
    back_ref,
    logits_ref,
    grad_ref,
    sums_ref,
    wo_low,
    norm,
    total,
):
    step = pl.program_id(0)
    block = pre_ref.shape[0]

    @pl.when(step == 0)
    def _():
        total[...] = jnp.zeros_like(total)
        grad_ref[...] = jnp.zeros_like(grad_ref)
        wo_low[...] = jnp.concatenate(
            [wo_ref[...], jnp.zeros((CPAD - CLS, HID), f32)], axis=0
        ).astype(bf16)
        mean, scale = mid_scale(stats_ref, all_rows)
        norm[0:1, :] = 0.5 * scale
        norm[1:2, :] = -0.5 * scale * mean

    kind = lax.broadcasted_iota(jnp.int32, (CPAD, HEAD), 0)
    for start in range(0, block, HEAD):
        rows = slice(start, start + HEAD)
        half = pre_ref[rows, :].astype(f32) * norm[0:1, :] + norm[1:2, :]
        raised = jnp.tanh(half) + 1.0
        hidden = half * raised
        slope = raised * ((half - 0.5 * hidden) + 0.5)
        hidden = hidden.astype(bf16)
        logits = dot_on(wo_low[...], hidden, 1, 1)
        logits_ref[:, rows] = logits.astype(bf16)
        column = step * block + start + lax.broadcasted_iota(jnp.int32, (CPAD, HEAD), 1)
        real = kind < CLS
        top = jnp.max(jnp.where(real, logits, -jnp.inf), axis=0, keepdims=True)
        powers = jnp.where(real, jnp.exp(logits - top), 0.0)
        probs = powers / jnp.sum(powers, axis=0, keepdims=True)
        score = (probs - jnp.where(kind == labels_ref[:, rows], 1.0, 0.0)) / all_rows
        score = jnp.where(column < own_count(counts), score, 0.0).astype(bf16)
        grad_ref[...] += dot_on(score, hidden, 1, 0)
        back = dot_on(score, wo_low[...], 0, 0) * slope
        total[0] += fold_rows(back)
        total[1] += fold_rows(back * half)
        back_ref[rows, :] = back.astype(bf16)

    @pl.when(step == pl.num_programs(0) - 1)
    def _():
        packed = pack_pair(
            jnp.sum(total[0], axis=0, keepdims=True),
            2.0 * jnp.sum(total[1], axis=0, keepdims=True),
        )
        for index in range(sums_ref.shape[0]):
            sums_ref[index] = packed


def head_call(all_rows, counts, pre, stats, w_out, labels, block):
    total = pre.shape[0]
    return pl.pallas_call(
        functools.partial(head_body, all_rows),
        grid_spec=pltpu.PrefetchScalarGridSpec(
            num_scalar_prefetch=1,
            grid=(total // block,),
            in_specs=[
                rows_of(block, HID),
                fixed(stats.shape),
                fixed((CLS, HID)),
                columns_of(1, block),
            ],
            out_specs=[
                rows_of(block, HID),
                columns_of(CPAD, block),
                fixed((CPAD, HID)),
                fixed(stats.shape),
            ],
            scratch_shapes=[
                pltpu.VMEM((CPAD, HID), bf16),
                pltpu.VMEM((8, HID), f32),
                pltpu.VMEM((2, 8, HID), f32),
            ],
        ),
        out_shape=[
            shape((total, HID), bf16),
            shape((CPAD, total), bf16),
            shape((CPAD, HID), f32),
            shape(stats.shape, f32),
        ],
        compiler_params=params(),
        cost_estimate=cost(18),
        name="head",
    )(counts, pre, stats, w_out, labels)


def add_windows(pieces, write):
    for op, piece in enumerate(pieces):
        start = op * STRIDE
        skip = WINDOW - STRIDE if op else 0
        stop = WINDOW if op == OPS - 1 else STRIDE
        if op:
            write(start, pieces[op - 1][STRIDE:WINDOW, :] + piece[:skip, :])
        write(start + skip, piece[skip:stop, :])


def branch_back_body(
    all_rows,
    counts,
    pre_ref,
    back_ref,
    slope_ref,
    x_ref,
    wm_ref,
    window_ref,
    mid_stats_ref,
    sums_ref,
    stats_ref,
    grad_out_ref,
    gram_ref,
    mid_ref,
    part_ref,
    all_ref,
    norm,
    halved,
    grad,
    xa_ref,
):
    step = pl.program_id(0)

    @pl.when(step == 0)
    def _():
        grad[...] = jnp.zeros_like(grad)
        stats = add_up(stats_ref)
        for op in range(OPS):
            halved[op : op + 1, :] = 0.5 * branch_scale(stats, op, all_rows)[1]
        mean, scale = mid_scale(mid_stats_ref, all_rows)
        level, slant = unpack_pair(add_up(sums_ref))
        slant = scale * scale * (slant / all_rows)
        norm[0:1, :] = scale
        norm[1:2, :] = slant
        norm[2:3, :] = mean * slant - scale * (level / all_rows)

    mask_rows(counts, x_ref, xa_ref)
    mid = (
        back_ref[...].astype(f32) * norm[0:1, :]
        - pre_ref[...].astype(f32) * norm[1:2, :]
        + norm[2:3, :]
    ).astype(bf16)
    mid_ref[...] = mid
    pieces = []
    for op in range(OPS):
        span = slice(op * HID, (op + 1) * HID)
        joined_back = dot_on(mid, wm_ref[span, :], 1, 1)
        back = (
            (joined_back * halved[op : op + 1, :]) * slope_ref[:, span].astype(f32)
        ).astype(bf16)
        line = slice(op * LANE, (op + 1) * LANE)
        grad[line, :HID] += dot_on(window_rows(xa_ref, op), back, 1, 0)
        pieces.append(dot_on(window_ref[op], back, 1, 1))

    def write(at, value):
        part_ref[at : at + value.shape[0], :] = value.astype(bf16)

    add_windows(pieces, write)

    @pl.when(step == pl.num_programs(0) - 1)
    def _():
        for op in range(OPS):
            start = op * LANE
            grad[start : start + LANE, HID:] = gram_ref[op]
            grad[start : start + LANE, :HID] = jnp.concatenate(
                [
                    grad[start : start + WINDOW + 1, :HID],
                    grad_out_ref[op * SHARE : (op + 1) * SHARE, :],
                    jnp.zeros((LANE - WINDOW - 1 - SHARE, HID), f32),
                ],
                axis=0,
            )
        size = all_ref.shape[1]
        for index in range(all_ref.shape[0]):
            all_ref[index] = grad[index * size : (index + 1) * size, :].astype(bf16)


def branch_back_call(
    all_rows,
    devices,
    counts,
    pre,
    back,
    slope,
    features,
    mid_low,
    window,
    mid_stats,
    sums,
    stats,
    grad_out,
    gram,
    block,
):
    total = pre.shape[0]
    wide = HID + LANE
    parts = (devices, OPS * LANE // devices, wide)
    return pl.pallas_call(
        functools.partial(branch_back_body, all_rows),
        grid_spec=pltpu.PrefetchScalarGridSpec(
            num_scalar_prefetch=1,
            grid=(total // block,),
            in_specs=[
                rows_of(block, HID),
                rows_of(block, HID),
                rows_of(block, CAT),
                columns_of(VALID, block),
                fixed((CAT, HID)),
                fixed((OPS, WINDOW, HID)),
                fixed(mid_stats.shape),
                fixed(sums.shape),
                fixed(stats.shape),
                fixed((CPAD, HID)),
                fixed((OPS, LANE, LANE)),
            ],
            out_specs=[rows_of(block, HID), columns_of(VALID, block), fixed(parts)],
            scratch_shapes=[
                pltpu.VMEM((8, HID), f32),
                pltpu.VMEM((8, HID), f32),
                pltpu.VMEM((OPS * LANE, wide), f32),
                pltpu.VMEM((WIDE, block), bf16),
            ],
        ),
        out_shape=[shape((total, HID), bf16), shape((VALID, total), bf16), shape(parts, bf16)],
        compiler_params=params(),
        cost_estimate=cost(48),
        name="branch_back",
    )(counts, pre, back, slope, features, mid_low, window, mid_stats, sums, stats, grad_out, gram)


def mid_grad_body(mid_ref, joined_ref, *refs):
    step = pl.program_id(0)
    parts, grad = refs[:-1], refs[-1]

    @pl.when(step == 0)
    def _():
        grad[...] = jnp.zeros_like(grad)

    for op in range(OPS):
        span = slice(op * HID, (op + 1) * HID)
        grad[span, :] += dot_on(joined_ref[:, span], mid_ref[...], 0, 0)

    @pl.when(step == pl.num_programs(0) - 1)
    def _():
        groups = lax.axis_size("row")
        row = lax.axis_index("row")
        core, far = lax.rem(row, 2), row // (groups // 2)
        pairs, size = parts[0].shape[0], parts[0].shape[1]
        for index, part in enumerate(parts):
            which = core if index < 2 else 1 - core
            half = far if index % 2 == 0 else 1 - far
            for pair in range(pairs):
                chunk = 2 * (half * pairs + pair) + which
                part[pair] = grad[pl.ds(pl.multiple_of(chunk * size, size), size), :]


def mid_grad_call(groups, mid, joined, block):
    total = mid.shape[0]
    parted = (groups // 4, CAT // groups, HID)
    return pl.pallas_call(
        mid_grad_body,
        grid=(total // block,),
        in_specs=[rows_of(block, HID), rows_of(block, CAT)],
        out_specs=[fixed(parted)] * 4,
        out_shape=[shape(parted, f32)] * 4,
        scratch_shapes=[pltpu.VMEM((CAT, HID), f32)],
        compiler_params=params(),
        cost_estimate=cost(25),
        name="mid_grad",
    )(mid, joined)


def branch_terms(all_rows, mean, scale, window, raw):
    level = raw[WINDOW : WINDOW + 1, :]
    inner = scale * (
        jnp.sum(window.astype(f32) * raw[:WINDOW, :], axis=0, keepdims=True) - mean * level
    )
    return level / all_rows, scale * (inner / all_rows)


def rows_back_body(
    all_rows,
    counts,
    x_ref,
    part_ref,
    stats_ref,
    window_ref,
    grads,
    out_ref,
    inner,
    base,
):
    step = pl.program_id(0)
    block = x_ref.shape[1]

    @pl.when(step == 0)
    def _():
        stats = add_up(stats_ref)
        for op in range(OPS):
            mean, scale = branch_scale(stats, op, all_rows)
            window = window_ref[op]
            level, slant = branch_terms(
                all_rows, mean, scale, window, grads[op * LANE : (op + 1) * LANE, :HID].astype(f32)
            )
            inner[op] = dot_on((window.astype(f32) * -slant).astype(bf16), window, 1, 1).astype(bf16)
            base[op] = jnp.sum(
                window.astype(f32) * (mean * slant - level), axis=1, keepdims=True
            )

    moved = []
    for op in range(OPS):
        rows = x_ref[op * STRIDE : op * STRIDE + WINDOW, :]
        moved.append(jnp.dot(inner[op], rows, preferred_element_type=f32) + base[op])
    column = step * block + lax.broadcasted_iota(jnp.int32, (1, block), 1)
    valid = column < own_count(counts)

    def write(at, value):
        span = slice(at, at + value.shape[0])
        value = jnp.where(valid, value + part_ref[span, :].astype(f32), 0.0)
        out_ref[span, :] = value.astype(bf16)

    add_windows(moved, write)


def rows_back_call(all_rows, counts, features, part, stats, window, grads, block):
    total = features.shape[1]
    return pl.pallas_call(
        functools.partial(rows_back_body, all_rows),
        grid_spec=pltpu.PrefetchScalarGridSpec(
            num_scalar_prefetch=1,
            grid=(total // block,),
            in_specs=[
                columns_of(VALID, block),
                columns_of(VALID, block),
                fixed(stats.shape),
                fixed((OPS, WINDOW, HID)),
                fixed(grads.shape),
            ],
            out_specs=columns_of(VALID, block),
            scratch_shapes=[
                pltpu.VMEM((OPS, WINDOW, WINDOW), bf16),
                pltpu.VMEM((OPS, WINDOW, 1), f32),
            ],
        ),
        out_shape=shape((VALID, total), bf16),
        compiler_params=params(),
        cost_estimate=cost(8),
        name="rows_back",
    )(counts, features, part, stats, window, grads)


def slots_of(rows, peers):
    return -(-(rows // LANE + 1) // peers)


def first_row(counts, source):
    row = lax.axis_index("row")
    begin = jnp.int32(0)
    for peer in range(counts.shape[1]):
        begin += jnp.where(peer < source, counts[row, peer], 0)
    return begin


def deal_body(counts, logits_ref, out_ref):
    peers = out_ref.shape[0]
    tiles = logits_ref.shape[1] // LANE
    begin = first_row(counts, lax.axis_index("col"))
    count = own_count(counts)
    shift = lax.rem(begin, LANE)
    chunk = begin // LANE
    lane = lax.broadcasted_iota(jnp.int32, (CPAD, LANE), 1)
    empty = jnp.zeros((CPAD, LANE), f32)
    left = empty
    for tile in range(peers * (out_ref.shape[2] // LANE)):
        right = empty
        if tile < tiles:
            piece = logits_ref[:, tile * LANE : (tile + 1) * LANE].astype(f32)
            piece = jnp.where(tile * LANE + lane < count, piece, 0.0)
            right = pltpu.roll(piece, shift, 1)
        slot = tile // peers * LANE
        peer = lax.rem(chunk + tile, peers)
        out_ref[peer, :, slot : slot + LANE] = jnp.where(lane < shift, left, right).astype(bf16)
        left = right


def deal_call(counts, logits, peers):
    total = logits.shape[1]
    dealt = (peers, CPAD, slots_of(total, peers) * LANE)
    return pl.pallas_call(
        deal_body,
        grid_spec=pltpu.PrefetchScalarGridSpec(
            num_scalar_prefetch=1,
            grid=(1,),
            in_specs=[fixed((CPAD, total))],
            out_specs=fixed(dealt),
        ),
        out_shape=shape(dealt, bf16),
        compiler_params=params(),
        cost_estimate=cost(3),
        name="deal_logits",
    )(counts, logits)


def collect_body(counts, dealt_ref, out_ref, held):
    peers, _, width = dealt_ref.shape
    member = lax.axis_index("col")
    held[...] = jnp.zeros_like(held)
    for source in range(peers):
        chunk = first_row(counts, source) // LANE
        ahead = lax.rem(member + peers - lax.rem(chunk, peers), peers)
        at = pl.ds(pl.multiple_of((chunk + ahead) // peers * LANE, LANE), width)
        held[:, at] += dealt_ref[source].astype(f32)
    share = out_ref.shape[2]
    for peer in range(peers):
        out_ref[peer] = held[:, peer * share : (peer + 1) * share].astype(bf16)


def collect_call(counts, dealt):
    peers, height, width = dealt.shape
    collected = (peers, height, AVG // peers)
    return pl.pallas_call(
        collect_body,
        grid_spec=pltpu.PrefetchScalarGridSpec(
            num_scalar_prefetch=1,
            grid=(1,),
            in_specs=[fixed(dealt.shape)],
            out_specs=fixed(collected),
            scratch_shapes=[pltpu.VMEM((height, AVG + LANE + width), f32)],
        ),
        out_shape=shape(collected, bf16),
        compiler_params=params(),
        cost_estimate=cost(3),
        name="collect_logits",
    )(counts, dealt)


def join_body(pieces_ref, out_ref):
    peers, _, share = pieces_ref.shape
    for peer in range(peers):
        for index in range(share // LANE):
            at = (index * peers + peer) * LANE
            piece = pieces_ref[peer, :, index * LANE : (index + 1) * LANE].astype(f32)
            out_ref[:, at : at + LANE] = piece[:CLS, :]


def join_call(pieces):
    return pl.pallas_call(
        join_body,
        out_shape=shape((CLS, AVG), f32),
        compiler_params=params(),
        cost_estimate=cost(2),
        name="join_logits",
    )(pieces)


def moments(turned, first, second):
    new_first = beta_first * first + (1.0 - beta_first) * turned
    new_second = beta_second * second + (1.0 - beta_second) * turned * turned
    direction = (
        new_first
        / (1.0 - beta_first**STEP)
        / (jnp.sqrt(new_second / (1.0 - beta_second**STEP)) + adam_eps)
    )
    return new_first, new_second, direction


def dot_parts(first_arg, second_arg, first_dim, second_dim):
    first_high, first_low = split_low(first_arg)
    second_high, second_low = split_low(second_arg)
    return dot_on(first_high, second_high, first_dim, second_dim) + (
        dot_on(first_high, second_low, first_dim, second_dim)
        + dot_on(first_low, second_high, first_dim, second_dim)
    )


def factor(old, grad, dim):
    low = grad.astype(bf16)
    return beta_factor * old + (1.0 - beta_factor) * dot_on(low, low, dim, dim)


def branch_update_body(
    all_rows,
    stats_ref,
    window_ref,
    grads,
    w_ref,
    left_ref,
    right_ref,
    basis_left_ref,
    basis_right_ref,
    first_ref,
    second_ref,
    new_left_ref,
    new_right_ref,
    new_first_ref,
    new_second_ref,
    new_w_ref,
    low_w_ref,
    grad_out_ref,
):
    step = pl.program_id(0)

    @pl.when(step == 0)
    def _():
        for op in range(OPS):
            at = op * LANE + WINDOW + 1
            grad_out_ref[op * SHARE : (op + 1) * SHARE, :] = grads[at : at + SHARE, :HID].astype(f32)

    for op in range(OPS):

        @pl.when(step == op)
        def _(op=op):
            mean, scale = branch_scale(add_up(stats_ref), op, all_rows)
            window = window_ref[op]
            raw = grads[op * LANE : (op + 1) * LANE, :HID].astype(f32)
            gram = grads[op * LANE : (op + 1) * LANE, HID:].astype(f32)
            level, slant = branch_terms(all_rows, mean, scale, window, raw)
            column = gram[:WINDOW, WINDOW : WINDOW + 1]
            normed = gram_product(gram, window)[:WINDOW, :] - column * mean
            grad = raw[:WINDOW, :] - column * level - normed * slant
            shift = op * (DIN - STRIDE)
            grad = grad[shift : shift + DIN, :]
            new_left_ref[:, op, :] = factor(left_ref[:, op, :], grad, 1)
            new_right_ref[0] = factor(right_ref[0], grad, 0)
            basis_left, basis_right = basis_left_ref[:, op, :], basis_right_ref[0]
            turned = dot_parts(basis_left, grad, 0, 0)
            turned = dot_parts(turned, basis_right, 1, 0)
            new_first, new_second, direction = moments(
                turned, first_ref[:, op, :], second_ref[:, op, :]
            )
            new_first_ref[:, op, :] = new_first
            new_second_ref[:, op, :] = new_second
            back = dot_parts(basis_left, direction, 1, 0)
            back = dot_parts(back, basis_right, 1, 1)
            new_w = w_ref[:, op, :] - rate_branch * back
            new_w_ref[:, op, :] = new_w
            low_w_ref[:, op, :] = new_w.astype(bf16)


def branch_update_call(
    all_rows, stats, window, grads, w, left, right, basis_left, basis_right, first, second
):
    small, wide = fixed((DIN, OPS, DIN)), fixed((DIN, OPS, HID))
    square = pl.BlockSpec((1, HID, HID), lambda k: (k, 0, 0))
    return pl.pallas_call(
        functools.partial(branch_update_body, all_rows),
        grid=(OPS,),
        in_specs=[fixed(stats.shape), fixed((OPS, WINDOW, HID)), fixed(grads.shape)]
        + [wide, small, square, small, square, wide, wide],
        out_specs=[small, square, wide, wide, wide, wide, fixed((CPAD, HID))],
        out_shape=[
            shape((DIN, OPS, DIN), f32),
            shape((OPS, HID, HID), f32),
            shape((DIN, OPS, HID), f32),
            shape((DIN, OPS, HID), f32),
            shape((DIN, OPS, HID), f32),
            shape((DIN, OPS, HID), bf16),
            shape((CPAD, HID), f32),
        ],
        compiler_params=params(),
        cost_estimate=cost(12),
        name="branch_update",
    )(stats, window, grads, w, left, right, basis_left, basis_right, first, second)


def out_update_body(
    grad_ref,
    w_ref,
    left_ref,
    right_ref,
    basis_left_ref,
    basis_right_ref,
    first_ref,
    second_ref,
    new_left_ref,
    new_right_ref,
    new_first_ref,
    new_second_ref,
    new_w_ref,
    low_w_ref,
):
    grad = grad_ref[:CLS, :]
    new_left_ref[...] = factor(left_ref[...], grad, 0)
    new_right_ref[...] = factor(right_ref[...], grad, 1)
    turned = dot_parts(grad, basis_left_ref[...], 1, 0)
    turned = dot_parts(basis_right_ref[...], turned, 0, 0)
    new_first, new_second, direction = moments(turned, first_ref[...], second_ref[...])
    new_first_ref[...] = new_first
    new_second_ref[...] = new_second
    back = dot_parts(direction, basis_left_ref[...], 1, 1)
    back = dot_parts(basis_right_ref[...], back, 1, 0)
    new_w = w_ref[...] - rate_out * back
    new_w_ref[...] = new_w
    low_w_ref[...] = new_w.astype(bf16)


def out_update_call(grad, w, left, right, basis_left, basis_right, first, second):
    return pl.pallas_call(
        out_update_body,
        out_shape=[
            shape((HID, HID), f32),
            shape((CLS, CLS), f32),
            shape((CLS, HID), f32),
            shape((CLS, HID), f32),
            shape((CLS, HID), f32),
            shape((CLS, HID), bf16),
        ],
        compiler_params=params(),
        cost_estimate=cost(4),
        name="out_update",
    )(grad, w, left, right, basis_left, basis_right, first, second)


def mid_update_body(
    grad_ref, w_ref, basis_ref, first_ref, second_ref, new_first_ref, new_second_ref, new_w_ref, low_w_ref
):
    turned = dot_parts(grad_ref[...], basis_ref[...], 1, 0)
    new_first, new_second, direction = moments(turned, first_ref[...], second_ref[...])
    new_first_ref[...] = new_first
    new_second_ref[...] = new_second
    new_w = w_ref[...] - rate_mid * dot_parts(direction, basis_ref[...], 1, 1)
    new_w_ref[...] = new_w
    low_w_ref[...] = new_w.astype(bf16)


def mid_update_call(grad, w, basis, first, second):
    rows = grad.shape[0]
    return pl.pallas_call(
        mid_update_body,
        out_shape=[shape((rows, HID), f32)] * 3 + [shape((rows, HID), bf16)],
        compiler_params=params(),
        cost_estimate=cost(3),
        name="mid_update",
    )(grad, w, basis, first, second)


def mid_gram_body(rows_ref, out_ref):
    rows = rows_ref[...]
    out_ref[...] = dot_on(rows, rows, 0, 0).astype(bf16)


def mid_gram_call(rows):
    return pl.pallas_call(
        mid_gram_body,
        out_shape=shape((HID, HID), bf16),
        compiler_params=params(),
        cost_estimate=cost(2),
        name="mid_gram",
    )(rows)


def after(values, *others):
    return lax.optimization_barrier((values,) + others)[0]


def swap(values, axis, distance):
    peers = lax.axis_size(axis)
    return lax.ppermute(values, axis, [(peer, peer ^ distance) for peer in range(peers)])


def add_all(values):
    while len(values) > 1:
        values = [values[i] + values[i + 1] for i in range(0, len(values), 2)]
    return values[0]


def exchange(values):
    return lax.all_to_all(values, "col", 0, 0, tiled=True)


def spread_out(values, dtype=f32):
    copies = jnp.broadcast_to(values[None], (lax.axis_size("col"),) + values.shape)
    return exchange(copies.astype(dtype))


def far_copies(values):
    pieces = {0: values}
    distance = lax.axis_size("row") // 2
    while distance > 1:
        pieces.update({d ^ distance: swap(v, "row", distance) for d, v in list(pieces.items())})
        distance //= 2
    return pieces


def near_copies(pieces, *others):
    held = lax.optimization_barrier((*[pieces[d] for d in sorted(pieces)], *others))
    pieces = dict(zip(sorted(pieces), held))
    pieces.update({d ^ 1: swap(v, "row", 1) for d, v in list(pieces.items())})
    return [pieces[d] for d in sorted(pieces)], held[len(held) - len(others) :]


def sum_in_row(values):
    return add_all([values] + [swap(values, "row", d) for d in range(1, lax.axis_size("row"))])


def keep_bit(values, distance):
    bit = lax.rem(lax.axis_index("row") // distance, 2)
    pairs = values.reshape((-1, 2) + values.shape[1:])
    kept = lax.dynamic_index_in_dim(pairs, bit, 1, keepdims=False)
    sent = lax.dynamic_index_in_dim(pairs, 1 - bit, 1, keepdims=False)
    return kept, sent


def finish_scatter(values, distance):
    while distance < lax.axis_size("row") // 2:
        kept, sent = keep_bit(values, distance)
        values = kept + swap(sent.astype(bf16), "row", distance).astype(f32)
        distance *= 2
    values = values.reshape((lax.axis_size("col"), -1) + values.shape[2:]).astype(bf16)
    return jnp.sum(exchange(values).astype(f32), axis=0)


def local(
    features,
    labels,
    counts,
    w_branch,
    w_mid,
    w_out,
    left_branch,
    right_branch,
    basis_left_branch,
    basis_right_branch,
    first_branch,
    second_branch,
    right_mid,
    basis_right_mid,
    first_mid,
    second_mid,
    left_out,
    right_out,
    basis_left_out,
    basis_right_out,
    first_out,
    second_out,
):
    groups, peers = lax.axis_size("row"), lax.axis_size("col")
    devices = groups * peers
    all_rows = float(AVG * devices)

    def by_input(values):
        return values.transpose(1, 0, 2)

    turned = features.T
    own_mid = spread_out(w_mid, bf16).reshape(-1, HID)
    window, gram, branch_sums = gram_call(counts, turned, by_input(w_branch), 4096)
    branch_sums = sum_in_row(branch_sums)
    own_mid = after(own_mid, branch_sums)
    pieces = far_copies(own_mid)
    branch_stats = spread_out(branch_sums)
    pieces, (branch_stats,) = near_copies(pieces, branch_stats)
    pre, joined, slope, mid_low, mid_sums = forward_call(
        all_rows, devices, counts, turned, branch_stats, window, pieces, 512
    )
    mid_stats = lax.all_to_all(mid_sums, BOTH, 0, 0, tiled=True)
    back, logits, grad_out, back_sums = head_call(
        all_rows, counts, pre, mid_stats, w_out.T, labels.reshape(1, -1), 2048
    )
    back_stats = lax.all_to_all(back_sums, BOTH, 0, 0, tiled=True)

    dealt = deal_call(counts, logits, peers)
    back_stats, dealt = lax.optimization_barrier((back_stats, dealt))
    dealt = exchange(dealt)
    mid, part, grad_branch = branch_back_call(
        all_rows,
        devices,
        counts,
        pre,
        back,
        slope,
        turned,
        mid_low,
        window,
        mid_stats,
        back_stats,
        branch_stats,
        grad_out,
        gram,
        1024,
    )
    grad_branch, dealt = lax.optimization_barrier((grad_branch, dealt))
    grad_branch = lax.all_to_all(grad_branch, BOTH, 0, 0, tiled=True)
    parts = mid_grad_call(groups, mid, joined, 1024)
    grad_branch, *parts = lax.optimization_barrier((grad_branch, *parts))
    kept, sent = parts[:2], parts[2:]
    grad_branch = jnp.sum(grad_branch.astype(f32), axis=0, keepdims=True).astype(bf16)
    grad_branch = jnp.broadcast_to(grad_branch, (devices,) + grad_branch.shape[1:])
    grad_branch = lax.all_to_all(grad_branch, BOTH, 0, 0, tiled=True)
    near = [swap(part, "row", 1) for part in sent]
    away = (kept[1] + near[1]).astype(bf16)
    far = swap(away, "row", groups // 2)
    collected = collect_call(counts, after(dealt, away))
    far, grad_branch, collected = lax.optimization_barrier((far, grad_branch, collected))
    grad_mid = finish_scatter(kept[0] + near[0] + far.astype(f32), 2)
    grad_branch = grad_branch.reshape(OPS * LANE, HID + LANE)
    grad_features = rows_back_call(
        all_rows, counts, turned, part, branch_stats, window, grad_branch, 4096
    )
    grad_mid, grad_features = lax.optimization_barrier((grad_mid, grad_features))
    all_mid = spread_out(grad_mid, bf16).reshape(-1, HID)
    *branch_parts, grad_out = branch_update_call(
        all_rows,
        branch_stats,
        window,
        grad_branch,
        by_input(w_branch),
        by_input(left_branch),
        right_branch,
        by_input(basis_left_branch),
        basis_right_branch,
        by_input(first_branch),
        by_input(second_branch),
    )
    held = lax.optimization_barrier((all_mid, *branch_parts))
    all_mid, branch_parts = held[0], held[1:]
    mid_gram = mid_gram_call(all_mid)
    collected = exchange(after(collected, mid_gram))
    distance = groups // 2
    others = swap(mid_gram, "row", distance)
    mid_parts = mid_update_call(grad_mid, w_mid, basis_right_mid, first_mid, second_mid)
    out_parts = out_update_call(
        grad_out,
        w_out.T,
        left_out,
        right_out,
        basis_left_out,
        basis_right_out,
        first_out.T,
        second_out.T,
    )
    mid_gram, others, collected, *held = lax.optimization_barrier(
        (mid_gram, others, collected, *mid_parts, *out_parts)
    )
    mid_parts, out_parts = held[:4], held[4:]
    mid_gram = mid_gram.astype(f32) + others.astype(f32)
    while distance > 1:
        distance //= 2
        mid_gram = mid_gram + swap(mid_gram, "row", distance)
    new_right_mid = beta_factor * right_mid + (1.0 - beta_factor) * mid_gram
    new_logits = join_call(collected)
    branch_parts = [
        part if index == 1 else by_input(part) for index, part in enumerate(branch_parts)
    ]
    out_parts = list(out_parts[:2]) + [part.T for part in out_parts[2:]]
    return (new_logits.T, grad_features.T, *branch_parts, new_right_mid, *mid_parts, *out_parts)


def solution(mesh):
    split, rows, whole = P(BOTH, None), P(BOTH), P()
    in_specs = (split, rows, whole, whole, split) + (whole,) * 9 + (split, split) + (whole,) * 6
    out_specs = (split, split) + (whole,) * 7 + (split,) * 4 + (whole,) * 6
    return jax.shard_map(local, mesh=mesh, in_specs=in_specs, out_specs=out_specs, check_vma=False)
```

```python
import functools

import jax
import jax.numpy as jnp
from jax import lax
from jax.experimental import pallas as pl
from jax.experimental.pallas import tpu as pltpu
from jax.sharding import PartitionSpec as P

OPS = 4
DIN = 100
HID = 512
CLS = 47
AVG = 4096
STEP = 5
CAT = 2048
LANE = 128
CPAD = 48
STRIDE = 96
WINDOW = 112
VALID = 400
HEAD = 512
WIDE = 416
SHARE = 12
BOTH = ("row", "col")

beta_first = 0.5
beta_second = 0.9
beta_factor = 0.95
adam_eps = 1e-08
norm_eps = 1e-05
rate_branch = 0.1
rate_mid = 0.02
rate_out = 0.04
f32 = jnp.float32
bf16 = jnp.bfloat16
VMEM_LIMIT = 60 * 2**20


def dot_on(first_arg, second_arg, first_dim, second_dim, precision=None):
    return lax.dot_general(
        first_arg,
        second_arg,
        (((first_dim,), (second_dim,)), ((), ())),
        precision=precision,
        preferred_element_type=f32,
    )


def params():
    return pltpu.CompilerParams(vmem_limit_bytes=VMEM_LIMIT)


def cost(microseconds):
    return pl.CostEstimate(
        flops=int(microseconds * 1e9), bytes_accessed=1, transcendentals=0
    )


def shape(dims, dtype):
    return jax.ShapeDtypeStruct(dims, dtype)


def fixed(dims):
    return pl.BlockSpec(dims, lambda *_: (0,) * len(dims))


def rows_of(block, width):
    return pl.BlockSpec((block, width), lambda i, *_: (i, 0))


def columns_of(height, block):
    return pl.BlockSpec((height, block), lambda i, *_: (0, i))


def low_f32(values):
    return values.astype(bf16).astype(f32)


def split_low(values):
    high = values.astype(bf16)
    return high, (values - high.astype(f32)).astype(bf16)


def fold_rows(values):
    return jnp.sum(values.reshape(values.shape[0] // 8, 8, values.shape[1]), axis=0)


def add_up(ref):
    value = ref[0]
    for index in range(1, ref.shape[0]):
        value = value + ref[index]
    return value


def own_count(counts):
    return counts[lax.axis_index("row"), lax.axis_index("col")]


def branch_scale(stats, op, all_rows):
    mean = stats[op : op + 1, :HID] / all_rows
    square = stats[OPS + op : OPS + op + 1, :HID] / all_rows
    return mean, lax.rsqrt(square - mean * mean + norm_eps)


def unpack_pair(packed):
    parts = HID // LANE
    return [
        jnp.concatenate(
            [packed[index * parts + part : index * parts + part + 1, :] for part in range(parts)],
            axis=1,
        )
        for index in range(2)
    ]


def pack_pair(first, second):
    parts = HID // LANE
    return jnp.concatenate(
        [
            value[:, part * LANE : (part + 1) * LANE]
            for value in (first, second)
            for part in range(parts)
        ],
        axis=0,
    )


def mid_scale(stats_ref, all_rows):
    total, square = unpack_pair(add_up(stats_ref))
    mean = total / all_rows
    return mean, lax.rsqrt(square / all_rows - mean * mean + norm_eps)


def window_rows(x_ref, op):
    return jnp.concatenate(
        [x_ref[op * STRIDE : op * STRIDE + WINDOW, :], x_ref[VALID:WIDE, :]], axis=0
    )


def padded(window):
    return jnp.concatenate([window, jnp.zeros((LANE - WINDOW, HID), bf16)], axis=0)


def gram_product(gram, window):
    weight = padded(window)
    product = None
    for _ in range(3):
        part = gram.astype(bf16)
        gram = gram - part.astype(f32)
        term = jnp.dot(part, weight, preferred_element_type=f32)
        product = term if product is None else product + term
    return product


def mask_rows(counts, x_ref, held):
    block = x_ref.shape[1]
    column = pl.program_id(0) * block + lax.broadcasted_iota(jnp.int32, (16, block), 1)
    valid = jnp.where(column < own_count(counts), 1.0, 0.0)
    line = lax.broadcasted_iota(jnp.int32, (16, block), 0)
    held[:VALID, :] = x_ref[...] * valid[0:1, :].astype(bf16)
    held[VALID:, :] = jnp.where(line < 2, valid, 0.0).astype(bf16)


def doubling_steps():
    steps = []
    distance = lax.axis_size("row") // 2
    while distance > 1:
        steps.append(("row", distance))
        distance //= 2
    distance = lax.axis_size("col") // 2
    while distance:
        steps.append(("col", distance))
        distance //= 2
    return steps + [("row", 1)]


def owned_order(devices):
    peers = lax.axis_size("col")
    order = []
    for device in range(devices):
        place = {"row": device // peers, "col": device % peers}
        bits = [place[axis] // distance % 2 for axis, distance in doubling_steps()]
        order.append(sum(bit << index for index, bit in enumerate(bits)))
    return order


def gather_halves(own_ref, near_ref, held):
    core = lax.rem(lax.axis_index("row"), 2)
    size = own_ref.shape[0]
    held[pl.ds(pl.multiple_of(core * size, size), size), :] = own_ref[...]
    held[pl.ds(pl.multiple_of((1 - core) * size, size), size), :] = near_ref[...]


def gather_pieces(refs, held):
    row = lax.axis_index("row")
    size = held.shape[0] // len(refs)
    for index, ref in enumerate(refs):
        at = pl.multiple_of((row ^ index) * size, size)
        held[pl.ds(at, size), :] = ref[...].reshape(size, held.shape[1]).astype(held.dtype)


def gram_body(counts, x_ref, w_ref, window_ref, gram_ref, stats_ref, xa_ref):
    step = pl.program_id(0)

    @pl.when(step == 0)
    def _():
        gram_ref[...] = jnp.zeros_like(gram_ref)
        for op in range(OPS):
            shift = op * (DIN - STRIDE)
            parts = [low_f32(w_ref[:, op, :])]
            if shift:
                parts.insert(0, jnp.zeros((shift, HID), f32))
            if WINDOW - DIN - shift:
                parts.append(jnp.zeros((WINDOW - DIN - shift, HID), f32))
            window_ref[op] = jnp.concatenate(parts, axis=0).astype(bf16)

    mask_rows(counts, x_ref, xa_ref)
    for op in range(0, OPS, 2):
        rows = jnp.concatenate([window_rows(xa_ref, op), window_rows(xa_ref, op + 1)], axis=0)
        both = dot_on(rows, rows, 1, 1)
        gram_ref[op] += both[:LANE, :LANE]
        gram_ref[op + 1] += both[LANE:, LANE:]

    @pl.when(step == pl.num_programs(0) - 1)
    def _():
        for op in range(OPS):
            turned = gram_product(gram_ref[op], window_ref[op])
            stats_ref[op : op + 1, :HID] = turned[WINDOW : WINDOW + 1, :]
            stats_ref[OPS + op : OPS + op + 1, :HID] = jnp.sum(
                window_ref[op].astype(f32) * turned[:WINDOW, :], axis=0, keepdims=True
            )
            stats_ref[op : op + 1, HID:] = gram_ref[op, WINDOW : WINDOW + 1, :]
            stats_ref[OPS + op : OPS + op + 1, HID:] = jnp.zeros((1, LANE), f32)


def gram_call(counts, features, w_branch, block):
    total = features.shape[1]
    return pl.pallas_call(
        gram_body,
        grid_spec=pltpu.PrefetchScalarGridSpec(
            num_scalar_prefetch=1,
            grid=(total // block,),
            in_specs=[columns_of(VALID, block), fixed((DIN, OPS, HID))],
            out_specs=[
                fixed((OPS, WINDOW, HID)),
                fixed((OPS, LANE, LANE)),
                fixed((2 * OPS, HID + LANE)),
            ],
            scratch_shapes=[pltpu.VMEM((WIDE, block), bf16)],
        ),
        out_shape=[
            shape((OPS, WINDOW, HID), bf16),
            shape((OPS, LANE, LANE), f32),
            shape((2 * OPS, HID + LANE), f32),
        ],
        compiler_params=params(),
        cost_estimate=cost(6),
        name="row_moments",
    )(counts, features, w_branch)


def forward_body(all_rows, count, counts, *refs):
    x_ref, stats_ref, window_ref = refs[:3]
    pieces = refs[3 : 3 + count]
    pre_ref, joined_ref, slope_ref, wm_ref, out_ref, wide, total, xa_ref = refs[3 + count :]
    step = pl.program_id(0)

    @pl.when(step == 0)
    def _():
        total[...] = jnp.zeros_like(total)
        gather_pieces(pieces, wm_ref)
        stats = add_up(stats_ref)
        line = lax.broadcasted_iota(jnp.int32, (LANE - WINDOW, HID), 0)
        for op in range(OPS):
            mean, scale = branch_scale(stats, op, all_rows)
            half = 0.5 * scale
            high, low = split_low(window_ref[op].astype(f32) * half)
            base = -mean * half
            base_high = low_f32(base)
            wide[op, :WINDOW, :] = high
            wide[op, WINDOW:LANE, :] = jnp.where(
                line == 0, base_high, jnp.where(line == 1, base - base_high, 0.0)
            ).astype(bf16)
            wide[op, LANE : LANE + WINDOW, :] = low
            wide[op, LANE + WINDOW :, :] = jnp.zeros((LANE - WINDOW, HID), bf16)

    mask_rows(counts, x_ref, xa_ref)
    pre = None
    for op in range(OPS):
        rows = window_rows(xa_ref, op).T
        half = jnp.dot(
            jnp.concatenate([rows, rows], axis=1), wide[op], preferred_element_type=f32
        ).astype(bf16)
        first = jnp.tanh(half) + 1.0
        act = half * first
        half_act = act * 0.5
        second = jnp.tanh(half_act) + 1.0
        joined = half_act * second
        slope = (first * ((half - half_act) + 0.5)) * (second * ((act - joined) + 1.0))
        joined_ref[:, op * HID : (op + 1) * HID] = joined
        slope_ref[:, op * HID : (op + 1) * HID] = slope
        term = jnp.dot(
            joined, wm_ref[op * HID : (op + 1) * HID, :], preferred_element_type=f32
        )
        pre = term if pre is None else pre + term
    pre_ref[...] = pre
    total[0] += fold_rows(pre)
    total[1] += fold_rows(pre * pre)

    @pl.when(step == pl.num_programs(0) - 1)
    def _():
        packed = pack_pair(
            jnp.sum(total[0], axis=0, keepdims=True), jnp.sum(total[1], axis=0, keepdims=True)
        )
        for index in range(out_ref.shape[0]):
            out_ref[index] = packed


def forward_call(all_rows, devices, counts, features, stats, window, pieces, block):
    total = features.shape[1]
    count = len(pieces)
    return pl.pallas_call(
        functools.partial(forward_body, all_rows, count),
        grid_spec=pltpu.PrefetchScalarGridSpec(
            num_scalar_prefetch=1,
            grid=(total // block,),
            in_specs=[
                columns_of(VALID, block),
                fixed(stats.shape),
                fixed((OPS, WINDOW, HID)),
            ]
            + [fixed(piece.shape) for piece in pieces],
            out_specs=[
                rows_of(block, HID),
                rows_of(block, CAT),
                rows_of(block, CAT),
                fixed((CAT, HID)),
                fixed((devices, 8, LANE)),
            ],
            scratch_shapes=[
                pltpu.VMEM((OPS, 2 * LANE, HID), bf16),
                pltpu.VMEM((2, 8, HID), f32),
                pltpu.VMEM((WIDE, block), bf16),
            ],
        ),
        out_shape=[
            shape((total, HID), f32),
            shape((total, CAT), bf16),
            shape((total, CAT), bf16),
            shape((CAT, HID), bf16),
            shape((devices, 8, LANE), f32),
        ],
        compiler_params=params(),
        cost_estimate=cost(44),
        name="forward_layers",
    )(counts, features, stats, window, *pieces)


def head_body(
    all_rows,
    counts,
    pre_ref,
    stats_ref,
    wo_ref,
    labels_ref,
    back_ref,
    logits_ref,
    grad_ref,
    sums_ref,
    wo_low,
    norm,
    total,
):
    step = pl.program_id(0)
    block = pre_ref.shape[0]

    @pl.when(step == 0)
    def _():
        total[...] = jnp.zeros_like(total)
        grad_ref[...] = jnp.zeros_like(grad_ref)
        wo_low[...] = jnp.concatenate(
            [wo_ref[...], jnp.zeros((CPAD - CLS, HID), f32)], axis=0
        ).astype(bf16)
        mean, scale = mid_scale(stats_ref, all_rows)
        norm[0:1, :] = 0.5 * scale
        norm[1:2, :] = -0.5 * scale * mean

    kind = lax.broadcasted_iota(jnp.int32, (CPAD, HEAD), 0)
    for start in range(0, block, HEAD):
        rows = slice(start, start + HEAD)
        half = pre_ref[rows, :] * norm[0:1, :] + norm[1:2, :]
        raised = jnp.tanh(half) + 1.0
        hidden = half * raised
        slope = raised * ((half - 0.5 * hidden) + 0.5)
        hidden = hidden.astype(bf16)
        logits = dot_on(wo_low[...], hidden, 1, 1)
        logits_ref[:, rows] = logits.astype(bf16)
        column = step * block + start + lax.broadcasted_iota(jnp.int32, (CPAD, HEAD), 1)
        real = kind < CLS
        top = jnp.max(jnp.where(real, logits, -jnp.inf), axis=0, keepdims=True)
        powers = jnp.where(real, jnp.exp(logits - top), 0.0)
        probs = powers / jnp.sum(powers, axis=0, keepdims=True)
        score = (probs - jnp.where(kind == labels_ref[:, rows], 1.0, 0.0)) / all_rows
        score = jnp.where(column < own_count(counts), score, 0.0).astype(bf16)
        grad_ref[...] += dot_on(score, hidden, 1, 0)
        back = dot_on(score, wo_low[...], 0, 0) * slope
        total[0] += fold_rows(back)
        total[1] += fold_rows(back * half)
        back_ref[rows, :] = back.astype(bf16)

    @pl.when(step == pl.num_programs(0) - 1)
    def _():
        packed = pack_pair(
            jnp.sum(total[0], axis=0, keepdims=True),
            2.0 * jnp.sum(total[1], axis=0, keepdims=True),
        )
        for index in range(sums_ref.shape[0]):
            sums_ref[index] = packed


def head_call(all_rows, counts, pre, stats, w_out, labels, block):
    total = pre.shape[0]
    return pl.pallas_call(
        functools.partial(head_body, all_rows),
        grid_spec=pltpu.PrefetchScalarGridSpec(
            num_scalar_prefetch=1,
            grid=(total // block,),
            in_specs=[
                rows_of(block, HID),
                fixed(stats.shape),
                fixed((CLS, HID)),
                columns_of(1, block),
            ],
            out_specs=[
                rows_of(block, HID),
                columns_of(CPAD, block),
                fixed((CPAD, HID)),
                fixed(stats.shape),
            ],
            scratch_shapes=[
                pltpu.VMEM((CPAD, HID), bf16),
                pltpu.VMEM((8, HID), f32),
                pltpu.VMEM((2, 8, HID), f32),
            ],
        ),
        out_shape=[
            shape((total, HID), bf16),
            shape((CPAD, total), bf16),
            shape((CPAD, HID), f32),
            shape(stats.shape, f32),
        ],
        compiler_params=params(),
        cost_estimate=cost(18),
        name="head",
    )(counts, pre, stats, w_out, labels)


def add_windows(pieces, write):
    for op, piece in enumerate(pieces):
        start = op * STRIDE
        skip = WINDOW - STRIDE if op else 0
        stop = WINDOW if op == OPS - 1 else STRIDE
        if op:
            write(start, pieces[op - 1][STRIDE:WINDOW, :] + piece[:skip, :])
        write(start + skip, piece[skip:stop, :])


def branch_back_body(
    all_rows,
    counts,
    pre_ref,
    back_ref,
    slope_ref,
    x_ref,
    wm_ref,
    window_ref,
    mid_stats_ref,
    sums_ref,
    stats_ref,
    grad_out_ref,
    gram_ref,
    mid_ref,
    part_ref,
    all_ref,
    norm,
    halved,
    grad,
    xa_ref,
):
    step = pl.program_id(0)

    @pl.when(step == 0)
    def _():
        grad[...] = jnp.zeros_like(grad)
        stats = add_up(stats_ref)
        for op in range(OPS):
            halved[op : op + 1, :] = 0.5 * branch_scale(stats, op, all_rows)[1]
        mean, scale = mid_scale(mid_stats_ref, all_rows)
        level, slant = unpack_pair(add_up(sums_ref))
        slant = scale * scale * (slant / all_rows)
        norm[0:1, :] = scale
        norm[1:2, :] = slant
        norm[2:3, :] = mean * slant - scale * (level / all_rows)

    mask_rows(counts, x_ref, xa_ref)
    mid = (
        back_ref[...].astype(f32) * norm[0:1, :]
        - pre_ref[...] * norm[1:2, :]
        + norm[2:3, :]
    ).astype(bf16)
    mid_ref[...] = mid
    pieces = []
    for op in range(OPS):
        span = slice(op * HID, (op + 1) * HID)
        joined_back = dot_on(mid, wm_ref[span, :], 1, 1)
        back = (
            (joined_back * halved[op : op + 1, :]) * slope_ref[:, span].astype(f32)
        ).astype(bf16)
        line = slice(op * LANE, (op + 1) * LANE)
        grad[line, :HID] += dot_on(window_rows(xa_ref, op), back, 1, 0)
        pieces.append(dot_on(window_ref[op], back, 1, 1))

    def write(at, value):
        part_ref[at : at + value.shape[0], :] = value.astype(bf16)

    add_windows(pieces, write)

    @pl.when(step == pl.num_programs(0) - 1)
    def _():
        means = add_up(stats_ref)[:, HID:] / all_rows
        means = jnp.where(
            lax.broadcasted_iota(jnp.int32, means.shape, 1) < WINDOW, means, 0.0
        )
        turned = means.T
        for op in range(OPS):
            start = op * LANE
            gram = gram_ref[op]
            mean, column = means[op : op + 1, :], turned[:, op : op + 1]
            sums, count = gram[WINDOW : WINDOW + 1, :], gram[WINDOW:WINDOW + 1, WINDOW : WINDOW + 1]
            gram = gram - column * (sums - count * mean) - gram[:, WINDOW : WINDOW + 1] * mean
            grad[start : start + LANE, HID:] = gram
            level = grad[start + WINDOW : start + WINDOW + 1, :HID]
            grad[start : start + LANE, :HID] = jnp.concatenate(
                [
                    grad[start : start + WINDOW, :HID] - column[:WINDOW] * level,
                    level,
                    grad_out_ref[op * SHARE : (op + 1) * SHARE, :],
                    jnp.zeros((LANE - WINDOW - 1 - SHARE, HID), f32),
                ],
                axis=0,
            )
        size = all_ref.shape[1]
        for index, block_index in enumerate(owned_order(all_ref.shape[0])):
            at = block_index * size
            all_ref[index] = grad[at : at + size, :].astype(bf16)


def branch_back_call(
    all_rows,
    devices,
    counts,
    pre,
    back,
    slope,
    features,
    mid_low,
    window,
    mid_stats,
    sums,
    stats,
    grad_out,
    gram,
    block,
):
    total = pre.shape[0]
    wide = HID + LANE
    parts = (devices, OPS * LANE // devices, wide)
    return pl.pallas_call(
        functools.partial(branch_back_body, all_rows),
        grid_spec=pltpu.PrefetchScalarGridSpec(
            num_scalar_prefetch=1,
            grid=(total // block,),
            in_specs=[
                rows_of(block, HID),
                rows_of(block, HID),
                rows_of(block, CAT),
                columns_of(VALID, block),
                fixed((CAT, HID)),
                fixed((OPS, WINDOW, HID)),
                fixed(mid_stats.shape),
                fixed(sums.shape),
                fixed(stats.shape),
                fixed((CPAD, HID)),
                fixed((OPS, LANE, LANE)),
            ],
            out_specs=[rows_of(block, HID), columns_of(VALID, block), fixed(parts)],
            scratch_shapes=[
                pltpu.VMEM((8, HID), f32),
                pltpu.VMEM((8, HID), f32),
                pltpu.VMEM((OPS * LANE, wide), f32),
                pltpu.VMEM((WIDE, block), bf16),
            ],
        ),
        out_shape=[shape((total, HID), bf16), shape((VALID, total), bf16), shape(parts, bf16)],
        compiler_params=params(),
        cost_estimate=cost(48),
        name="branch_back",
    )(counts, pre, back, slope, features, mid_low, window, mid_stats, sums, stats, grad_out, gram)


def mid_grad_body(mid_ref, joined_ref, *refs):
    step = pl.program_id(0)
    parts, grad = refs[:-1], refs[-1]

    @pl.when(step == 0)
    def _():
        grad[...] = jnp.zeros_like(grad)

    for op in range(OPS):
        span = slice(op * HID, (op + 1) * HID)
        grad[span, :] += dot_on(joined_ref[:, span], mid_ref[...], 0, 0)

    @pl.when(step == pl.num_programs(0) - 1)
    def _():
        groups = lax.axis_size("row")
        row = lax.axis_index("row")
        core, far = lax.rem(row, 2), row // (groups // 2)
        pairs, size = parts[0].shape[0], parts[0].shape[1]
        for index, part in enumerate(parts):
            which = core if index < 2 else 1 - core
            half = far if index % 2 == 0 else 1 - far
            for pair in range(pairs):
                chunk = 2 * (half * pairs + pair) + which
                part[pair] = grad[pl.ds(pl.multiple_of(chunk * size, size), size), :]


def mid_grad_call(groups, mid, joined, block):
    total = mid.shape[0]
    parted = (groups // 4, CAT // groups, HID)
    return pl.pallas_call(
        mid_grad_body,
        grid=(total // block,),
        in_specs=[rows_of(block, HID), rows_of(block, CAT)],
        out_specs=[fixed(parted)] * 4,
        out_shape=[shape(parted, f32)] * 4,
        scratch_shapes=[pltpu.VMEM((CAT, HID), f32)],
        compiler_params=params(),
        cost_estimate=cost(25),
        name="mid_grad",
    )(mid, joined)


def branch_terms(all_rows, scale, window, raw):
    level = raw[WINDOW : WINDOW + 1, :]
    inner = scale * jnp.sum(window.astype(f32) * raw[:WINDOW, :], axis=0, keepdims=True)
    return level / all_rows, scale * (inner / all_rows)


def rows_back_body(
    all_rows,
    counts,
    x_ref,
    part_ref,
    stats_ref,
    window_ref,
    own_ref,
    near_ref,
    out_ref,
    inner,
    base,
    grads,
):
    step = pl.program_id(0)
    block = x_ref.shape[1]

    @pl.when(step == 0)
    def _():
        gather_halves(own_ref, near_ref, grads)
        stats = add_up(stats_ref)
        for op in range(OPS):
            mean, scale = branch_scale(stats, op, all_rows)
            window = window_ref[op]
            level, slant = branch_terms(
                all_rows, scale, window, grads[op * LANE : (op + 1) * LANE, :HID].astype(f32)
            )
            inner[op] = dot_on((window.astype(f32) * -slant).astype(bf16), window, 1, 1).astype(bf16)
            base[op] = jnp.sum(
                window.astype(f32) * (mean * slant - level), axis=1, keepdims=True
            )

    moved = []
    for op in range(OPS):
        rows = x_ref[op * STRIDE : op * STRIDE + WINDOW, :]
        moved.append(jnp.dot(inner[op], rows, preferred_element_type=f32) + base[op])
    column = step * block + lax.broadcasted_iota(jnp.int32, (1, block), 1)
    valid = column < own_count(counts)

    def write(at, value):
        span = slice(at, at + value.shape[0])
        value = jnp.where(valid, value + part_ref[span, :].astype(f32), 0.0)
        out_ref[span, :] = value.astype(bf16)

    add_windows(moved, write)


def rows_back_call(all_rows, counts, features, part, stats, window, halves, block):
    total = features.shape[1]
    return pl.pallas_call(
        functools.partial(rows_back_body, all_rows),
        grid_spec=pltpu.PrefetchScalarGridSpec(
            num_scalar_prefetch=1,
            grid=(total // block,),
            in_specs=[
                columns_of(VALID, block),
                columns_of(VALID, block),
                fixed(stats.shape),
                fixed((OPS, WINDOW, HID)),
            ]
            + [fixed(half.shape) for half in halves],
            out_specs=columns_of(VALID, block),
            scratch_shapes=[
                pltpu.VMEM((OPS, WINDOW, WINDOW), bf16),
                pltpu.VMEM((OPS, WINDOW, 1), f32),
                pltpu.VMEM((OPS * LANE, HID + LANE), bf16),
            ],
        ),
        out_shape=shape((VALID, total), bf16),
        compiler_params=params(),
        cost_estimate=cost(8),
        name="rows_back",
    )(counts, features, part, stats, window, *halves)


def slots_of(rows, peers):
    return -(-(rows // LANE + 1) // peers)


def first_row(counts, source):
    row = lax.axis_index("row")
    begin = jnp.int32(0)
    for peer in range(counts.shape[1]):
        begin += jnp.where(peer < source, counts[row, peer], 0)
    return begin


def deal_body(counts, logits_ref, out_ref):
    peers = out_ref.shape[0]
    tiles = logits_ref.shape[1] // LANE
    begin = first_row(counts, lax.axis_index("col"))
    count = own_count(counts)
    shift = lax.rem(begin, LANE)
    chunk = begin // LANE
    lane = lax.broadcasted_iota(jnp.int32, (CPAD, LANE), 1)
    empty = jnp.zeros((CPAD, LANE), f32)
    left = empty
    for tile in range(peers * (out_ref.shape[2] // LANE)):
        right = empty
        if tile < tiles:
            piece = logits_ref[:, tile * LANE : (tile + 1) * LANE].astype(f32)
            piece = jnp.where(tile * LANE + lane < count, piece, 0.0)
            right = pltpu.roll(piece, shift, 1)
        slot = tile // peers * LANE
        peer = lax.rem(chunk + tile, peers)
        out_ref[peer, :, slot : slot + LANE] = jnp.where(lane < shift, left, right).astype(bf16)
        left = right


def deal_call(counts, logits, peers):
    total = logits.shape[1]
    dealt = (peers, CPAD, slots_of(total, peers) * LANE)
    return pl.pallas_call(
        deal_body,
        grid_spec=pltpu.PrefetchScalarGridSpec(
            num_scalar_prefetch=1,
            grid=(1,),
            in_specs=[fixed((CPAD, total))],
            out_specs=fixed(dealt),
        ),
        out_shape=shape(dealt, bf16),
        compiler_params=params(),
        cost_estimate=cost(3),
        name="deal_logits",
    )(counts, logits)


def collect_body(counts, dealt_ref, out_ref, held):
    peers, _, width = dealt_ref.shape
    member = lax.axis_index("col")
    held[...] = jnp.zeros_like(held)
    for source in range(peers):
        chunk = first_row(counts, source) // LANE
        ahead = lax.rem(member + peers - lax.rem(chunk, peers), peers)
        at = pl.ds(pl.multiple_of((chunk + ahead) // peers * LANE, LANE), width)
        held[:, at] += dealt_ref[source].astype(f32)
    share = out_ref.shape[2]
    for peer in range(peers):
        out_ref[peer] = held[:, peer * share : (peer + 1) * share].astype(bf16)


def collect_call(counts, dealt):
    peers, height, width = dealt.shape
    collected = (peers, height, AVG // peers)
    return pl.pallas_call(
        collect_body,
        grid_spec=pltpu.PrefetchScalarGridSpec(
            num_scalar_prefetch=1,
            grid=(1,),
            in_specs=[fixed(dealt.shape)],
            out_specs=fixed(collected),
            scratch_shapes=[pltpu.VMEM((height, AVG + LANE + width), f32)],
        ),
        out_shape=shape(collected, bf16),
        compiler_params=params(),
        cost_estimate=cost(3),
        name="collect_logits",
    )(counts, dealt)


def join_body(pieces_ref, out_ref):
    peers, _, share = pieces_ref.shape
    for peer in range(peers):
        for index in range(share // LANE):
            at = (index * peers + peer) * LANE
            piece = pieces_ref[peer, :, index * LANE : (index + 1) * LANE].astype(f32)
            out_ref[:, at : at + LANE] = piece[:CLS, :]


def join_call(pieces):
    return pl.pallas_call(
        join_body,
        out_shape=shape((CLS, AVG), f32),
        compiler_params=params(),
        cost_estimate=cost(2),
        name="join_logits",
    )(pieces)


def moments(turned, first, second):
    new_first = beta_first * first + (1.0 - beta_first) * turned
    new_second = beta_second * second + (1.0 - beta_second) * turned * turned
    direction = (
        new_first
        / (1.0 - beta_first**STEP)
        / (jnp.sqrt(new_second / (1.0 - beta_second**STEP)) + adam_eps)
    )
    return new_first, new_second, direction


def dot_parts(first_arg, second_arg, first_dim, second_dim):
    first_high, first_low = split_low(first_arg)
    second_high, second_low = split_low(second_arg)
    return dot_on(first_high, second_high, first_dim, second_dim) + (
        dot_on(first_high, second_low, first_dim, second_dim)
        + dot_on(first_low, second_high, first_dim, second_dim)
    )


def factor(old, grad, dim):
    low = grad.astype(bf16)
    return beta_factor * old + (1.0 - beta_factor) * dot_on(low, low, dim, dim)


def branch_update_body(
    all_rows,
    stats_ref,
    window_ref,
    own_ref,
    near_ref,
    w_ref,
    left_ref,
    right_ref,
    basis_left_ref,
    basis_right_ref,
    first_ref,
    second_ref,
    new_left_ref,
    new_right_ref,
    new_first_ref,
    new_second_ref,
    new_w_ref,
    low_w_ref,
    grad_out_ref,
    grads,
):
    step = pl.program_id(0)

    @pl.when(step == 0)
    def _():
        gather_halves(own_ref, near_ref, grads)
        for op in range(OPS):
            at = op * LANE + WINDOW + 1
            grad_out_ref[op * SHARE : (op + 1) * SHARE, :] = grads[at : at + SHARE, :HID].astype(f32)

    for op in range(OPS):

        @pl.when(step == op)
        def _(op=op):
            mean, scale = branch_scale(add_up(stats_ref), op, all_rows)
            window = window_ref[op]
            raw = grads[op * LANE : (op + 1) * LANE, :HID].astype(f32)
            gram = grads[op * LANE : (op + 1) * LANE, HID:]
            level, slant = branch_terms(all_rows, scale, window, raw)
            normed = jnp.dot(gram, padded(window), preferred_element_type=f32)
            grad = raw[:WINDOW, :] - normed[:WINDOW, :] * slant
            shift = op * (DIN - STRIDE)
            grad = grad[shift : shift + DIN, :]
            new_left_ref[:, op, :] = factor(left_ref[:, op, :], grad, 1)
            new_right_ref[0] = factor(right_ref[0], grad, 0)
            basis_left, basis_right = basis_left_ref[:, op, :], basis_right_ref[0]
            turned = dot_parts(basis_left, grad, 0, 0)
            turned = dot_parts(turned, basis_right, 1, 0)
            new_first, new_second, direction = moments(
                turned, first_ref[:, op, :], second_ref[:, op, :]
            )
            new_first_ref[:, op, :] = new_first
            new_second_ref[:, op, :] = new_second
            back = dot_parts(basis_left, direction, 1, 0)
            back = dot_parts(back, basis_right, 1, 1)
            new_w = w_ref[:, op, :] - rate_branch * back
            new_w_ref[:, op, :] = new_w
            low_w_ref[:, op, :] = new_w.astype(bf16)


def branch_update_call(
    all_rows, stats, window, halves, w, left, right, basis_left, basis_right, first, second
):
    small, wide = fixed((DIN, OPS, DIN)), fixed((DIN, OPS, HID))
    square = pl.BlockSpec((1, HID, HID), lambda k: (k, 0, 0))
    return pl.pallas_call(
        functools.partial(branch_update_body, all_rows),
        grid=(OPS,),
        in_specs=[fixed(stats.shape), fixed((OPS, WINDOW, HID))]
        + [fixed(half.shape) for half in halves]
        + [wide, small, square, small, square, wide, wide],
        out_specs=[small, square, wide, wide, wide, wide, fixed((CPAD, HID))],
        out_shape=[
            shape((DIN, OPS, DIN), f32),
            shape((OPS, HID, HID), f32),
            shape((DIN, OPS, HID), f32),
            shape((DIN, OPS, HID), f32),
            shape((DIN, OPS, HID), f32),
            shape((DIN, OPS, HID), bf16),
            shape((CPAD, HID), f32),
        ],
        scratch_shapes=[pltpu.VMEM((OPS * LANE, HID + LANE), bf16)],
        compiler_params=params(),
        cost_estimate=cost(12),
        name="branch_update",
    )(stats, window, *halves, w, left, right, basis_left, basis_right, first, second)


def out_update_body(
    grad_ref,
    w_ref,
    left_ref,
    right_ref,
    basis_left_ref,
    basis_right_ref,
    first_ref,
    second_ref,
    new_left_ref,
    new_right_ref,
    new_first_ref,
    new_second_ref,
    new_w_ref,
    low_w_ref,
):
    grad = grad_ref[:CLS, :]
    new_left_ref[...] = factor(left_ref[...], grad, 0)
    new_right_ref[...] = factor(right_ref[...], grad, 1)
    turned = dot_parts(grad, basis_left_ref[...], 1, 0)
    turned = dot_parts(basis_right_ref[...], turned, 0, 0)
    new_first, new_second, direction = moments(turned, first_ref[...], second_ref[...])
    new_first_ref[...] = new_first
    new_second_ref[...] = new_second
    back = dot_parts(direction, basis_left_ref[...], 1, 1)
    back = dot_parts(basis_right_ref[...], back, 1, 0)
    new_w = w_ref[...] - rate_out * back
    new_w_ref[...] = new_w
    low_w_ref[...] = new_w.astype(bf16)


def out_update_call(grad, w, left, right, basis_left, basis_right, first, second):
    return pl.pallas_call(
        out_update_body,
        out_shape=[
            shape((HID, HID), f32),
            shape((CLS, CLS), f32),
            shape((CLS, HID), f32),
            shape((CLS, HID), f32),
            shape((CLS, HID), f32),
            shape((CLS, HID), bf16),
        ],
        compiler_params=params(),
        cost_estimate=cost(4),
        name="out_update",
    )(grad, w, left, right, basis_left, basis_right, first, second)


def mid_update_body(
    grad_ref, w_ref, basis_ref, first_ref, second_ref, new_first_ref, new_second_ref, new_w_ref, low_w_ref
):
    turned = dot_parts(grad_ref[...], basis_ref[...], 1, 0)
    new_first, new_second, direction = moments(turned, first_ref[...], second_ref[...])
    new_first_ref[...] = new_first
    new_second_ref[...] = new_second
    new_w = w_ref[...] - rate_mid * dot_parts(direction, basis_ref[...], 1, 1)
    new_w_ref[...] = new_w
    low_w_ref[...] = new_w.astype(bf16)


def mid_update_call(grad, w, basis, first, second):
    rows = grad.shape[0]
    return pl.pallas_call(
        mid_update_body,
        out_shape=[shape((rows, HID), f32)] * 3 + [shape((rows, HID), bf16)],
        compiler_params=params(),
        cost_estimate=cost(3),
        name="mid_update",
    )(grad, w, basis, first, second)


def half_blocks():
    parts = HID // LANE
    return [(i, j) for i in range(parts) for j in range(i, parts)]


def mid_gram_body(rows_ref, out_ref):
    rows = rows_ref[...]
    gram = dot_on(rows, rows, 0, 0)
    for index, (i, j) in enumerate(half_blocks()):
        out_ref[index] = gram[i * LANE : (i + 1) * LANE, j * LANE : (j + 1) * LANE].astype(bf16)


def mid_gram_call(rows):
    return pl.pallas_call(
        mid_gram_body,
        out_shape=shape((len(half_blocks()), LANE, LANE), bf16),
        compiler_params=params(),
        cost_estimate=cost(2),
        name="mid_gram",
    )(rows)


def mid_factor_body(right_ref, own_ref, near_ref, out_ref):
    for index, (i, j) in enumerate(half_blocks()):
        block = (1.0 - beta_factor) * (own_ref[index] + near_ref[index])
        rows, columns = slice(i * LANE, (i + 1) * LANE), slice(j * LANE, (j + 1) * LANE)
        out_ref[rows, columns] = beta_factor * right_ref[rows, columns] + block
        if i != j:
            out_ref[columns, rows] = beta_factor * right_ref[columns, rows] + block.T


def mid_factor_call(right, own, near):
    return pl.pallas_call(
        mid_factor_body,
        out_shape=shape((HID, HID), f32),
        compiler_params=params(),
        cost_estimate=cost(2),
        name="mid_factor",
    )(right, own, near)


def after(values, *others):
    return lax.optimization_barrier((values,) + others)[0]


def swap(values, axis, distance):
    peers = lax.axis_size(axis)
    return lax.ppermute(values, axis, [(peer, peer ^ distance) for peer in range(peers)])


def gather_by_doubling(values):
    steps = doubling_steps()
    for axis, distance in steps[:-1]:
        other = swap(values, axis, distance)
        bit = lax.rem(lax.axis_index(axis) // distance, 2) > 0
        values = jnp.where(
            bit,
            jnp.concatenate([other, values], axis=0),
            jnp.concatenate([values, other], axis=0),
        )
    return values, swap(values, *steps[-1])


def add_all(values):
    while len(values) > 1:
        values = [values[i] + values[i + 1] for i in range(0, len(values), 2)]
    return values[0]


def exchange(values):
    return lax.all_to_all(values, "col", 0, 0, tiled=True)


def spread_out(values, dtype=f32):
    copies = jnp.broadcast_to(values[None], (lax.axis_size("col"),) + values.shape)
    return exchange(copies.astype(dtype))


def far_copies(values):
    pieces = {0: values}
    distance = lax.axis_size("row") // 2
    while distance > 1:
        pieces.update({d ^ distance: swap(v, "row", distance) for d, v in list(pieces.items())})
        distance //= 2
    return pieces


def near_copies(pieces, *others):
    held = lax.optimization_barrier((*[pieces[d] for d in sorted(pieces)], *others))
    pieces = dict(zip(sorted(pieces), held))
    pieces.update({d ^ 1: swap(v, "row", 1) for d, v in list(pieces.items())})
    return [pieces[d] for d in sorted(pieces)], held[len(held) - len(others) :]


def sum_in_row(values):
    return add_all([values] + [swap(values, "row", d) for d in range(1, lax.axis_size("row"))])


def keep_bit(values, distance):
    bit = lax.rem(lax.axis_index("row") // distance, 2)
    pairs = values.reshape((-1, 2) + values.shape[1:])
    kept = lax.dynamic_index_in_dim(pairs, bit, 1, keepdims=False)
    sent = lax.dynamic_index_in_dim(pairs, 1 - bit, 1, keepdims=False)
    return kept, sent


def finish_scatter(values, distance):
    while distance < lax.axis_size("row") // 2:
        kept, sent = keep_bit(values, distance)
        values = kept + swap(sent.astype(bf16), "row", distance).astype(f32)
        distance *= 2
    values = values.reshape((lax.axis_size("col"), -1) + values.shape[2:]).astype(bf16)
    return jnp.sum(exchange(values).astype(f32), axis=0)


def local(
    features,
    labels,
    counts,
    w_branch,
    w_mid,
    w_out,
    left_branch,
    right_branch,
    basis_left_branch,
    basis_right_branch,
    first_branch,
    second_branch,
    right_mid,
    basis_right_mid,
    first_mid,
    second_mid,
    left_out,
    right_out,
    basis_left_out,
    basis_right_out,
    first_out,
    second_out,
):
    groups, peers = lax.axis_size("row"), lax.axis_size("col")
    devices = groups * peers
    all_rows = float(AVG * devices)

    def by_input(values):
        return values.transpose(1, 0, 2)

    turned = features.T
    own_mid = spread_out(w_mid, bf16).reshape(-1, HID)
    window, gram, branch_sums = gram_call(counts, turned, by_input(w_branch), 4096)
    branch_sums = sum_in_row(branch_sums)
    own_mid = after(own_mid, branch_sums)
    pieces = far_copies(own_mid)
    branch_stats = spread_out(branch_sums)
    pieces, (branch_stats,) = near_copies(pieces, branch_stats)
    pre, joined, slope, mid_low, mid_sums = forward_call(
        all_rows, devices, counts, turned, branch_stats, window, pieces, 512
    )
    mid_stats = lax.all_to_all(mid_sums, BOTH, 0, 0, tiled=True)
    back, logits, grad_out, back_sums = head_call(
        all_rows, counts, pre, mid_stats, w_out.T, labels.reshape(1, -1), 2048
    )
    back_stats = lax.all_to_all(back_sums, BOTH, 0, 0, tiled=True)

    dealt = deal_call(counts, logits, peers)
    back_stats, dealt = lax.optimization_barrier((back_stats, dealt))
    dealt = exchange(dealt)
    mid, part, grad_branch = branch_back_call(
        all_rows,
        devices,
        counts,
        pre,
        back,
        slope,
        turned,
        mid_low,
        window,
        mid_stats,
        back_stats,
        branch_stats,
        grad_out,
        gram,
        1024,
    )
    grad_branch, dealt = lax.optimization_barrier((grad_branch, dealt))
    grad_branch = lax.all_to_all(grad_branch, BOTH, 0, 0, tiled=True)
    parts = mid_grad_call(groups, mid, joined, 1024)
    grad_branch, *parts = lax.optimization_barrier((grad_branch, *parts))
    kept, sent = parts[:2], parts[2:]
    grad_branch = jnp.sum(grad_branch.astype(f32), axis=0).astype(bf16)
    near = [swap(part, "row", 1) for part in sent]
    halves = [half.reshape(-1, HID + LANE) for half in gather_by_doubling(grad_branch)]
    away = (kept[1] + near[1]).astype(bf16)
    far = swap(away, "row", groups // 2)
    grad_mid = finish_scatter(kept[0] + near[0] + far.astype(f32), 2)
    grad_features = rows_back_call(
        all_rows, counts, turned, part, branch_stats, window, halves, 4096
    )
    collected = collect_call(counts, after(dealt, grad_features))
    grad_mid, grad_features, collected = lax.optimization_barrier(
        (grad_mid, grad_features, collected)
    )
    all_mid = spread_out(grad_mid, bf16).reshape(-1, HID)
    *branch_parts, grad_out = branch_update_call(
        all_rows,
        branch_stats,
        window,
        halves,
        by_input(w_branch),
        by_input(left_branch),
        right_branch,
        by_input(basis_left_branch),
        basis_right_branch,
        by_input(first_branch),
        by_input(second_branch),
    )
    held = lax.optimization_barrier((all_mid, *branch_parts))
    all_mid, branch_parts = held[0], held[1:]
    collected = exchange(after(collected, all_mid))
    mid_gram = mid_gram_call(all_mid)
    distance = groups // 2
    others = swap(mid_gram, "row", distance)
    mid_parts = mid_update_call(
        after(grad_mid, mid_gram), w_mid, basis_right_mid, first_mid, second_mid
    )
    out_parts = out_update_call(
        after(grad_out, mid_gram),
        w_out.T,
        left_out,
        right_out,
        basis_left_out,
        basis_right_out,
        first_out.T,
        second_out.T,
    )
    mid_gram, others, *held = lax.optimization_barrier(
        (mid_gram, others, *mid_parts, *out_parts)
    )
    mid_parts, out_parts = held[:4], held[4:]
    mid_gram = mid_gram.astype(f32) + others.astype(f32)
    while distance > 2:
        distance //= 2
        mid_gram = mid_gram + swap(mid_gram, "row", distance)
    others = swap(mid_gram, "row", 1)
    new_logits = join_call(after(collected, mid_gram))
    others, new_logits = lax.optimization_barrier((others, new_logits))
    new_right_mid = mid_factor_call(right_mid, mid_gram, others)
    branch_parts = [
        part if index == 1 else by_input(part) for index, part in enumerate(branch_parts)
    ]
    out_parts = list(out_parts[:2]) + [part.T for part in out_parts[2:]]
    return (new_logits.T, grad_features.T, *branch_parts, new_right_mid, *mid_parts, *out_parts)


def solution(mesh):
    split, rows, whole = P(BOTH, None), P(BOTH), P()
    in_specs = (split, rows, whole, whole, split) + (whole,) * 9 + (split, split) + (whole,) * 6
    out_specs = (split, split) + (whole,) * 7 + (split,) * 4 + (whole,) * 6
    return jax.shard_map(local, mesh=mesh, in_specs=in_specs, out_specs=out_specs, check_vma=False)
```

```python
import functools

import jax
import jax.numpy as jnp
from jax import lax
from jax.experimental import pallas as pl
from jax.experimental.pallas import tpu as pltpu
from jax.sharding import PartitionSpec as P

OPS = 4
DIN = 100
HID = 512
CLS = 47
AVG = 4096
STEP = 5
CAT = 2048
LANE = 128
CPAD = 48
STRIDE = 96
WINDOW = 112
VALID = 400
HEAD = 2048
PART = 256
WIDE = 416
SHARE = 12
BOTH = ("row", "col")

beta_first = 0.5
beta_second = 0.9
beta_factor = 0.95
adam_eps = 1e-08
norm_eps = 1e-05
rate_branch = 0.1
rate_mid = 0.02
rate_out = 0.04
f32 = jnp.float32
bf16 = jnp.bfloat16
VMEM_LIMIT = 60 * 2**20


def dot_on(first_arg, second_arg, first_dim, second_dim, precision=None):
    return lax.dot_general(
        first_arg,
        second_arg,
        (((first_dim,), (second_dim,)), ((), ())),
        precision=precision,
        preferred_element_type=f32,
    )


def params():
    return pltpu.CompilerParams(vmem_limit_bytes=VMEM_LIMIT)


def cost(microseconds):
    return pl.CostEstimate(
        flops=int(microseconds * 1e9), bytes_accessed=1, transcendentals=0
    )


def shape(dims, dtype):
    return jax.ShapeDtypeStruct(dims, dtype)


def fixed(dims):
    return pl.BlockSpec(dims, lambda *_: (0,) * len(dims))


def rows_of(block, width):
    return pl.BlockSpec((block, width), lambda i, *_: (i, 0))


def columns_of(height, block):
    return pl.BlockSpec((height, block), lambda i, *_: (0, i))


def low_f32(values):
    return values.astype(bf16).astype(f32)


def split_low(values):
    high = values.astype(bf16)
    return high, (values - high.astype(f32)).astype(bf16)


def fold_rows(values):
    return jnp.sum(values.reshape(values.shape[0] // 8, 8, values.shape[1]), axis=0)


def add_up(ref):
    value = ref[0]
    for index in range(1, ref.shape[0]):
        value = value + ref[index]
    return value


def own_count(counts):
    return counts[lax.axis_index("row"), lax.axis_index("col")]


def branch_scale(stats, op, all_rows):
    mean = stats[op : op + 1, :HID] / all_rows
    square = stats[OPS + op : OPS + op + 1, :HID] / all_rows
    return mean, lax.rsqrt(square - mean * mean + norm_eps)


def unpack_pair(packed):
    parts = HID // LANE
    return [
        jnp.concatenate(
            [packed[index * parts + part : index * parts + part + 1, :] for part in range(parts)],
            axis=1,
        )
        for index in range(2)
    ]


def pack_pair(first, second):
    parts = HID // LANE
    return jnp.concatenate(
        [
            value[:, part * LANE : (part + 1) * LANE]
            for value in (first, second)
            for part in range(parts)
        ],
        axis=0,
    )


def mid_scale(stats_ref, all_rows):
    total, square = unpack_pair(add_up(stats_ref))
    mean = total / all_rows
    return mean, lax.rsqrt(square / all_rows - mean * mean + norm_eps)


def window_rows(x_ref, op):
    return jnp.concatenate(
        [x_ref[op * STRIDE : op * STRIDE + WINDOW, :], x_ref[VALID:WIDE, :]], axis=0
    )


def padded(window):
    return jnp.concatenate([window, jnp.zeros((LANE - WINDOW, HID), bf16)], axis=0)


def gram_product(gram, window):
    weight = padded(window)
    product = None
    for _ in range(3):
        part = gram.astype(bf16)
        gram = gram - part.astype(f32)
        term = jnp.dot(part, weight, preferred_element_type=f32)
        product = term if product is None else product + term
    return product


def mask_rows(counts, x_ref, held):
    block = x_ref.shape[1]
    column = pl.program_id(0) * block + lax.broadcasted_iota(jnp.int32, (16, block), 1)
    valid = jnp.where(column < own_count(counts), 1.0, 0.0)
    line = lax.broadcasted_iota(jnp.int32, (16, block), 0)
    held[:VALID, :] = x_ref[...] * valid[0:1, :].astype(bf16)
    held[VALID:, :] = jnp.where(line < 2, valid, 0.0).astype(bf16)


def doubling_steps():
    steps = []
    distance = lax.axis_size("row") // 2
    while distance > 1:
        steps.append(("row", distance))
        distance //= 2
    distance = lax.axis_size("col") // 2
    while distance:
        steps.append(("col", distance))
        distance //= 2
    return steps + [("row", 1)]


def owned_order(devices):
    peers = lax.axis_size("col")
    order = []
    for device in range(devices):
        place = {"row": device // peers, "col": device % peers}
        bits = [place[axis] // distance % 2 for axis, distance in doubling_steps()]
        order.append(sum(bit << index for index, bit in enumerate(bits)))
    return order


def gather_halves(own_ref, near_ref, held):
    core = lax.rem(lax.axis_index("row"), 2)
    size = own_ref.shape[0]
    held[pl.ds(pl.multiple_of(core * size, size), size), :] = own_ref[...]
    held[pl.ds(pl.multiple_of((1 - core) * size, size), size), :] = near_ref[...]


def gather_pieces(refs, held):
    row = lax.axis_index("row")
    size = held.shape[0] // len(refs)
    for index, ref in enumerate(refs):
        at = pl.multiple_of((row ^ index) * size, size)
        held[pl.ds(at, size), :] = ref[...].reshape(size, held.shape[1]).astype(held.dtype)


def gram_body(counts, x_ref, w_ref, window_ref, gram_ref, stats_ref, xa_ref):
    step = pl.program_id(0)

    @pl.when(step == 0)
    def _():
        gram_ref[...] = jnp.zeros_like(gram_ref)
        for op in range(OPS):
            shift = op * (DIN - STRIDE)
            parts = [low_f32(w_ref[:, op, :])]
            if shift:
                parts.insert(0, jnp.zeros((shift, HID), f32))
            if WINDOW - DIN - shift:
                parts.append(jnp.zeros((WINDOW - DIN - shift, HID), f32))
            window_ref[op] = jnp.concatenate(parts, axis=0).astype(bf16)

    mask_rows(counts, x_ref, xa_ref)
    for op in range(0, OPS, 2):
        rows = jnp.concatenate([window_rows(xa_ref, op), window_rows(xa_ref, op + 1)], axis=0)
        both = dot_on(rows, rows, 1, 1)
        gram_ref[op] += both[:LANE, :LANE]
        gram_ref[op + 1] += both[LANE:, LANE:]

    @pl.when(step == pl.num_programs(0) - 1)
    def _():
        for op in range(OPS):
            turned = gram_product(gram_ref[op], window_ref[op])
            stats_ref[op : op + 1, :HID] = turned[WINDOW : WINDOW + 1, :]
            stats_ref[OPS + op : OPS + op + 1, :HID] = jnp.sum(
                window_ref[op].astype(f32) * turned[:WINDOW, :], axis=0, keepdims=True
            )
            stats_ref[op : op + 1, HID:] = gram_ref[op, WINDOW : WINDOW + 1, :]
            stats_ref[OPS + op : OPS + op + 1, HID:] = jnp.zeros((1, LANE), f32)


def gram_call(counts, features, w_branch, block):
    total = features.shape[1]
    return pl.pallas_call(
        gram_body,
        grid_spec=pltpu.PrefetchScalarGridSpec(
            num_scalar_prefetch=1,
            grid=(total // block,),
            in_specs=[columns_of(VALID, block), fixed((DIN, OPS, HID))],
            out_specs=[
                fixed((OPS, WINDOW, HID)),
                fixed((OPS, LANE, LANE)),
                fixed((2 * OPS, HID + LANE)),
            ],
            scratch_shapes=[pltpu.VMEM((WIDE, block), bf16)],
        ),
        out_shape=[
            shape((OPS, WINDOW, HID), bf16),
            shape((OPS, LANE, LANE), f32),
            shape((2 * OPS, HID + LANE), f32),
        ],
        compiler_params=params(),
        cost_estimate=cost(6),
        name="row_moments",
    )(counts, features, w_branch)


def forward_body(all_rows, count, counts, *refs):
    x_ref, stats_ref, window_ref = refs[:3]
    pieces = refs[3 : 3 + count]
    pre_ref, joined_ref, slope_ref, wm_ref, out_ref, wide, total, xa_ref = refs[3 + count :]
    step = pl.program_id(0)

    @pl.when(step == 0)
    def _():
        total[...] = jnp.zeros_like(total)
        gather_pieces(pieces, wm_ref)
        stats = add_up(stats_ref)
        line = lax.broadcasted_iota(jnp.int32, (LANE - WINDOW, HID), 0)
        for op in range(OPS):
            mean, scale = branch_scale(stats, op, all_rows)
            half = 0.5 * scale
            high, low = split_low(window_ref[op].astype(f32) * half)
            base = -mean * half
            base_high = low_f32(base)
            wide[op, :WINDOW, :] = high
            wide[op, WINDOW:LANE, :] = jnp.where(
                line == 0, base_high, jnp.where(line == 1, base - base_high, 0.0)
            ).astype(bf16)
            wide[op, LANE : LANE + WINDOW, :] = low
            wide[op, LANE + WINDOW :, :] = jnp.zeros((LANE - WINDOW, HID), bf16)

    mask_rows(counts, x_ref, xa_ref)
    pre = None
    for op in range(OPS):
        rows = window_rows(xa_ref, op).T
        rows = jnp.concatenate([rows, rows], axis=1)
        for start in range(0, HID, PART):
            half = jnp.dot(
                rows, wide[op, :, start : start + PART], preferred_element_type=f32
            ).astype(bf16)
            first = jnp.tanh(half) + 1.0
            act = half * first
            half_act = act * 0.5
            second = jnp.tanh(half_act) + 1.0
            joined = half_act * second
            slope = (first * ((half - half_act) + 0.5)) * (second * ((act - joined) + 1.0))
            span = slice(op * HID + start, op * HID + start + PART)
            joined_ref[:, span] = joined
            slope_ref[:, span] = slope
            term = jnp.dot(joined, wm_ref[span, :], preferred_element_type=f32)
            pre = term if pre is None else pre + term
    pre_ref[...] = pre
    total[0] += fold_rows(pre)
    total[1] += fold_rows(pre * pre)

    @pl.when(step == pl.num_programs(0) - 1)
    def _():
        packed = pack_pair(
            jnp.sum(total[0], axis=0, keepdims=True), jnp.sum(total[1], axis=0, keepdims=True)
        )
        for index in range(out_ref.shape[0]):
            out_ref[index] = packed


def forward_call(all_rows, devices, counts, features, stats, window, pieces, block):
    total = features.shape[1]
    count = len(pieces)
    return pl.pallas_call(
        functools.partial(forward_body, all_rows, count),
        grid_spec=pltpu.PrefetchScalarGridSpec(
            num_scalar_prefetch=1,
            grid=(total // block,),
            in_specs=[
                columns_of(VALID, block),
                fixed(stats.shape),
                fixed((OPS, WINDOW, HID)),
            ]
            + [fixed(piece.shape) for piece in pieces],
            out_specs=[
                rows_of(block, HID),
                rows_of(block, CAT),
                rows_of(block, CAT),
                fixed((CAT, HID)),
                fixed((devices, 8, LANE)),
            ],
            scratch_shapes=[
                pltpu.VMEM((OPS, 2 * LANE, HID), bf16),
                pltpu.VMEM((2, 8, HID), f32),
                pltpu.VMEM((WIDE, block), bf16),
            ],
        ),
        out_shape=[
            shape((total, HID), f32),
            shape((total, CAT), bf16),
            shape((total, CAT), bf16),
            shape((CAT, HID), bf16),
            shape((devices, 8, LANE), f32),
        ],
        compiler_params=params(),
        cost_estimate=cost(44),
        name="forward_layers",
    )(counts, features, stats, window, *pieces)


def head_body(
    all_rows,
    counts,
    pre_ref,
    stats_ref,
    wo_ref,
    labels_ref,
    back_ref,
    logits_ref,
    grad_ref,
    sums_ref,
    wo_low,
    norm,
    total,
):
    step = pl.program_id(0)
    block = pre_ref.shape[0]

    @pl.when(step == 0)
    def _():
        total[...] = jnp.zeros_like(total)
        grad_ref[...] = jnp.zeros_like(grad_ref)
        wo_low[...] = jnp.concatenate(
            [wo_ref[...], jnp.zeros((CPAD - CLS, HID), f32)], axis=0
        ).astype(bf16)
        mean, scale = mid_scale(stats_ref, all_rows)
        norm[0:1, :] = 0.5 * scale
        norm[1:2, :] = -0.5 * scale * mean

    kind = lax.broadcasted_iota(jnp.int32, (CPAD, HEAD), 0)
    for start in range(0, block, HEAD):
        rows = slice(start, start + HEAD)
        logits = None
        kept = []
        for at in range(0, HID, PART):
            span = slice(at, at + PART)
            half = pre_ref[rows, span] * norm[0:1, span] + norm[1:2, span]
            raised = jnp.tanh(half) + 1.0
            hidden = half * raised
            slope = raised * ((half - 0.5 * hidden) + 0.5)
            hidden = hidden.astype(bf16)
            term = dot_on(wo_low[:, span], hidden, 1, 1)
            logits = term if logits is None else logits + term
            kept.append((span, half, hidden, slope))
        logits_ref[:, rows] = logits.astype(bf16)
        column = step * block + start + lax.broadcasted_iota(jnp.int32, (CPAD, HEAD), 1)
        real = kind < CLS
        top = jnp.max(jnp.where(real, logits, -jnp.inf), axis=0, keepdims=True)
        powers = jnp.where(real, jnp.exp(logits - top), 0.0)
        probs = powers / jnp.sum(powers, axis=0, keepdims=True)
        score = (probs - jnp.where(kind == labels_ref[:, rows], 1.0, 0.0)) / all_rows
        score = jnp.where(column < own_count(counts), score, 0.0).astype(bf16)
        for span, half, hidden, slope in kept:
            grad_ref[:, span] += dot_on(score, hidden, 1, 0)
            back = dot_on(score, wo_low[:, span], 0, 0) * slope
            total[0, :, span] += fold_rows(back)
            total[1, :, span] += fold_rows(back * half)
            back_ref[rows, span] = back.astype(bf16)

    @pl.when(step == pl.num_programs(0) - 1)
    def _():
        packed = pack_pair(
            jnp.sum(total[0], axis=0, keepdims=True),
            2.0 * jnp.sum(total[1], axis=0, keepdims=True),
        )
        for index in range(sums_ref.shape[0]):
            sums_ref[index] = packed


def head_call(all_rows, counts, pre, stats, w_out, labels, block):
    total = pre.shape[0]
    return pl.pallas_call(
        functools.partial(head_body, all_rows),
        grid_spec=pltpu.PrefetchScalarGridSpec(
            num_scalar_prefetch=1,
            grid=(total // block,),
            in_specs=[
                rows_of(block, HID),
                fixed(stats.shape),
                fixed((CLS, HID)),
                columns_of(1, block),
            ],
            out_specs=[
                rows_of(block, HID),
                columns_of(CPAD, block),
                fixed((CPAD, HID)),
                fixed(stats.shape),
            ],
            scratch_shapes=[
                pltpu.VMEM((CPAD, HID), bf16),
                pltpu.VMEM((8, HID), f32),
                pltpu.VMEM((2, 8, HID), f32),
            ],
        ),
        out_shape=[
            shape((total, HID), bf16),
            shape((CPAD, total), bf16),
            shape((CPAD, HID), f32),
            shape(stats.shape, f32),
        ],
        compiler_params=params(),
        cost_estimate=cost(18),
        name="head",
    )(counts, pre, stats, w_out, labels)


def add_windows(pieces, write):
    for op, piece in enumerate(pieces):
        start = op * STRIDE
        skip = WINDOW - STRIDE if op else 0
        stop = WINDOW if op == OPS - 1 else STRIDE
        if op:
            write(start, pieces[op - 1][STRIDE:WINDOW, :] + piece[:skip, :])
        write(start + skip, piece[skip:stop, :])


def branch_back_body(
    all_rows,
    counts,
    pre_ref,
    back_ref,
    slope_ref,
    x_ref,
    wm_ref,
    window_ref,
    mid_stats_ref,
    sums_ref,
    stats_ref,
    grad_out_ref,
    gram_ref,
    mid_ref,
    part_ref,
    all_ref,
    norm,
    halved,
    grad,
    xa_ref,
):
    step = pl.program_id(0)

    @pl.when(step == 0)
    def _():
        grad[...] = jnp.zeros_like(grad)
        stats = add_up(stats_ref)
        for op in range(OPS):
            halved[op : op + 1, :] = 0.5 * branch_scale(stats, op, all_rows)[1]
        mean, scale = mid_scale(mid_stats_ref, all_rows)
        level, slant = unpack_pair(add_up(sums_ref))
        slant = scale * scale * (slant / all_rows)
        norm[0:1, :] = scale
        norm[1:2, :] = slant
        norm[2:3, :] = mean * slant - scale * (level / all_rows)

    mask_rows(counts, x_ref, xa_ref)
    mid = (
        back_ref[...].astype(f32) * norm[0:1, :]
        - pre_ref[...] * norm[1:2, :]
        + norm[2:3, :]
    ).astype(bf16)
    mid_ref[...] = mid
    pieces = []
    for op in range(OPS):
        span = slice(op * HID, (op + 1) * HID)
        joined_back = dot_on(mid, wm_ref[span, :], 1, 1)
        back = (
            (joined_back * halved[op : op + 1, :]) * slope_ref[:, span].astype(f32)
        ).astype(bf16)
        line = slice(op * LANE, (op + 1) * LANE)
        grad[line, :HID] += dot_on(window_rows(xa_ref, op), back, 1, 0)
        pieces.append(dot_on(window_ref[op], back, 1, 1))

    def write(at, value):
        part_ref[at : at + value.shape[0], :] = value.astype(bf16)

    add_windows(pieces, write)

    @pl.when(step == pl.num_programs(0) - 1)
    def _():
        means = add_up(stats_ref)[:, HID:] / all_rows
        means = jnp.where(
            lax.broadcasted_iota(jnp.int32, means.shape, 1) < WINDOW, means, 0.0
        )
        turned = means.T
        for op in range(OPS):
            start = op * LANE
            gram = gram_ref[op]
            mean, column = means[op : op + 1, :], turned[:, op : op + 1]
            sums, count = gram[WINDOW : WINDOW + 1, :], gram[WINDOW:WINDOW + 1, WINDOW : WINDOW + 1]
            gram = gram - column * (sums - count * mean) - gram[:, WINDOW : WINDOW + 1] * mean
            grad[start : start + LANE, HID:] = gram
            level = grad[start + WINDOW : start + WINDOW + 1, :HID]
            grad[start : start + LANE, :HID] = jnp.concatenate(
                [
                    grad[start : start + WINDOW, :HID] - column[:WINDOW] * level,
                    level,
                    grad_out_ref[op * SHARE : (op + 1) * SHARE, :],
                    jnp.zeros((LANE - WINDOW - 1 - SHARE, HID), f32),
                ],
                axis=0,
            )
        size = all_ref.shape[1]
        for index, block_index in enumerate(owned_order(all_ref.shape[0])):
            at = block_index * size
            all_ref[index] = grad[at : at + size, :].astype(bf16)


def branch_back_call(
    all_rows,
    devices,
    counts,
    pre,
    back,
    slope,
    features,
    mid_low,
    window,
    mid_stats,
    sums,
    stats,
    grad_out,
    gram,
    block,
):
    total = pre.shape[0]
    wide = HID + LANE
    parts = (devices, OPS * LANE // devices, wide)
    return pl.pallas_call(
        functools.partial(branch_back_body, all_rows),
        grid_spec=pltpu.PrefetchScalarGridSpec(
            num_scalar_prefetch=1,
            grid=(total // block,),
            in_specs=[
                rows_of(block, HID),
                rows_of(block, HID),
                rows_of(block, CAT),
                columns_of(VALID, block),
                fixed((CAT, HID)),
                fixed((OPS, WINDOW, HID)),
                fixed(mid_stats.shape),
                fixed(sums.shape),
                fixed(stats.shape),
                fixed((CPAD, HID)),
                fixed((OPS, LANE, LANE)),
            ],
            out_specs=[rows_of(block, HID), columns_of(VALID, block), fixed(parts)],
            scratch_shapes=[
                pltpu.VMEM((8, HID), f32),
                pltpu.VMEM((8, HID), f32),
                pltpu.VMEM((OPS * LANE, wide), f32),
                pltpu.VMEM((WIDE, block), bf16),
            ],
        ),
        out_shape=[shape((total, HID), bf16), shape((VALID, total), bf16), shape(parts, bf16)],
        compiler_params=params(),
        cost_estimate=cost(48),
        name="branch_back",
    )(counts, pre, back, slope, features, mid_low, window, mid_stats, sums, stats, grad_out, gram)


def mid_grad_body(mid_ref, joined_ref, *refs):
    step = pl.program_id(0)
    parts, grad = refs[:-1], refs[-1]

    @pl.when(step == 0)
    def _():
        grad[...] = jnp.zeros_like(grad)

    for op in range(OPS):
        span = slice(op * HID, (op + 1) * HID)
        grad[span, :] += dot_on(joined_ref[:, span], mid_ref[...], 0, 0)

    @pl.when(step == pl.num_programs(0) - 1)
    def _():
        groups = lax.axis_size("row")
        row = lax.axis_index("row")
        core, far = lax.rem(row, 2), row // (groups // 2)
        pairs, size = parts[0].shape[0], parts[0].shape[1]
        for index, part in enumerate(parts):
            which = core if index < 2 else 1 - core
            half = far if index % 2 == 0 else 1 - far
            for pair in range(pairs):
                chunk = 2 * (half * pairs + pair) + which
                part[pair] = grad[pl.ds(pl.multiple_of(chunk * size, size), size), :]


def mid_grad_call(groups, mid, joined, block):
    total = mid.shape[0]
    parted = (groups // 4, CAT // groups, HID)
    return pl.pallas_call(
        mid_grad_body,
        grid=(total // block,),
        in_specs=[rows_of(block, HID), rows_of(block, CAT)],
        out_specs=[fixed(parted)] * 4,
        out_shape=[shape(parted, f32)] * 4,
        scratch_shapes=[pltpu.VMEM((CAT, HID), f32)],
        compiler_params=params(),
        cost_estimate=cost(25),
        name="mid_grad",
    )(mid, joined)


def branch_terms(all_rows, scale, window, raw):
    level = raw[WINDOW : WINDOW + 1, :]
    inner = scale * jnp.sum(window.astype(f32) * raw[:WINDOW, :], axis=0, keepdims=True)
    return level / all_rows, scale * (inner / all_rows)


def rows_back_body(
    all_rows,
    counts,
    x_ref,
    part_ref,
    stats_ref,
    window_ref,
    own_ref,
    near_ref,
    out_ref,
    inner,
    base,
    grads,
):
    step = pl.program_id(0)
    block = x_ref.shape[1]

    @pl.when(step == 0)
    def _():
        gather_halves(own_ref, near_ref, grads)
        stats = add_up(stats_ref)
        for op in range(OPS):
            mean, scale = branch_scale(stats, op, all_rows)
            window = window_ref[op]
            level, slant = branch_terms(
                all_rows, scale, window, grads[op * LANE : (op + 1) * LANE, :HID].astype(f32)
            )
            inner[op] = dot_on((window.astype(f32) * -slant).astype(bf16), window, 1, 1).astype(bf16)
            base[op] = jnp.sum(
                window.astype(f32) * (mean * slant - level), axis=1, keepdims=True
            )

    moved = []
    for op in range(OPS):
        rows = x_ref[op * STRIDE : op * STRIDE + WINDOW, :]
        moved.append(jnp.dot(inner[op], rows, preferred_element_type=f32) + base[op])
    column = step * block + lax.broadcasted_iota(jnp.int32, (1, block), 1)
    valid = column < own_count(counts)

    def write(at, value):
        span = slice(at, at + value.shape[0])
        value = jnp.where(valid, value + part_ref[span, :].astype(f32), 0.0)
        out_ref[span, :] = value.astype(bf16)

    add_windows(moved, write)


def rows_back_call(all_rows, counts, features, part, stats, window, halves, block):
    total = features.shape[1]
    return pl.pallas_call(
        functools.partial(rows_back_body, all_rows),
        grid_spec=pltpu.PrefetchScalarGridSpec(
            num_scalar_prefetch=1,
            grid=(total // block,),
            in_specs=[
                columns_of(VALID, block),
                columns_of(VALID, block),
                fixed(stats.shape),
                fixed((OPS, WINDOW, HID)),
            ]
            + [fixed(half.shape) for half in halves],
            out_specs=columns_of(VALID, block),
            scratch_shapes=[
                pltpu.VMEM((OPS, WINDOW, WINDOW), bf16),
                pltpu.VMEM((OPS, WINDOW, 1), f32),
                pltpu.VMEM((OPS * LANE, HID + LANE), bf16),
            ],
        ),
        out_shape=shape((VALID, total), bf16),
        compiler_params=params(),
        cost_estimate=cost(8),
        name="rows_back",
    )(counts, features, part, stats, window, *halves)


def slots_of(rows, peers):
    return -(-(rows // LANE + 1) // peers)


def first_row(counts, source):
    row = lax.axis_index("row")
    begin = jnp.int32(0)
    for peer in range(counts.shape[1]):
        begin += jnp.where(peer < source, counts[row, peer], 0)
    return begin


def deal_body(counts, logits_ref, out_ref):
    peers = out_ref.shape[0]
    tiles = logits_ref.shape[1] // LANE
    begin = first_row(counts, lax.axis_index("col"))
    count = own_count(counts)
    shift = lax.rem(begin, LANE)
    chunk = begin // LANE
    lane = lax.broadcasted_iota(jnp.int32, (CPAD, LANE), 1)
    empty = jnp.zeros((CPAD, LANE), f32)
    left = empty
    for tile in range(peers * (out_ref.shape[2] // LANE)):
        right = empty
        if tile < tiles:
            piece = logits_ref[:, tile * LANE : (tile + 1) * LANE].astype(f32)
            piece = jnp.where(tile * LANE + lane < count, piece, 0.0)
            right = pltpu.roll(piece, shift, 1)
        slot = tile // peers * LANE
        peer = lax.rem(chunk + tile, peers)
        out_ref[peer, :, slot : slot + LANE] = jnp.where(lane < shift, left, right).astype(bf16)
        left = right


def deal_call(counts, logits, peers):
    total = logits.shape[1]
    dealt = (peers, CPAD, slots_of(total, peers) * LANE)
    return pl.pallas_call(
        deal_body,
        grid_spec=pltpu.PrefetchScalarGridSpec(
            num_scalar_prefetch=1,
            grid=(1,),
            in_specs=[fixed((CPAD, total))],
            out_specs=fixed(dealt),
        ),
        out_shape=shape(dealt, bf16),
        compiler_params=params(),
        cost_estimate=cost(3),
        name="deal_logits",
    )(counts, logits)


def collect_body(counts, dealt_ref, out_ref, held):
    peers, _, width = dealt_ref.shape
    member = lax.axis_index("col")
    held[...] = jnp.zeros_like(held)
    for source in range(peers):
        chunk = first_row(counts, source) // LANE
        ahead = lax.rem(member + peers - lax.rem(chunk, peers), peers)
        at = pl.ds(pl.multiple_of((chunk + ahead) // peers * LANE, LANE), width)
        held[:, at] += dealt_ref[source].astype(f32)
    share = out_ref.shape[2]
    for peer in range(peers):
        out_ref[peer] = held[:, peer * share : (peer + 1) * share].astype(bf16)


def collect_call(counts, dealt):
    peers, height, width = dealt.shape
    collected = (peers, height, AVG // peers)
    return pl.pallas_call(
        collect_body,
        grid_spec=pltpu.PrefetchScalarGridSpec(
            num_scalar_prefetch=1,
            grid=(1,),
            in_specs=[fixed(dealt.shape)],
            out_specs=fixed(collected),
            scratch_shapes=[pltpu.VMEM((height, AVG + LANE + width), f32)],
        ),
        out_shape=shape(collected, bf16),
        compiler_params=params(),
        cost_estimate=cost(3),
        name="collect_logits",
    )(counts, dealt)


def join_body(pieces_ref, out_ref):
    peers, _, share = pieces_ref.shape
    for peer in range(peers):
        for index in range(share // LANE):
            at = (index * peers + peer) * LANE
            piece = pieces_ref[peer, :, index * LANE : (index + 1) * LANE].astype(f32)
            out_ref[:, at : at + LANE] = piece[:CLS, :]


def join_call(pieces):
    return pl.pallas_call(
        join_body,
        out_shape=shape((CLS, AVG), f32),
        compiler_params=params(),
        cost_estimate=cost(2),
        name="join_logits",
    )(pieces)


def moments(turned, first, second):
    new_first = beta_first * first + (1.0 - beta_first) * turned
    new_second = beta_second * second + (1.0 - beta_second) * turned * turned
    direction = (
        new_first
        / (1.0 - beta_first**STEP)
        / (jnp.sqrt(new_second / (1.0 - beta_second**STEP)) + adam_eps)
    )
    return new_first, new_second, direction


def dot_parts(first_arg, second_arg, first_dim, second_dim):
    first_high, first_low = split_low(first_arg)
    second_high, second_low = split_low(second_arg)
    return dot_on(first_high, second_high, first_dim, second_dim) + (
        dot_on(first_high, second_low, first_dim, second_dim)
        + dot_on(first_low, second_high, first_dim, second_dim)
    )


def factor(old, grad, dim):
    low = grad.astype(bf16)
    return beta_factor * old + (1.0 - beta_factor) * dot_on(low, low, dim, dim)


def branch_update_body(
    all_rows,
    stats_ref,
    window_ref,
    own_ref,
    near_ref,
    w_ref,
    left_ref,
    right_ref,
    basis_left_ref,
    basis_right_ref,
    first_ref,
    second_ref,
    new_left_ref,
    new_right_ref,
    new_first_ref,
    new_second_ref,
    new_w_ref,
    low_w_ref,
    grad_out_ref,
    grads,
):
    step = pl.program_id(0)

    @pl.when(step == 0)
    def _():
        gather_halves(own_ref, near_ref, grads)
        for op in range(OPS):
            at = op * LANE + WINDOW + 1
            grad_out_ref[op * SHARE : (op + 1) * SHARE, :] = grads[at : at + SHARE, :HID].astype(f32)

    for op in range(OPS):

        @pl.when(step == op)
        def _(op=op):
            mean, scale = branch_scale(add_up(stats_ref), op, all_rows)
            window = window_ref[op]
            raw = grads[op * LANE : (op + 1) * LANE, :HID].astype(f32)
            gram = grads[op * LANE : (op + 1) * LANE, HID:]
            level, slant = branch_terms(all_rows, scale, window, raw)
            normed = jnp.dot(gram, padded(window), preferred_element_type=f32)
            grad = raw[:WINDOW, :] - normed[:WINDOW, :] * slant
            shift = op * (DIN - STRIDE)
            grad = grad[shift : shift + DIN, :]
            new_left_ref[:, op, :] = factor(left_ref[:, op, :], grad, 1)
            new_right_ref[0] = factor(right_ref[0], grad, 0)
            basis_left, basis_right = basis_left_ref[:, op, :], basis_right_ref[0]
            turned = dot_parts(basis_left, grad, 0, 0)
            turned = dot_parts(turned, basis_right, 1, 0)
            new_first, new_second, direction = moments(
                turned, first_ref[:, op, :], second_ref[:, op, :]
            )
            new_first_ref[:, op, :] = new_first
            new_second_ref[:, op, :] = new_second
            back = dot_parts(basis_left, direction, 1, 0)
            back = dot_parts(back, basis_right, 1, 1)
            new_w = w_ref[:, op, :] - rate_branch * back
            new_w_ref[:, op, :] = new_w
            low_w_ref[:, op, :] = new_w.astype(bf16)


def branch_update_call(
    all_rows, stats, window, halves, w, left, right, basis_left, basis_right, first, second
):
    small, wide = fixed((DIN, OPS, DIN)), fixed((DIN, OPS, HID))
    square = pl.BlockSpec((1, HID, HID), lambda k: (k, 0, 0))
    return pl.pallas_call(
        functools.partial(branch_update_body, all_rows),
        grid=(OPS,),
        in_specs=[fixed(stats.shape), fixed((OPS, WINDOW, HID))]
        + [fixed(half.shape) for half in halves]
        + [wide, small, square, small, square, wide, wide],
        out_specs=[small, square, wide, wide, wide, wide, fixed((CPAD, HID))],
        out_shape=[
            shape((DIN, OPS, DIN), f32),
            shape((OPS, HID, HID), f32),
            shape((DIN, OPS, HID), f32),
            shape((DIN, OPS, HID), f32),
            shape((DIN, OPS, HID), f32),
            shape((DIN, OPS, HID), bf16),
            shape((CPAD, HID), f32),
        ],
        scratch_shapes=[pltpu.VMEM((OPS * LANE, HID + LANE), bf16)],
        compiler_params=params(),
        cost_estimate=cost(12),
        name="branch_update",
    )(stats, window, *halves, w, left, right, basis_left, basis_right, first, second)


def out_update_body(
    grad_ref,
    w_ref,
    left_ref,
    right_ref,
    basis_left_ref,
    basis_right_ref,
    first_ref,
    second_ref,
    new_left_ref,
    new_right_ref,
    new_first_ref,
    new_second_ref,
    new_w_ref,
    low_w_ref,
):
    grad = grad_ref[:CLS, :]
    new_left_ref[...] = factor(left_ref[...], grad, 0)
    new_right_ref[...] = factor(right_ref[...], grad, 1)
    turned = dot_parts(grad, basis_left_ref[...], 1, 0)
    turned = dot_parts(basis_right_ref[...], turned, 0, 0)
    new_first, new_second, direction = moments(turned, first_ref[...], second_ref[...])
    new_first_ref[...] = new_first
    new_second_ref[...] = new_second
    back = dot_parts(direction, basis_left_ref[...], 1, 1)
    back = dot_parts(basis_right_ref[...], back, 1, 0)
    new_w = w_ref[...] - rate_out * back
    new_w_ref[...] = new_w
    low_w_ref[...] = new_w.astype(bf16)


def out_update_call(grad, w, left, right, basis_left, basis_right, first, second):
    return pl.pallas_call(
        out_update_body,
        out_shape=[
            shape((HID, HID), f32),
            shape((CLS, CLS), f32),
            shape((CLS, HID), f32),
            shape((CLS, HID), f32),
            shape((CLS, HID), f32),
            shape((CLS, HID), bf16),
        ],
        compiler_params=params(),
        cost_estimate=cost(4),
        name="out_update",
    )(grad, w, left, right, basis_left, basis_right, first, second)


def mid_update_body(
    grad_ref, w_ref, basis_ref, first_ref, second_ref, new_first_ref, new_second_ref, new_w_ref, low_w_ref
):
    turned = dot_parts(grad_ref[...], basis_ref[...], 1, 0)
    new_first, new_second, direction = moments(turned, first_ref[...], second_ref[...])
    new_first_ref[...] = new_first
    new_second_ref[...] = new_second
    new_w = w_ref[...] - rate_mid * dot_parts(direction, basis_ref[...], 1, 1)
    new_w_ref[...] = new_w
    low_w_ref[...] = new_w.astype(bf16)


def mid_update_call(grad, w, basis, first, second):
    rows = grad.shape[0]
    return pl.pallas_call(
        mid_update_body,
        out_shape=[shape((rows, HID), f32)] * 3 + [shape((rows, HID), bf16)],
        compiler_params=params(),
        cost_estimate=cost(3),
        name="mid_update",
    )(grad, w, basis, first, second)


def half_blocks():
    parts = HID // LANE
    return [(i, j) for i in range(parts) for j in range(i, parts)]


def mid_gram_body(rows_ref, out_ref):
    rows = rows_ref[...]
    gram = dot_on(rows, rows, 0, 0)
    for index, (i, j) in enumerate(half_blocks()):
        out_ref[index] = gram[i * LANE : (i + 1) * LANE, j * LANE : (j + 1) * LANE].astype(bf16)


def mid_gram_call(rows):
    return pl.pallas_call(
        mid_gram_body,
        out_shape=shape((len(half_blocks()), LANE, LANE), bf16),
        compiler_params=params(),
        cost_estimate=cost(2),
        name="mid_gram",
    )(rows)


def mid_factor_body(right_ref, own_ref, near_ref, out_ref):
    for index, (i, j) in enumerate(half_blocks()):
        block = (1.0 - beta_factor) * (own_ref[index] + near_ref[index])
        rows, columns = slice(i * LANE, (i + 1) * LANE), slice(j * LANE, (j + 1) * LANE)
        out_ref[rows, columns] = beta_factor * right_ref[rows, columns] + block
        if i != j:
            out_ref[columns, rows] = beta_factor * right_ref[columns, rows] + block.T


def mid_factor_call(right, own, near):
    return pl.pallas_call(
        mid_factor_body,
        out_shape=shape((HID, HID), f32),
        compiler_params=params(),
        cost_estimate=cost(2),
        name="mid_factor",
    )(right, own, near)


def after(values, *others):
    return lax.optimization_barrier((values,) + others)[0]


def swap(values, axis, distance):
    peers = lax.axis_size(axis)
    return lax.ppermute(values, axis, [(peer, peer ^ distance) for peer in range(peers)])


def gather_by_doubling(values):
    steps = doubling_steps()
    for axis, distance in steps[:-1]:
        other = swap(values, axis, distance)
        bit = lax.rem(lax.axis_index(axis) // distance, 2) > 0
        values = jnp.where(
            bit,
            jnp.concatenate([other, values], axis=0),
            jnp.concatenate([values, other], axis=0),
        )
    return values, swap(values, *steps[-1])


def add_all(values):
    while len(values) > 1:
        values = [values[i] + values[i + 1] for i in range(0, len(values), 2)]
    return values[0]


def exchange(values):
    return lax.all_to_all(values, "col", 0, 0, tiled=True)


def spread_out(values, dtype=f32):
    copies = jnp.broadcast_to(values[None], (lax.axis_size("col"),) + values.shape)
    return exchange(copies.astype(dtype))


def far_copies(values):
    pieces = {0: values}
    distance = lax.axis_size("row") // 2
    while distance > 1:
        pieces.update({d ^ distance: swap(v, "row", distance) for d, v in list(pieces.items())})
        distance //= 2
    return pieces


def near_copies(pieces, *others):
    held = lax.optimization_barrier((*[pieces[d] for d in sorted(pieces)], *others))
    pieces = dict(zip(sorted(pieces), held))
    pieces.update({d ^ 1: swap(v, "row", 1) for d, v in list(pieces.items())})
    return [pieces[d] for d in sorted(pieces)], held[len(held) - len(others) :]


def sum_in_row(values):
    return add_all([values] + [swap(values, "row", d) for d in range(1, lax.axis_size("row"))])


def keep_bit(values, distance):
    bit = lax.rem(lax.axis_index("row") // distance, 2)
    pairs = values.reshape((-1, 2) + values.shape[1:])
    kept = lax.dynamic_index_in_dim(pairs, bit, 1, keepdims=False)
    sent = lax.dynamic_index_in_dim(pairs, 1 - bit, 1, keepdims=False)
    return kept, sent


def finish_scatter(values, distance):
    while distance < lax.axis_size("row") // 2:
        kept, sent = keep_bit(values, distance)
        values = kept + swap(sent.astype(bf16), "row", distance).astype(f32)
        distance *= 2
    values = values.reshape((lax.axis_size("col"), -1) + values.shape[2:]).astype(bf16)
    return jnp.sum(exchange(values).astype(f32), axis=0)


def local(
    features,
    labels,
    counts,
    w_branch,
    w_mid,
    w_out,
    left_branch,
    right_branch,
    basis_left_branch,
    basis_right_branch,
    first_branch,
    second_branch,
    right_mid,
    basis_right_mid,
    first_mid,
    second_mid,
    left_out,
    right_out,
    basis_left_out,
    basis_right_out,
    first_out,
    second_out,
):
    groups, peers = lax.axis_size("row"), lax.axis_size("col")
    devices = groups * peers
    all_rows = float(AVG * devices)

    def by_input(values):
        return values.transpose(1, 0, 2)

    turned = features.T
    own_mid = spread_out(w_mid, bf16).reshape(-1, HID)
    window, gram, branch_sums = gram_call(counts, turned, by_input(w_branch), 4096)
    branch_sums = sum_in_row(branch_sums)
    own_mid = after(own_mid, branch_sums)
    pieces = far_copies(own_mid)
    branch_stats = spread_out(branch_sums)
    pieces, (branch_stats,) = near_copies(pieces, branch_stats)
    pre, joined, slope, mid_low, mid_sums = forward_call(
        all_rows, devices, counts, turned, branch_stats, window, pieces, 1024
    )
    mid_stats = lax.all_to_all(mid_sums, BOTH, 0, 0, tiled=True)
    back, logits, grad_out, back_sums = head_call(
        all_rows, counts, pre, mid_stats, w_out.T, labels.reshape(1, -1), 2048
    )
    back_stats = lax.all_to_all(back_sums, BOTH, 0, 0, tiled=True)

    dealt = deal_call(counts, logits, peers)
    back_stats, dealt = lax.optimization_barrier((back_stats, dealt))
    dealt = exchange(dealt)
    mid, part, grad_branch = branch_back_call(
        all_rows,
        devices,
        counts,
        pre,
        back,
        slope,
        turned,
        mid_low,
        window,
        mid_stats,
        back_stats,
        branch_stats,
        grad_out,
        gram,
        1024,
    )
    grad_branch, dealt = lax.optimization_barrier((grad_branch, dealt))
    grad_branch = lax.all_to_all(grad_branch, BOTH, 0, 0, tiled=True)
    parts = mid_grad_call(groups, mid, joined, 1024)
    grad_branch, *parts = lax.optimization_barrier((grad_branch, *parts))
    kept, sent = parts[:2], parts[2:]
    grad_branch = jnp.sum(grad_branch.astype(f32), axis=0).astype(bf16)
    near = [swap(part, "row", 1) for part in sent]
    halves = [half.reshape(-1, HID + LANE) for half in gather_by_doubling(grad_branch)]
    away = (kept[1] + near[1]).astype(bf16)
    far = swap(away, "row", groups // 2)
    grad_mid = finish_scatter(kept[0] + near[0] + far.astype(f32), 2)
    grad_features = rows_back_call(
        all_rows, counts, turned, part, branch_stats, window, halves, 4096
    )
    collected = collect_call(counts, after(dealt, grad_features))
    grad_mid, grad_features, collected = lax.optimization_barrier(
        (grad_mid, grad_features, collected)
    )
    all_mid = spread_out(grad_mid, bf16).reshape(-1, HID)
    *branch_parts, grad_out = branch_update_call(
        all_rows,
        branch_stats,
        window,
        halves,
        by_input(w_branch),
        by_input(left_branch),
        right_branch,
        by_input(basis_left_branch),
        basis_right_branch,
        by_input(first_branch),
        by_input(second_branch),
    )
    held = lax.optimization_barrier((all_mid, *branch_parts))
    all_mid, branch_parts = held[0], held[1:]
    collected = exchange(after(collected, all_mid))
    mid_gram = mid_gram_call(all_mid)
    distance = groups // 2
    others = swap(mid_gram, "row", distance)
    mid_parts = mid_update_call(
        after(grad_mid, mid_gram), w_mid, basis_right_mid, first_mid, second_mid
    )
    out_parts = out_update_call(
        after(grad_out, mid_gram),
        w_out.T,
        left_out,
        right_out,
        basis_left_out,
        basis_right_out,
        first_out.T,
        second_out.T,
    )
    mid_gram, others, *held = lax.optimization_barrier(
        (mid_gram, others, *mid_parts, *out_parts)
    )
    mid_parts, out_parts = held[:4], held[4:]
    mid_gram = mid_gram.astype(f32) + others.astype(f32)
    while distance > 2:
        distance //= 2
        mid_gram = mid_gram + swap(mid_gram, "row", distance)
    others = swap(mid_gram, "row", 1)
    new_logits = join_call(after(collected, mid_gram))
    others, new_logits = lax.optimization_barrier((others, new_logits))
    new_right_mid = mid_factor_call(right_mid, mid_gram, others)
    branch_parts = [
        part if index == 1 else by_input(part) for index, part in enumerate(branch_parts)
    ]
    out_parts = list(out_parts[:2]) + [part.T for part in out_parts[2:]]
    return (new_logits.T, grad_features.T, *branch_parts, new_right_mid, *mid_parts, *out_parts)


def solution(mesh):
    split, rows, whole = P(BOTH, None), P(BOTH), P()
    in_specs = (split, rows, whole, whole, split) + (whole,) * 9 + (split, split) + (whole,) * 6
    out_specs = (split, split) + (whole,) * 7 + (split,) * 4 + (whole,) * 6
    return jax.shard_map(local, mesh=mesh, in_specs=in_specs, out_specs=out_specs, check_vma=False)
```

```python
import functools

import jax
import jax.numpy as jnp
from jax import lax
from jax.experimental import pallas as pl
from jax.experimental.pallas import tpu as pltpu
from jax.sharding import PartitionSpec as P

OPS = 4
DIN = 100
HID = 512
CLS = 47
AVG = 4096
STEP = 5
CAT = 2048
LANE = 128
CPAD = 48
STRIDE = 96
WINDOW = 112
VALID = 400
HEAD = 2048
PART = 256
WIDE = 416
SHARE = 12
BOTH = ("row", "col")

beta_first = 0.5
beta_second = 0.9
beta_factor = 0.95
adam_eps = 1e-08
norm_eps = 1e-05
rate_branch = 0.1
rate_mid = 0.02
rate_out = 0.04
f32 = jnp.float32
bf16 = jnp.bfloat16
VMEM_LIMIT = 50 * 2**20
VMEM_WHOLE = 60 * 2**20


def dot_on(first_arg, second_arg, first_dim, second_dim, precision=None):
    return lax.dot_general(
        first_arg,
        second_arg,
        (((first_dim,), (second_dim,)), ((), ())),
        precision=precision,
        preferred_element_type=f32,
    )


def params(limit=VMEM_LIMIT):
    return pltpu.CompilerParams(vmem_limit_bytes=limit)


def cost(microseconds):
    return pl.CostEstimate(
        flops=int(microseconds * 1e9), bytes_accessed=1, transcendentals=0
    )


def shape(dims, dtype):
    return jax.ShapeDtypeStruct(dims, dtype)


def fixed(dims):
    return pl.BlockSpec(dims, lambda *_: (0,) * len(dims))


def rows_of(block, width):
    return pl.BlockSpec((block, width), lambda i, *_: (i, 0))


def columns_of(height, block):
    return pl.BlockSpec((height, block), lambda i, *_: (0, i))


def low_f32(values):
    return values.astype(bf16).astype(f32)


def split_low(values):
    high = values.astype(bf16)
    return high, (values - high.astype(f32)).astype(bf16)


def fold_rows(values):
    return jnp.sum(values.reshape(values.shape[0] // 8, 8, values.shape[1]), axis=0)


def add_up(ref):
    value = ref[0]
    for index in range(1, ref.shape[0]):
        value = value + ref[index]
    return value


def own_count(counts):
    return counts[lax.axis_index("row"), lax.axis_index("col")]


def branch_scale(stats, op, all_rows):
    mean = stats[op : op + 1, :HID] / all_rows
    square = stats[OPS + op : OPS + op + 1, :HID] / all_rows
    return mean, lax.rsqrt(square - mean * mean + norm_eps)


def unpack_pair(packed):
    parts = HID // LANE
    return [
        jnp.concatenate(
            [packed[index * parts + part : index * parts + part + 1, :] for part in range(parts)],
            axis=1,
        )
        for index in range(2)
    ]


def pack_pair(first, second):
    parts = HID // LANE
    return jnp.concatenate(
        [
            value[:, part * LANE : (part + 1) * LANE]
            for value in (first, second)
            for part in range(parts)
        ],
        axis=0,
    )


def mid_scale(stats_ref, all_rows):
    total, square = unpack_pair(add_up(stats_ref))
    mean = total / all_rows
    return mean, lax.rsqrt(square / all_rows - mean * mean + norm_eps)


def window_rows(x_ref, op):
    return jnp.concatenate(
        [x_ref[op * STRIDE : op * STRIDE + WINDOW, :], x_ref[VALID:WIDE, :]], axis=0
    )


def padded(window):
    return jnp.concatenate([window, jnp.zeros((LANE - WINDOW, HID), bf16)], axis=0)


def gram_product(gram, window):
    weight = padded(window)
    product = None
    for _ in range(3):
        part = gram.astype(bf16)
        gram = gram - part.astype(f32)
        term = jnp.dot(part, weight, preferred_element_type=f32)
        product = term if product is None else product + term
    return product


def mask_rows(counts, x_ref, held):
    block = x_ref.shape[1]
    column = pl.program_id(0) * block + lax.broadcasted_iota(jnp.int32, (16, block), 1)
    valid = jnp.where(column < own_count(counts), 1.0, 0.0)
    line = lax.broadcasted_iota(jnp.int32, (16, block), 0)
    held[:VALID, :] = x_ref[...] * valid[0:1, :].astype(bf16)
    held[VALID:, :] = jnp.where(line < 2, valid, 0.0).astype(bf16)


def doubling_steps():
    steps = []
    distance = lax.axis_size("row") // 2
    while distance > 1:
        steps.append(("row", distance))
        distance //= 2
    distance = lax.axis_size("col") // 2
    while distance:
        steps.append(("col", distance))
        distance //= 2
    return steps + [("row", 1)]


def owned_order(devices):
    peers = lax.axis_size("col")
    order = []
    for device in range(devices):
        place = {"row": device // peers, "col": device % peers}
        bits = [place[axis] // distance % 2 for axis, distance in doubling_steps()]
        order.append(sum(bit << index for index, bit in enumerate(bits)))
    return order


def gather_quarters(refs, held):
    core = lax.rem(lax.axis_index("row"), 2)
    side = lax.rem(lax.axis_index("col"), 2)
    size = refs[0].shape[0]
    for index, ref in enumerate(refs):
        place = (core ^ (index // 2)) * 2 + (side ^ (index % 2))
        held[pl.ds(pl.multiple_of(place * size, size), size), :] = ref[...]


def gather_pieces(refs, held):
    row = lax.axis_index("row")
    size = held.shape[0] // len(refs)
    for index, ref in enumerate(refs):
        at = pl.multiple_of((row ^ index) * size, size)
        held[pl.ds(at, size), :] = ref[...].reshape(size, held.shape[1]).astype(held.dtype)


def gram_body(counts, x_ref, w_ref, window_ref, gram_ref, stats_ref, xa_ref):
    step = pl.program_id(0)

    @pl.when(step == 0)
    def _():
        gram_ref[...] = jnp.zeros_like(gram_ref)
        for op in range(OPS):
            shift = op * (DIN - STRIDE)
            parts = [low_f32(w_ref[:, op, :])]
            if shift:
                parts.insert(0, jnp.zeros((shift, HID), f32))
            if WINDOW - DIN - shift:
                parts.append(jnp.zeros((WINDOW - DIN - shift, HID), f32))
            window_ref[op] = jnp.concatenate(parts, axis=0).astype(bf16)

    mask_rows(counts, x_ref, xa_ref)
    for op in range(0, OPS, 2):
        rows = jnp.concatenate([window_rows(xa_ref, op), window_rows(xa_ref, op + 1)], axis=0)
        both = dot_on(rows, rows, 1, 1)
        gram_ref[op] += both[:LANE, :LANE]
        gram_ref[op + 1] += both[LANE:, LANE:]

    @pl.when(step == pl.num_programs(0) - 1)
    def _():
        for op in range(OPS):
            turned = gram_product(gram_ref[op], window_ref[op])
            stats_ref[op : op + 1, :HID] = turned[WINDOW : WINDOW + 1, :]
            stats_ref[OPS + op : OPS + op + 1, :HID] = jnp.sum(
                window_ref[op].astype(f32) * turned[:WINDOW, :], axis=0, keepdims=True
            )
            stats_ref[op : op + 1, HID:] = gram_ref[op, WINDOW : WINDOW + 1, :]
            stats_ref[OPS + op : OPS + op + 1, HID:] = jnp.zeros((1, LANE), f32)


def gram_call(counts, features, w_branch, block):
    total = features.shape[1]
    return pl.pallas_call(
        gram_body,
        grid_spec=pltpu.PrefetchScalarGridSpec(
            num_scalar_prefetch=1,
            grid=(total // block,),
            in_specs=[columns_of(VALID, block), fixed((DIN, OPS, HID))],
            out_specs=[
                fixed((OPS, WINDOW, HID)),
                fixed((OPS, LANE, LANE)),
                fixed((2 * OPS, HID + LANE)),
            ],
            scratch_shapes=[pltpu.VMEM((WIDE, block), bf16)],
        ),
        out_shape=[
            shape((OPS, WINDOW, HID), bf16),
            shape((OPS, LANE, LANE), f32),
            shape((2 * OPS, HID + LANE), f32),
        ],
        compiler_params=params(),
        cost_estimate=cost(6),
        name="row_moments",
    )(counts, features, w_branch)


def forward_body(all_rows, count, counts, *refs):
    x_ref, stats_ref, window_ref = refs[:3]
    pieces = refs[3 : 3 + count]
    pre_ref, joined_ref, slope_ref, wm_ref, out_ref, wide, total, xa_ref = refs[3 + count :]
    step = pl.program_id(0)

    @pl.when(step == 0)
    def _():
        total[...] = jnp.zeros_like(total)
        gather_pieces(pieces, wm_ref)
        stats = add_up(stats_ref)
        line = lax.broadcasted_iota(jnp.int32, (LANE - WINDOW, HID), 0)
        for op in range(OPS):
            mean, scale = branch_scale(stats, op, all_rows)
            half = 0.5 * scale
            high, low = split_low(window_ref[op].astype(f32) * half)
            base = -mean * half
            base_high = low_f32(base)
            wide[op, :WINDOW, :] = high
            wide[op, WINDOW:LANE, :] = jnp.where(
                line == 0, base_high, jnp.where(line == 1, base - base_high, 0.0)
            ).astype(bf16)
            wide[op, LANE : LANE + WINDOW, :] = low
            wide[op, LANE + WINDOW :, :] = jnp.zeros((LANE - WINDOW, HID), bf16)

    mask_rows(counts, x_ref, xa_ref)
    pre = None
    for op in range(OPS):
        rows = window_rows(xa_ref, op).T
        rows = jnp.concatenate([rows, rows], axis=1)
        for start in range(0, HID, PART):
            half = jnp.dot(
                rows, wide[op, :, start : start + PART], preferred_element_type=f32
            ).astype(bf16)
            first = jnp.tanh(half) + 1.0
            act = half * first
            half_act = act * 0.5
            second = jnp.tanh(half_act) + 1.0
            joined = half_act * second
            slope = (first * ((half - half_act) + 0.5)) * (second * ((act - joined) + 1.0))
            span = slice(op * HID + start, op * HID + start + PART)
            joined_ref[:, span] = joined
            slope_ref[:, span] = slope
            term = jnp.dot(joined, wm_ref[span, :], preferred_element_type=f32)
            pre = term if pre is None else pre + term
    pre_ref[...] = pre
    total[0] += fold_rows(pre)
    total[1] += fold_rows(pre * pre)

    @pl.when(step == pl.num_programs(0) - 1)
    def _():
        packed = pack_pair(
            jnp.sum(total[0], axis=0, keepdims=True), jnp.sum(total[1], axis=0, keepdims=True)
        )
        for index in range(out_ref.shape[0]):
            out_ref[index] = packed


def forward_call(all_rows, devices, counts, features, stats, window, pieces, block):
    total = features.shape[1]
    count = len(pieces)
    return pl.pallas_call(
        functools.partial(forward_body, all_rows, count),
        grid_spec=pltpu.PrefetchScalarGridSpec(
            num_scalar_prefetch=1,
            grid=(total // block,),
            in_specs=[
                columns_of(VALID, block),
                fixed(stats.shape),
                fixed((OPS, WINDOW, HID)),
            ]
            + [fixed(piece.shape) for piece in pieces],
            out_specs=[
                rows_of(block, HID),
                rows_of(block, CAT),
                rows_of(block, CAT),
                fixed((CAT, HID)),
                fixed((devices, 8, LANE)),
            ],
            scratch_shapes=[
                pltpu.VMEM((OPS, 2 * LANE, HID), bf16),
                pltpu.VMEM((2, 8, HID), f32),
                pltpu.VMEM((WIDE, block), bf16),
            ],
        ),
        out_shape=[
            shape((total, HID), f32),
            shape((total, CAT), bf16),
            shape((total, CAT), bf16),
            shape((CAT, HID), bf16),
            shape((devices, 8, LANE), f32),
        ],
        compiler_params=params(),
        cost_estimate=cost(44),
        name="forward_layers",
    )(counts, features, stats, window, *pieces)


def head_body(
    all_rows,
    counts,
    pre_ref,
    stats_ref,
    wo_ref,
    labels_ref,
    back_ref,
    logits_ref,
    grad_ref,
    sums_ref,
    wo_low,
    norm,
    total,
):
    step = pl.program_id(0)
    block = pre_ref.shape[0]

    @pl.when(step == 0)
    def _():
        total[...] = jnp.zeros_like(total)
        grad_ref[...] = jnp.zeros_like(grad_ref)
        wo_low[...] = jnp.concatenate(
            [wo_ref[...], jnp.zeros((CPAD - CLS, HID), f32)], axis=0
        ).astype(bf16)
        mean, scale = mid_scale(stats_ref, all_rows)
        norm[0:1, :] = 0.5 * scale
        norm[1:2, :] = -0.5 * scale * mean

    kind = lax.broadcasted_iota(jnp.int32, (CPAD, HEAD), 0)
    for start in range(0, block, HEAD):
        rows = slice(start, start + HEAD)
        logits = None
        kept = []
        for at in range(0, HID, PART):
            span = slice(at, at + PART)
            half = pre_ref[rows, span] * norm[0:1, span] + norm[1:2, span]
            raised = jnp.tanh(half) + 1.0
            hidden = half * raised
            slope = raised * ((half - 0.5 * hidden) + 0.5)
            hidden = hidden.astype(bf16)
            term = dot_on(wo_low[:, span], hidden, 1, 1)
            logits = term if logits is None else logits + term
            kept.append((span, half, hidden, slope))
        logits_ref[:, rows] = logits.astype(bf16)
        column = step * block + start + lax.broadcasted_iota(jnp.int32, (CPAD, HEAD), 1)
        real = kind < CLS
        top = jnp.max(jnp.where(real, logits, -jnp.inf), axis=0, keepdims=True)
        powers = jnp.where(real, jnp.exp(logits - top), 0.0)
        probs = powers / jnp.sum(powers, axis=0, keepdims=True)
        score = (probs - jnp.where(kind == labels_ref[:, rows], 1.0, 0.0)) / all_rows
        score = jnp.where(column < own_count(counts), score, 0.0).astype(bf16)
        for span, half, hidden, slope in kept:
            grad_ref[:, span] += dot_on(score, hidden, 1, 0)
            back = dot_on(score, wo_low[:, span], 0, 0) * slope
            total[0, :, span] += fold_rows(back)
            total[1, :, span] += fold_rows(back * half)
            back_ref[rows, span] = back.astype(bf16)

    @pl.when(step == pl.num_programs(0) - 1)
    def _():
        packed = pack_pair(
            jnp.sum(total[0], axis=0, keepdims=True),
            2.0 * jnp.sum(total[1], axis=0, keepdims=True),
        )
        for index in range(sums_ref.shape[0]):
            sums_ref[index] = packed


def head_call(all_rows, counts, pre, stats, w_out, labels, block):
    total = pre.shape[0]
    return pl.pallas_call(
        functools.partial(head_body, all_rows),
        grid_spec=pltpu.PrefetchScalarGridSpec(
            num_scalar_prefetch=1,
            grid=(total // block,),
            in_specs=[
                rows_of(block, HID),
                fixed(stats.shape),
                fixed((CLS, HID)),
                columns_of(1, block),
            ],
            out_specs=[
                rows_of(block, HID),
                columns_of(CPAD, block),
                fixed((CPAD, HID)),
                fixed(stats.shape),
            ],
            scratch_shapes=[
                pltpu.VMEM((CPAD, HID), bf16),
                pltpu.VMEM((8, HID), f32),
                pltpu.VMEM((2, 8, HID), f32),
            ],
        ),
        out_shape=[
            shape((total, HID), bf16),
            shape((CPAD, total), bf16),
            shape((CPAD, HID), f32),
            shape(stats.shape, f32),
        ],
        compiler_params=params(),
        cost_estimate=cost(18),
        name="head",
    )(counts, pre, stats, w_out, labels)


def add_windows(pieces, write):
    for op, piece in enumerate(pieces):
        start = op * STRIDE
        skip = WINDOW - STRIDE if op else 0
        stop = WINDOW if op == OPS - 1 else STRIDE
        if op:
            write(start, pieces[op - 1][STRIDE:WINDOW, :] + piece[:skip, :])
        write(start + skip, piece[skip:stop, :])


def branch_back_body(
    all_rows,
    counts,
    pre_ref,
    back_ref,
    slope_ref,
    x_ref,
    wm_ref,
    window_ref,
    mid_stats_ref,
    sums_ref,
    stats_ref,
    grad_out_ref,
    gram_ref,
    mid_ref,
    part_ref,
    all_ref,
    norm,
    halved,
    grad,
    xa_ref,
):
    step = pl.program_id(0)

    @pl.when(step == 0)
    def _():
        grad[...] = jnp.zeros_like(grad)
        stats = add_up(stats_ref)
        for op in range(OPS):
            halved[op : op + 1, :] = 0.5 * branch_scale(stats, op, all_rows)[1]
        mean, scale = mid_scale(mid_stats_ref, all_rows)
        level, slant = unpack_pair(add_up(sums_ref))
        slant = scale * scale * (slant / all_rows)
        norm[0:1, :] = scale
        norm[1:2, :] = slant
        norm[2:3, :] = mean * slant - scale * (level / all_rows)

    mask_rows(counts, x_ref, xa_ref)
    mid = (
        back_ref[...].astype(f32) * norm[0:1, :]
        - pre_ref[...] * norm[1:2, :]
        + norm[2:3, :]
    ).astype(bf16)
    mid_ref[...] = mid
    pieces = []
    for op in range(OPS):
        span = slice(op * HID, (op + 1) * HID)
        joined_back = dot_on(mid, wm_ref[span, :], 1, 1)
        back = (
            (joined_back * halved[op : op + 1, :]) * slope_ref[:, span].astype(f32)
        ).astype(bf16)
        line = slice(op * LANE, (op + 1) * LANE)
        grad[line, :HID] += dot_on(window_rows(xa_ref, op), back, 1, 0)
        pieces.append(dot_on(window_ref[op], back, 1, 1))

    def write(at, value):
        part_ref[at : at + value.shape[0], :] = value.astype(bf16)

    add_windows(pieces, write)

    @pl.when(step == pl.num_programs(0) - 1)
    def _():
        means = add_up(stats_ref)[:, HID:] / all_rows
        means = jnp.where(
            lax.broadcasted_iota(jnp.int32, means.shape, 1) < WINDOW, means, 0.0
        )
        turned = means.T
        for op in range(OPS):
            start = op * LANE
            gram = gram_ref[op]
            mean, column = means[op : op + 1, :], turned[:, op : op + 1]
            sums, count = gram[WINDOW : WINDOW + 1, :], gram[WINDOW:WINDOW + 1, WINDOW : WINDOW + 1]
            gram = gram - column * (sums - count * mean) - gram[:, WINDOW : WINDOW + 1] * mean
            grad[start : start + LANE, HID:] = gram
            level = grad[start + WINDOW : start + WINDOW + 1, :HID]
            grad[start : start + LANE, :HID] = jnp.concatenate(
                [
                    grad[start : start + WINDOW, :HID] - column[:WINDOW] * level,
                    level,
                    grad_out_ref[op * SHARE : (op + 1) * SHARE, :],
                    jnp.zeros((LANE - WINDOW - 1 - SHARE, HID), f32),
                ],
                axis=0,
            )
        size = all_ref.shape[1]
        for index, block_index in enumerate(owned_order(all_ref.shape[0])):
            at = block_index * size
            all_ref[index] = grad[at : at + size, :].astype(bf16)


def branch_back_call(
    all_rows,
    devices,
    counts,
    pre,
    back,
    slope,
    features,
    mid_low,
    window,
    mid_stats,
    sums,
    stats,
    grad_out,
    gram,
    block,
):
    total = pre.shape[0]
    wide = HID + LANE
    parts = (devices, OPS * LANE // devices, wide)
    return pl.pallas_call(
        functools.partial(branch_back_body, all_rows),
        grid_spec=pltpu.PrefetchScalarGridSpec(
            num_scalar_prefetch=1,
            grid=(total // block,),
            in_specs=[
                rows_of(block, HID),
                rows_of(block, HID),
                rows_of(block, CAT),
                columns_of(VALID, block),
                fixed((CAT, HID)),
                fixed((OPS, WINDOW, HID)),
                fixed(mid_stats.shape),
                fixed(sums.shape),
                fixed(stats.shape),
                fixed((CPAD, HID)),
                fixed((OPS, LANE, LANE)),
            ],
            out_specs=[rows_of(block, HID), columns_of(VALID, block), fixed(parts)],
            scratch_shapes=[
                pltpu.VMEM((8, HID), f32),
                pltpu.VMEM((8, HID), f32),
                pltpu.VMEM((OPS * LANE, wide), f32),
                pltpu.VMEM((WIDE, block), bf16),
            ],
        ),
        out_shape=[shape((total, HID), bf16), shape((VALID, total), bf16), shape(parts, bf16)],
        compiler_params=params(),
        cost_estimate=cost(48),
        name="branch_back",
    )(counts, pre, back, slope, features, mid_low, window, mid_stats, sums, stats, grad_out, gram)


def mid_grad_body(mid_ref, joined_ref, *refs):
    step = pl.program_id(0)
    parts, grad = refs[:-1], refs[-1]

    @pl.when(step == 0)
    def _():
        grad[...] = jnp.zeros_like(grad)

    for op in range(OPS):
        span = slice(op * HID, (op + 1) * HID)
        grad[span, :] += dot_on(joined_ref[:, span], mid_ref[...], 0, 0)

    @pl.when(step == pl.num_programs(0) - 1)
    def _():
        groups = lax.axis_size("row")
        row = lax.axis_index("row")
        core, far = lax.rem(row, 2), row // (groups // 2)
        pairs, size = parts[0].shape[0], parts[0].shape[1]
        for index, part in enumerate(parts):
            which = core if index < 2 else 1 - core
            half = far if index % 2 == 0 else 1 - far
            for pair in range(pairs):
                chunk = 2 * (half * pairs + pair) + which
                part[pair] = grad[pl.ds(pl.multiple_of(chunk * size, size), size), :]


def mid_grad_call(groups, mid, joined, block):
    total = mid.shape[0]
    parted = (groups // 4, CAT // groups, HID)
    return pl.pallas_call(
        mid_grad_body,
        grid=(total // block,),
        in_specs=[rows_of(block, HID), rows_of(block, CAT)],
        out_specs=[fixed(parted)] * 4,
        out_shape=[shape(parted, f32)] * 4,
        scratch_shapes=[pltpu.VMEM((CAT, HID), f32)],
        compiler_params=params(),
        cost_estimate=cost(25),
        name="mid_grad",
    )(mid, joined)


def branch_terms(all_rows, scale, window, raw):
    level = raw[WINDOW : WINDOW + 1, :]
    inner = scale * jnp.sum(window.astype(f32) * raw[:WINDOW, :], axis=0, keepdims=True)
    return level / all_rows, scale * (inner / all_rows)


def rows_back_body(
    all_rows,
    counts,
    x_ref,
    part_ref,
    stats_ref,
    window_ref,
    *refs,
):
    out_ref, inner, base, grads = refs[4:]
    step = pl.program_id(0)
    block = x_ref.shape[1]

    @pl.when(step == 0)
    def _():
        gather_quarters(refs[:4], grads)
        stats = add_up(stats_ref)
        for op in range(OPS):
            mean, scale = branch_scale(stats, op, all_rows)
            window = window_ref[op]
            level, slant = branch_terms(
                all_rows, scale, window, grads[op * LANE : (op + 1) * LANE, :HID].astype(f32)
            )
            inner[op] = dot_on((window.astype(f32) * -slant).astype(bf16), window, 1, 1).astype(bf16)
            base[op] = jnp.sum(
                window.astype(f32) * (mean * slant - level), axis=1, keepdims=True
            )

    moved = []
    for op in range(OPS):
        rows = x_ref[op * STRIDE : op * STRIDE + WINDOW, :]
        moved.append(jnp.dot(inner[op], rows, preferred_element_type=f32) + base[op])
    column = step * block + lax.broadcasted_iota(jnp.int32, (1, block), 1)
    valid = column < own_count(counts)

    def write(at, value):
        span = slice(at, at + value.shape[0])
        value = jnp.where(valid, value + part_ref[span, :].astype(f32), 0.0)
        out_ref[span, :] = value.astype(bf16)

    add_windows(moved, write)


def rows_back_call(all_rows, counts, features, part, stats, window, quarters, block):
    total = features.shape[1]
    return pl.pallas_call(
        functools.partial(rows_back_body, all_rows),
        grid_spec=pltpu.PrefetchScalarGridSpec(
            num_scalar_prefetch=1,
            grid=(total // block,),
            in_specs=[
                columns_of(VALID, block),
                columns_of(VALID, block),
                fixed(stats.shape),
                fixed((OPS, WINDOW, HID)),
            ]
            + [fixed(part.shape) for part in quarters],
            out_specs=columns_of(VALID, block),
            scratch_shapes=[
                pltpu.VMEM((OPS, WINDOW, WINDOW), bf16),
                pltpu.VMEM((OPS, WINDOW, 1), f32),
                pltpu.VMEM((OPS * LANE, HID + LANE), bf16),
            ],
        ),
        out_shape=shape((VALID, total), bf16),
        compiler_params=params(),
        cost_estimate=cost(8),
        name="rows_back",
    )(counts, features, part, stats, window, *quarters)


def slots_of(rows, peers):
    return -(-(rows // LANE + 1) // peers)


def first_row(counts, source):
    row = lax.axis_index("row")
    begin = jnp.int32(0)
    for peer in range(counts.shape[1]):
        begin += jnp.where(peer < source, counts[row, peer], 0)
    return begin


def deal_body(counts, logits_ref, out_ref):
    peers = out_ref.shape[0]
    tiles = logits_ref.shape[1] // LANE
    begin = first_row(counts, lax.axis_index("col"))
    count = own_count(counts)
    shift = lax.rem(begin, LANE)
    chunk = begin // LANE
    lane = lax.broadcasted_iota(jnp.int32, (CPAD, LANE), 1)
    empty = jnp.zeros((CPAD, LANE), f32)
    left = empty
    for tile in range(peers * (out_ref.shape[2] // LANE)):
        right = empty
        if tile < tiles:
            piece = logits_ref[:, tile * LANE : (tile + 1) * LANE].astype(f32)
            piece = jnp.where(tile * LANE + lane < count, piece, 0.0)
            right = pltpu.roll(piece, shift, 1)
        slot = tile // peers * LANE
        peer = lax.rem(chunk + tile, peers)
        out_ref[peer, :, slot : slot + LANE] = jnp.where(lane < shift, left, right).astype(bf16)
        left = right


def deal_call(counts, logits, peers):
    total = logits.shape[1]
    dealt = (peers, CPAD, slots_of(total, peers) * LANE)
    return pl.pallas_call(
        deal_body,
        grid_spec=pltpu.PrefetchScalarGridSpec(
            num_scalar_prefetch=1,
            grid=(1,),
            in_specs=[fixed((CPAD, total))],
            out_specs=fixed(dealt),
        ),
        out_shape=shape(dealt, bf16),
        compiler_params=params(),
        cost_estimate=cost(3),
        name="deal_logits",
    )(counts, logits)


def collect_body(counts, dealt_ref, out_ref, held):
    peers, _, width = dealt_ref.shape
    member = lax.axis_index("col")
    held[...] = jnp.zeros_like(held)
    for source in range(peers):
        chunk = first_row(counts, source) // LANE
        ahead = lax.rem(member + peers - lax.rem(chunk, peers), peers)
        at = pl.ds(pl.multiple_of((chunk + ahead) // peers * LANE, LANE), width)
        held[:, at] += dealt_ref[source].astype(f32)
    share = out_ref.shape[2]
    for peer in range(peers):
        out_ref[peer] = held[:, peer * share : (peer + 1) * share].astype(bf16)


def collect_call(counts, dealt):
    peers, height, width = dealt.shape
    collected = (peers, height, AVG // peers)
    return pl.pallas_call(
        collect_body,
        grid_spec=pltpu.PrefetchScalarGridSpec(
            num_scalar_prefetch=1,
            grid=(1,),
            in_specs=[fixed(dealt.shape)],
            out_specs=fixed(collected),
            scratch_shapes=[pltpu.VMEM((height, AVG + LANE + width), f32)],
        ),
        out_shape=shape(collected, bf16),
        compiler_params=params(),
        cost_estimate=cost(3),
        name="collect_logits",
    )(counts, dealt)


def join_body(pieces_ref, out_ref):
    peers, _, share = pieces_ref.shape
    for peer in range(peers):
        for index in range(share // LANE):
            at = (index * peers + peer) * LANE
            piece = pieces_ref[peer, :, index * LANE : (index + 1) * LANE].astype(f32)
            out_ref[:, at : at + LANE] = piece[:CLS, :]


def join_call(pieces):
    return pl.pallas_call(
        join_body,
        out_shape=shape((CLS, AVG), f32),
        compiler_params=params(),
        cost_estimate=cost(2),
        name="join_logits",
    )(pieces)


def moments(turned, first, second):
    new_first = beta_first * first + (1.0 - beta_first) * turned
    new_second = beta_second * second + (1.0 - beta_second) * turned * turned
    direction = (
        new_first
        / (1.0 - beta_first**STEP)
        / (jnp.sqrt(new_second / (1.0 - beta_second**STEP)) + adam_eps)
    )
    return new_first, new_second, direction


def dot_parts(first_arg, second_arg, first_dim, second_dim):
    first_high, first_low = split_low(first_arg)
    second_high, second_low = split_low(second_arg)
    return dot_on(first_high, second_high, first_dim, second_dim) + (
        dot_on(first_high, second_low, first_dim, second_dim)
        + dot_on(first_low, second_high, first_dim, second_dim)
    )


def factor(old, grad, dim):
    low = grad.astype(bf16)
    return beta_factor * old + (1.0 - beta_factor) * dot_on(low, low, dim, dim)


def branch_update_body(all_rows, stats_ref, window_ref, *refs):
    (
        w_ref,
        left_ref,
        right_ref,
        basis_left_ref,
        basis_right_ref,
        first_ref,
        second_ref,
        new_left_ref,
        new_right_ref,
        new_first_ref,
        new_second_ref,
        new_w_ref,
        low_w_ref,
        grad_out_ref,
        grads,
    ) = refs[4:]
    step = pl.program_id(0)

    @pl.when(step == 0)
    def _():
        gather_quarters(refs[:4], grads)
        for op in range(OPS):
            at = op * LANE + WINDOW + 1
            grad_out_ref[op * SHARE : (op + 1) * SHARE, :] = grads[at : at + SHARE, :HID].astype(f32)

    for op in range(OPS):

        @pl.when(step == op)
        def _(op=op):
            mean, scale = branch_scale(add_up(stats_ref), op, all_rows)
            window = window_ref[op]
            raw = grads[op * LANE : (op + 1) * LANE, :HID].astype(f32)
            gram = grads[op * LANE : (op + 1) * LANE, HID:]
            level, slant = branch_terms(all_rows, scale, window, raw)
            normed = jnp.dot(gram, padded(window), preferred_element_type=f32)
            grad = raw[:WINDOW, :] - normed[:WINDOW, :] * slant
            shift = op * (DIN - STRIDE)
            grad = grad[shift : shift + DIN, :]
            new_left_ref[:, op, :] = factor(left_ref[:, op, :], grad, 1)
            new_right_ref[0] = factor(right_ref[0], grad, 0)
            basis_left, basis_right = basis_left_ref[:, op, :], basis_right_ref[0]
            turned = dot_parts(basis_left, grad, 0, 0)
            turned = dot_parts(turned, basis_right, 1, 0)
            new_first, new_second, direction = moments(
                turned, first_ref[:, op, :], second_ref[:, op, :]
            )
            new_first_ref[:, op, :] = new_first
            new_second_ref[:, op, :] = new_second
            back = dot_parts(basis_left, direction, 1, 0)
            back = dot_parts(back, basis_right, 1, 1)
            new_w = w_ref[:, op, :] - rate_branch * back
            new_w_ref[:, op, :] = new_w
            low_w_ref[:, op, :] = new_w.astype(bf16)


def branch_update_call(
    all_rows, stats, window, quarters, w, left, right, basis_left, basis_right, first, second
):
    small, wide = fixed((DIN, OPS, DIN)), fixed((DIN, OPS, HID))
    square = pl.BlockSpec((1, HID, HID), lambda k: (k, 0, 0))
    return pl.pallas_call(
        functools.partial(branch_update_body, all_rows),
        grid=(OPS,),
        in_specs=[fixed(stats.shape), fixed((OPS, WINDOW, HID))]
        + [fixed(part.shape) for part in quarters]
        + [wide, small, square, small, square, wide, wide],
        out_specs=[small, square, wide, wide, wide, wide, fixed((CPAD, HID))],
        out_shape=[
            shape((DIN, OPS, DIN), f32),
            shape((OPS, HID, HID), f32),
            shape((DIN, OPS, HID), f32),
            shape((DIN, OPS, HID), f32),
            shape((DIN, OPS, HID), f32),
            shape((DIN, OPS, HID), bf16),
            shape((CPAD, HID), f32),
        ],
        scratch_shapes=[pltpu.VMEM((OPS * LANE, HID + LANE), bf16)],
        compiler_params=params(VMEM_WHOLE),
        cost_estimate=cost(12),
        name="branch_update",
    )(stats, window, *quarters, w, left, right, basis_left, basis_right, first, second)


def out_update_body(
    grad_ref,
    w_ref,
    left_ref,
    right_ref,
    basis_left_ref,
    basis_right_ref,
    first_ref,
    second_ref,
    new_left_ref,
    new_right_ref,
    new_first_ref,
    new_second_ref,
    new_w_ref,
    low_w_ref,
):
    grad = grad_ref[:CLS, :]
    new_left_ref[...] = factor(left_ref[...], grad, 0)
    new_right_ref[...] = factor(right_ref[...], grad, 1)
    turned = dot_parts(grad, basis_left_ref[...], 1, 0)
    turned = dot_parts(basis_right_ref[...], turned, 0, 0)
    new_first, new_second, direction = moments(turned, first_ref[...], second_ref[...])
    new_first_ref[...] = new_first
    new_second_ref[...] = new_second
    back = dot_parts(direction, basis_left_ref[...], 1, 1)
    back = dot_parts(basis_right_ref[...], back, 1, 0)
    new_w = w_ref[...] - rate_out * back
    new_w_ref[...] = new_w
    low_w_ref[...] = new_w.astype(bf16)


def out_update_call(grad, w, left, right, basis_left, basis_right, first, second):
    return pl.pallas_call(
        out_update_body,
        out_shape=[
            shape((HID, HID), f32),
            shape((CLS, CLS), f32),
            shape((CLS, HID), f32),
            shape((CLS, HID), f32),
            shape((CLS, HID), f32),
            shape((CLS, HID), bf16),
        ],
        compiler_params=params(),
        cost_estimate=cost(4),
        name="out_update",
    )(grad, w, left, right, basis_left, basis_right, first, second)


def mid_update_body(
    grad_ref, w_ref, basis_ref, first_ref, second_ref, new_first_ref, new_second_ref, new_w_ref, low_w_ref
):
    turned = dot_parts(grad_ref[...], basis_ref[...], 1, 0)
    new_first, new_second, direction = moments(turned, first_ref[...], second_ref[...])
    new_first_ref[...] = new_first
    new_second_ref[...] = new_second
    new_w = w_ref[...] - rate_mid * dot_parts(direction, basis_ref[...], 1, 1)
    new_w_ref[...] = new_w
    low_w_ref[...] = new_w.astype(bf16)


def mid_update_call(grad, w, basis, first, second):
    rows = grad.shape[0]
    return pl.pallas_call(
        mid_update_body,
        out_shape=[shape((rows, HID), f32)] * 3 + [shape((rows, HID), bf16)],
        compiler_params=params(),
        cost_estimate=cost(3),
        name="mid_update",
    )(grad, w, basis, first, second)


def half_blocks():
    parts = HID // LANE
    return [(i, j) for i in range(parts) for j in range(i, parts)]


def mid_gram_body(rows_ref, out_ref):
    rows = rows_ref[...]
    gram = dot_on(rows, rows, 0, 0)
    for index, (i, j) in enumerate(half_blocks()):
        out_ref[index] = gram[i * LANE : (i + 1) * LANE, j * LANE : (j + 1) * LANE].astype(bf16)


def mid_gram_call(rows):
    return pl.pallas_call(
        mid_gram_body,
        out_shape=shape((len(half_blocks()), LANE, LANE), bf16),
        compiler_params=params(),
        cost_estimate=cost(2),
        name="mid_gram",
    )(rows)


def mid_factor_body(right_ref, own_ref, near_ref, out_ref):
    for index, (i, j) in enumerate(half_blocks()):
        block = (1.0 - beta_factor) * (own_ref[index] + near_ref[index])
        rows, columns = slice(i * LANE, (i + 1) * LANE), slice(j * LANE, (j + 1) * LANE)
        out_ref[rows, columns] = beta_factor * right_ref[rows, columns] + block
        if i != j:
            out_ref[columns, rows] = beta_factor * right_ref[columns, rows] + block.T


def mid_factor_call(right, own, near):
    return pl.pallas_call(
        mid_factor_body,
        out_shape=shape((HID, HID), f32),
        compiler_params=params(),
        cost_estimate=cost(2),
        name="mid_factor",
    )(right, own, near)


def after(values, *others):
    return lax.optimization_barrier((values,) + others)[0]


def swap(values, axis, distance):
    peers = lax.axis_size(axis)
    return lax.ppermute(values, axis, [(peer, peer ^ distance) for peer in range(peers)])


def swap_both(values, first, second):
    groups, peers = lax.axis_size("row"), lax.axis_size("col")
    away = {"row": 0, "col": 0}
    for axis, distance in (first, second):
        away[axis] ^= distance
    pairs = [
        (row * peers + col, (row ^ away["row"]) * peers + (col ^ away["col"]))
        for row in range(groups)
        for col in range(peers)
    ]
    return lax.ppermute(values, BOTH, pairs)


def in_order(values, other, step):
    axis, distance = step
    bit = lax.rem(lax.axis_index(axis) // distance, 2) > 0
    return jnp.where(
        bit,
        jnp.concatenate([other, values], axis=0),
        jnp.concatenate([values, other], axis=0),
    )


def gather_by_steps(values):
    steps = doubling_steps()
    while len(steps) > 3:
        first, second = steps[:2]
        steps = steps[2:]
        near, far, both = (
            swap(values, *first),
            swap(values, *second),
            swap_both(values, first, second),
        )
        values = in_order(
            in_order(values, near, first), in_order(far, both, first), second
        )
    while len(steps) > 2:
        values = in_order(values, swap(values, *steps[0]), steps[0])
        steps = steps[1:]
    first, second = steps
    return [values, swap(values, *first), swap(values, *second), swap_both(values, first, second)]


def add_all(values):
    while len(values) > 1:
        values = [values[i] + values[i + 1] for i in range(0, len(values), 2)]
    return values[0]


def exchange(values):
    return lax.all_to_all(values, "col", 0, 0, tiled=True)


def spread_out(values, dtype=f32):
    copies = jnp.broadcast_to(values[None], (lax.axis_size("col"),) + values.shape)
    return exchange(copies.astype(dtype))


def far_copies(values):
    pieces = {0: values}
    distance = lax.axis_size("row") // 2
    while distance > 1:
        pieces.update({d ^ distance: swap(v, "row", distance) for d, v in list(pieces.items())})
        distance //= 2
    return pieces


def near_copies(pieces, *others):
    held = lax.optimization_barrier((*[pieces[d] for d in sorted(pieces)], *others))
    pieces = dict(zip(sorted(pieces), held))
    pieces.update({d ^ 1: swap(v, "row", 1) for d, v in list(pieces.items())})
    return [pieces[d] for d in sorted(pieces)], held[len(held) - len(others) :]


def sum_in_row(values):
    return add_all([values] + [swap(values, "row", d) for d in range(1, lax.axis_size("row"))])


def keep_bit(values, distance):
    bit = lax.rem(lax.axis_index("row") // distance, 2)
    pairs = values.reshape((-1, 2) + values.shape[1:])
    kept = lax.dynamic_index_in_dim(pairs, bit, 1, keepdims=False)
    sent = lax.dynamic_index_in_dim(pairs, 1 - bit, 1, keepdims=False)
    return kept, sent


def finish_scatter(values, distance):
    while distance < lax.axis_size("row") // 2:
        kept, sent = keep_bit(values, distance)
        values = kept + swap(sent.astype(bf16), "row", distance).astype(f32)
        distance *= 2
    values = values.reshape((lax.axis_size("col"), -1) + values.shape[2:]).astype(bf16)
    return jnp.sum(exchange(values).astype(f32), axis=0)


def local(
    features,
    labels,
    counts,
    w_branch,
    w_mid,
    w_out,
    left_branch,
    right_branch,
    basis_left_branch,
    basis_right_branch,
    first_branch,
    second_branch,
    right_mid,
    basis_right_mid,
    first_mid,
    second_mid,
    left_out,
    right_out,
    basis_left_out,
    basis_right_out,
    first_out,
    second_out,
):
    groups, peers = lax.axis_size("row"), lax.axis_size("col")
    devices = groups * peers
    all_rows = float(AVG * devices)

    def by_input(values):
        return values.transpose(1, 0, 2)

    turned = features.T
    own_mid = spread_out(w_mid, bf16).reshape(-1, HID)
    window, gram, branch_sums = gram_call(counts, turned, by_input(w_branch), 4096)
    branch_sums = sum_in_row(branch_sums)
    own_mid = after(own_mid, branch_sums)
    pieces = far_copies(own_mid)
    branch_stats = spread_out(branch_sums)
    pieces, (branch_stats,) = near_copies(pieces, branch_stats)
    pre, joined, slope, mid_low, mid_sums = forward_call(
        all_rows, devices, counts, turned, branch_stats, window, pieces, 1024
    )
    mid_stats = lax.all_to_all(mid_sums, BOTH, 0, 0, tiled=True)
    back, logits, grad_out, back_sums = head_call(
        all_rows, counts, pre, mid_stats, w_out.T, labels.reshape(1, -1), 2048
    )
    back_stats = lax.all_to_all(back_sums, BOTH, 0, 0, tiled=True)

    dealt = deal_call(counts, logits, peers)
    back_stats, dealt = lax.optimization_barrier((back_stats, dealt))
    dealt = exchange(dealt)
    mid, part, grad_branch = branch_back_call(
        all_rows,
        devices,
        counts,
        pre,
        back,
        slope,
        turned,
        mid_low,
        window,
        mid_stats,
        back_stats,
        branch_stats,
        grad_out,
        gram,
        1024,
    )
    grad_branch, dealt = lax.optimization_barrier((grad_branch, dealt))
    grad_branch = lax.all_to_all(grad_branch, BOTH, 0, 0, tiled=True)
    parts = mid_grad_call(groups, mid, joined, 1024)
    grad_branch, *parts = lax.optimization_barrier((grad_branch, *parts))
    kept, sent = parts[:2], parts[2:]
    grad_branch = jnp.sum(grad_branch.astype(f32), axis=0).astype(bf16)
    near = [swap(part, "row", 1) for part in sent]
    quarters = [part.reshape(-1, HID + LANE) for part in gather_by_steps(grad_branch)]
    away = (kept[1] + near[1]).astype(bf16)
    far = swap(away, "row", groups // 2)
    grad_mid = finish_scatter(kept[0] + near[0] + far.astype(f32), 2)
    grad_features = rows_back_call(
        all_rows, counts, turned, part, branch_stats, window, quarters, 4096
    )
    collected = collect_call(counts, after(dealt, grad_features))
    grad_mid, grad_features, collected = lax.optimization_barrier(
        (grad_mid, grad_features, collected)
    )
    all_mid = spread_out(grad_mid, bf16).reshape(-1, HID)
    *branch_parts, grad_out = branch_update_call(
        all_rows,
        branch_stats,
        window,
        quarters,
        by_input(w_branch),
        by_input(left_branch),
        right_branch,
        by_input(basis_left_branch),
        basis_right_branch,
        by_input(first_branch),
        by_input(second_branch),
    )
    held = lax.optimization_barrier((all_mid, *branch_parts))
    all_mid, branch_parts = held[0], held[1:]
    collected = exchange(after(collected, all_mid))
    mid_gram = mid_gram_call(all_mid)
    distance = groups // 2
    others = swap(mid_gram, "row", distance)
    mid_parts = mid_update_call(
        after(grad_mid, mid_gram), w_mid, basis_right_mid, first_mid, second_mid
    )
    out_parts = out_update_call(
        after(grad_out, mid_gram),
        w_out.T,
        left_out,
        right_out,
        basis_left_out,
        basis_right_out,
        first_out.T,
        second_out.T,
    )
    mid_gram, others, *held = lax.optimization_barrier(
        (mid_gram, others, *mid_parts, *out_parts)
    )
    mid_parts, out_parts = held[:4], held[4:]
    mid_gram = mid_gram.astype(f32) + others.astype(f32)
    while distance > 2:
        distance //= 2
        mid_gram = mid_gram + swap(mid_gram, "row", distance)
    others = swap(mid_gram, "row", 1)
    new_logits = join_call(after(collected, mid_gram))
    others, new_logits = lax.optimization_barrier((others, new_logits))
    new_right_mid = mid_factor_call(right_mid, mid_gram, others)
    branch_parts = [
        part if index == 1 else by_input(part) for index, part in enumerate(branch_parts)
    ]
    out_parts = list(out_parts[:2]) + [part.T for part in out_parts[2:]]
    return (new_logits.T, grad_features.T, *branch_parts, new_right_mid, *mid_parts, *out_parts)


def solution(mesh):
    split, rows, whole = P(BOTH, None), P(BOTH), P()
    in_specs = (split, rows, whole, whole, split) + (whole,) * 9 + (split, split) + (whole,) * 6
    out_specs = (split, split) + (whole,) * 7 + (split,) * 4 + (whole,) * 6
    return jax.shard_map(local, mesh=mesh, in_specs=in_specs, out_specs=out_specs, check_vma=False)
```

```python
import functools

import jax
import jax.numpy as jnp
from jax import lax
from jax.experimental import pallas as pl
from jax.experimental.pallas import tpu as pltpu
from jax.sharding import PartitionSpec as P

OPS = 4
DIN = 100
HID = 512
CLS = 47
AVG = 4096
STEP = 5
CAT = 2048
LANE = 128
CPAD = 48
STRIDE = 96
WINDOW = 112
VALID = 400
HEAD = 2048
PART = 256
WIDE = 416
SHARE = 12
BOTH = ("row", "col")

beta_first = 0.5
beta_second = 0.9
beta_factor = 0.95
adam_eps = 1e-08
norm_eps = 1e-05
rate_branch = 0.1
rate_mid = 0.02
rate_out = 0.04
f32 = jnp.float32
bf16 = jnp.bfloat16
VMEM_LIMIT = 50 * 2**20
VMEM_WHOLE = 60 * 2**20


def dot_on(first_arg, second_arg, first_dim, second_dim, precision=None):
    return lax.dot_general(
        first_arg,
        second_arg,
        (((first_dim,), (second_dim,)), ((), ())),
        precision=precision,
        preferred_element_type=f32,
    )


def params(limit=VMEM_LIMIT):
    return pltpu.CompilerParams(vmem_limit_bytes=limit)


def cost(microseconds):
    return pl.CostEstimate(
        flops=int(microseconds * 1e9), bytes_accessed=1, transcendentals=0
    )


def shape(dims, dtype):
    return jax.ShapeDtypeStruct(dims, dtype)


def fixed(dims):
    return pl.BlockSpec(dims, lambda *_: (0,) * len(dims))


def rows_of(block, width):
    return pl.BlockSpec((block, width), lambda i, *_: (i, 0))


def columns_of(height, block):
    return pl.BlockSpec((height, block), lambda i, *_: (0, i))


def low_f32(values):
    return values.astype(bf16).astype(f32)


def split_low(values):
    high = values.astype(bf16)
    return high, (values - high.astype(f32)).astype(bf16)


def fold_rows(values):
    return jnp.sum(values.reshape(values.shape[0] // 8, 8, values.shape[1]), axis=0)


def add_up(ref):
    value = ref[0]
    for index in range(1, ref.shape[0]):
        value = value + ref[index]
    return value


def own_count(counts):
    return counts[lax.axis_index("row"), lax.axis_index("col")]


def branch_scale(stats, op, all_rows):
    mean = stats[op : op + 1, :HID] / all_rows
    square = stats[OPS + op : OPS + op + 1, :HID] / all_rows
    return mean, lax.rsqrt(square - mean * mean + norm_eps)


def unpack_pair(packed):
    parts = HID // LANE
    return [
        jnp.concatenate(
            [packed[index * parts + part : index * parts + part + 1, :] for part in range(parts)],
            axis=1,
        )
        for index in range(2)
    ]


def pack_pair(first, second):
    parts = HID // LANE
    return jnp.concatenate(
        [
            value[:, part * LANE : (part + 1) * LANE]
            for value in (first, second)
            for part in range(parts)
        ],
        axis=0,
    )


def mid_scale(stats_ref, all_rows):
    total, square = unpack_pair(add_up(stats_ref))
    mean = total / all_rows
    return mean, lax.rsqrt(square / all_rows - mean * mean + norm_eps)


def window_rows(x_ref, op):
    return jnp.concatenate(
        [x_ref[op * STRIDE : op * STRIDE + WINDOW, :], x_ref[VALID:WIDE, :]], axis=0
    )


def padded(window):
    return jnp.concatenate([window, jnp.zeros((LANE - WINDOW, HID), bf16)], axis=0)


def gram_product(gram, window):
    weight = padded(window)
    product = None
    for _ in range(3):
        part = gram.astype(bf16)
        gram = gram - part.astype(f32)
        term = jnp.dot(part, weight, preferred_element_type=f32)
        product = term if product is None else product + term
    return product


def mask_rows(counts, x_ref, held):
    block = x_ref.shape[1]
    column = pl.program_id(0) * block + lax.broadcasted_iota(jnp.int32, (16, block), 1)
    valid = jnp.where(column < own_count(counts), 1.0, 0.0)
    line = lax.broadcasted_iota(jnp.int32, (16, block), 0)
    held[:VALID, :] = x_ref[...] * valid[0:1, :].astype(bf16)
    held[VALID:, :] = jnp.where(line < 2, valid, 0.0).astype(bf16)


def doubling_steps():
    steps = []
    for axis in ("col", "row"):
        distance = lax.axis_size(axis) // 2
        while distance > 1:
            steps.append((axis, distance))
            distance //= 2
    return steps + [("col", 1), ("row", 1)]


def owned_order(devices):
    peers = lax.axis_size("col")
    order = []
    for device in range(devices):
        place = {"row": device // peers, "col": device % peers}
        bits = [place[axis] // distance % 2 for axis, distance in doubling_steps()]
        order.append(sum(bit << index for index, bit in enumerate(bits)))
    return order


def gather_quarters(refs, held):
    core = lax.rem(lax.axis_index("row"), 2)
    side = lax.rem(lax.axis_index("col"), 2)
    size = refs[0].shape[0]
    for index, ref in enumerate(refs):
        place = (core ^ (index // 2)) * 2 + (side ^ (index % 2))
        held[pl.ds(pl.multiple_of(place * size, size), size), :] = ref[...]


def gather_pieces(refs, held):
    row = lax.axis_index("row")
    size = held.shape[0] // len(refs)
    for index, ref in enumerate(refs):
        at = pl.multiple_of((row ^ index) * size, size)
        held[pl.ds(at, size), :] = ref[...].reshape(size, held.shape[1]).astype(held.dtype)


def gram_body(counts, x_ref, w_ref, window_ref, gram_ref, stats_ref, xa_ref):
    step = pl.program_id(0)

    @pl.when(step == 0)
    def _():
        gram_ref[...] = jnp.zeros_like(gram_ref)
        for op in range(OPS):
            shift = op * (DIN - STRIDE)
            parts = [low_f32(w_ref[:, op, :])]
            if shift:
                parts.insert(0, jnp.zeros((shift, HID), f32))
            if WINDOW - DIN - shift:
                parts.append(jnp.zeros((WINDOW - DIN - shift, HID), f32))
            window_ref[op] = jnp.concatenate(parts, axis=0).astype(bf16)

    mask_rows(counts, x_ref, xa_ref)
    for op in range(0, OPS, 2):
        rows = jnp.concatenate([window_rows(xa_ref, op), window_rows(xa_ref, op + 1)], axis=0)
        both = dot_on(rows, rows, 1, 1)
        gram_ref[op] += both[:LANE, :LANE]
        gram_ref[op + 1] += both[LANE:, LANE:]

    @pl.when(step == pl.num_programs(0) - 1)
    def _():
        for op in range(OPS):
            turned = gram_product(gram_ref[op], window_ref[op])
            stats_ref[op : op + 1, :HID] = turned[WINDOW : WINDOW + 1, :]
            stats_ref[OPS + op : OPS + op + 1, :HID] = jnp.sum(
                window_ref[op].astype(f32) * turned[:WINDOW, :], axis=0, keepdims=True
            )
            stats_ref[op : op + 1, HID:] = gram_ref[op, WINDOW : WINDOW + 1, :]
            stats_ref[OPS + op : OPS + op + 1, HID:] = jnp.zeros((1, LANE), f32)


def gram_call(counts, features, w_branch, block):
    total = features.shape[1]
    return pl.pallas_call(
        gram_body,
        grid_spec=pltpu.PrefetchScalarGridSpec(
            num_scalar_prefetch=1,
            grid=(total // block,),
            in_specs=[columns_of(VALID, block), fixed((DIN, OPS, HID))],
            out_specs=[
                fixed((OPS, WINDOW, HID)),
                fixed((OPS, LANE, LANE)),
                fixed((2 * OPS, HID + LANE)),
            ],
            scratch_shapes=[pltpu.VMEM((WIDE, block), bf16)],
        ),
        out_shape=[
            shape((OPS, WINDOW, HID), bf16),
            shape((OPS, LANE, LANE), f32),
            shape((2 * OPS, HID + LANE), f32),
        ],
        compiler_params=params(),
        cost_estimate=cost(6),
        name="row_moments",
    )(counts, features, w_branch)


def forward_body(all_rows, count, counts, *refs):
    x_ref, stats_ref, window_ref = refs[:3]
    pieces = refs[3 : 3 + count]
    pre_ref, joined_ref, slope_ref, wm_ref, out_ref, wide, total, xa_ref = refs[3 + count :]
    step = pl.program_id(0)

    @pl.when(step == 0)
    def _():
        total[...] = jnp.zeros_like(total)
        gather_pieces(pieces, wm_ref)
        stats = add_up(stats_ref)
        line = lax.broadcasted_iota(jnp.int32, (LANE - WINDOW, HID), 0)
        for op in range(OPS):
            mean, scale = branch_scale(stats, op, all_rows)
            half = 0.5 * scale
            high, low = split_low(window_ref[op].astype(f32) * half)
            base = -mean * half
            base_high = low_f32(base)
            wide[op, :WINDOW, :] = high
            wide[op, WINDOW:LANE, :] = jnp.where(
                line == 0, base_high, jnp.where(line == 1, base - base_high, 0.0)
            ).astype(bf16)
            wide[op, LANE : LANE + WINDOW, :] = low
            wide[op, LANE + WINDOW :, :] = jnp.zeros((LANE - WINDOW, HID), bf16)

    mask_rows(counts, x_ref, xa_ref)
    pre = None
    for op in range(OPS):
        rows = window_rows(xa_ref, op).T
        rows = jnp.concatenate([rows, rows], axis=1)
        for start in range(0, HID, PART):
            half = jnp.dot(
                rows, wide[op, :, start : start + PART], preferred_element_type=f32
            ).astype(bf16)
            first = jnp.tanh(half) + 1.0
            act = half * first
            half_act = act * 0.5
            second = jnp.tanh(half_act) + 1.0
            joined = half_act * second
            slope = (first * ((half - half_act) + 0.5)) * (second * ((act - joined) + 1.0))
            span = slice(op * HID + start, op * HID + start + PART)
            joined_ref[:, span] = joined
            slope_ref[:, span] = slope
            term = jnp.dot(joined, wm_ref[span, :], preferred_element_type=f32)
            pre = term if pre is None else pre + term
    pre_ref[...] = pre
    total[0] += fold_rows(pre)
    total[1] += fold_rows(pre * pre)

    @pl.when(step == pl.num_programs(0) - 1)
    def _():
        packed = pack_pair(
            jnp.sum(total[0], axis=0, keepdims=True), jnp.sum(total[1], axis=0, keepdims=True)
        )
        for index in range(out_ref.shape[0]):
            out_ref[index] = packed


def forward_call(all_rows, devices, counts, features, stats, window, pieces, block):
    total = features.shape[1]
    count = len(pieces)
    return pl.pallas_call(
        functools.partial(forward_body, all_rows, count),
        grid_spec=pltpu.PrefetchScalarGridSpec(
            num_scalar_prefetch=1,
            grid=(total // block,),
            in_specs=[
                columns_of(VALID, block),
                fixed(stats.shape),
                fixed((OPS, WINDOW, HID)),
            ]
            + [fixed(piece.shape) for piece in pieces],
            out_specs=[
                rows_of(block, HID),
                rows_of(block, CAT),
                rows_of(block, CAT),
                fixed((CAT, HID)),
                fixed((devices, 8, LANE)),
            ],
            scratch_shapes=[
                pltpu.VMEM((OPS, 2 * LANE, HID), bf16),
                pltpu.VMEM((2, 8, HID), f32),
                pltpu.VMEM((WIDE, block), bf16),
            ],
        ),
        out_shape=[
            shape((total, HID), f32),
            shape((total, CAT), bf16),
            shape((total, CAT), bf16),
            shape((CAT, HID), bf16),
            shape((devices, 8, LANE), f32),
        ],
        compiler_params=params(),
        cost_estimate=cost(44),
        name="forward_layers",
    )(counts, features, stats, window, *pieces)


def head_body(
    all_rows,
    counts,
    pre_ref,
    stats_ref,
    wo_ref,
    labels_ref,
    back_ref,
    logits_ref,
    grad_ref,
    sums_ref,
    wo_low,
    norm,
    total,
):
    step = pl.program_id(0)
    block = pre_ref.shape[0]

    @pl.when(step == 0)
    def _():
        total[...] = jnp.zeros_like(total)
        grad_ref[...] = jnp.zeros_like(grad_ref)
        wo_low[...] = jnp.concatenate(
            [wo_ref[...], jnp.zeros((CPAD - CLS, HID), f32)], axis=0
        ).astype(bf16)
        mean, scale = mid_scale(stats_ref, all_rows)
        norm[0:1, :] = 0.5 * scale
        norm[1:2, :] = -0.5 * scale * mean

    kind = lax.broadcasted_iota(jnp.int32, (CPAD, HEAD), 0)
    for start in range(0, block, HEAD):
        rows = slice(start, start + HEAD)
        logits = None
        kept = []
        for at in range(0, HID, PART):
            span = slice(at, at + PART)
            half = pre_ref[rows, span] * norm[0:1, span] + norm[1:2, span]
            raised = jnp.tanh(half) + 1.0
            hidden = half * raised
            slope = raised * ((half - 0.5 * hidden) + 0.5)
            hidden = hidden.astype(bf16)
            term = dot_on(wo_low[:, span], hidden, 1, 1)
            logits = term if logits is None else logits + term
            kept.append((span, half, hidden, slope))
        logits_ref[:, rows] = logits.astype(bf16)
        column = step * block + start + lax.broadcasted_iota(jnp.int32, (CPAD, HEAD), 1)
        real = kind < CLS
        top = jnp.max(jnp.where(real, logits, -jnp.inf), axis=0, keepdims=True)
        powers = jnp.where(real, jnp.exp(logits - top), 0.0)
        probs = powers / jnp.sum(powers, axis=0, keepdims=True)
        score = (probs - jnp.where(kind == labels_ref[:, rows], 1.0, 0.0)) / all_rows
        score = jnp.where(column < own_count(counts), score, 0.0).astype(bf16)
        for span, half, hidden, slope in kept:
            grad_ref[:, span] += dot_on(score, hidden, 1, 0)
            back = dot_on(score, wo_low[:, span], 0, 0) * slope
            total[0, :, span] += fold_rows(back)
            total[1, :, span] += fold_rows(back * half)
            back_ref[rows, span] = back.astype(bf16)

    @pl.when(step == pl.num_programs(0) - 1)
    def _():
        packed = pack_pair(
            jnp.sum(total[0], axis=0, keepdims=True),
            2.0 * jnp.sum(total[1], axis=0, keepdims=True),
        )
        for index in range(sums_ref.shape[0]):
            sums_ref[index] = packed


def head_call(all_rows, counts, pre, stats, w_out, labels, block):
    total = pre.shape[0]
    return pl.pallas_call(
        functools.partial(head_body, all_rows),
        grid_spec=pltpu.PrefetchScalarGridSpec(
            num_scalar_prefetch=1,
            grid=(total // block,),
            in_specs=[
                rows_of(block, HID),
                fixed(stats.shape),
                fixed((CLS, HID)),
                columns_of(1, block),
            ],
            out_specs=[
                rows_of(block, HID),
                columns_of(CPAD, block),
                fixed((CPAD, HID)),
                fixed(stats.shape),
            ],
            scratch_shapes=[
                pltpu.VMEM((CPAD, HID), bf16),
                pltpu.VMEM((8, HID), f32),
                pltpu.VMEM((2, 8, HID), f32),
            ],
        ),
        out_shape=[
            shape((total, HID), bf16),
            shape((CPAD, total), bf16),
            shape((CPAD, HID), f32),
            shape(stats.shape, f32),
        ],
        compiler_params=params(),
        cost_estimate=cost(18),
        name="head",
    )(counts, pre, stats, w_out, labels)


def add_windows(pieces, write):
    for op, piece in enumerate(pieces):
        start = op * STRIDE
        skip = WINDOW - STRIDE if op else 0
        stop = WINDOW if op == OPS - 1 else STRIDE
        if op:
            write(start, pieces[op - 1][STRIDE:WINDOW, :] + piece[:skip, :])
        write(start + skip, piece[skip:stop, :])


def branch_back_body(
    all_rows,
    counts,
    pre_ref,
    back_ref,
    slope_ref,
    x_ref,
    wm_ref,
    window_ref,
    mid_stats_ref,
    sums_ref,
    stats_ref,
    grad_out_ref,
    gram_ref,
    mid_ref,
    part_ref,
    all_ref,
    norm,
    halved,
    grad,
    xa_ref,
):
    step = pl.program_id(0)

    @pl.when(step == 0)
    def _():
        grad[...] = jnp.zeros_like(grad)
        stats = add_up(stats_ref)
        for op in range(OPS):
            halved[op : op + 1, :] = 0.5 * branch_scale(stats, op, all_rows)[1]
        mean, scale = mid_scale(mid_stats_ref, all_rows)
        level, slant = unpack_pair(add_up(sums_ref))
        slant = scale * scale * (slant / all_rows)
        norm[0:1, :] = scale
        norm[1:2, :] = slant
        norm[2:3, :] = mean * slant - scale * (level / all_rows)

    mask_rows(counts, x_ref, xa_ref)
    mid = (
        back_ref[...].astype(f32) * norm[0:1, :]
        - pre_ref[...] * norm[1:2, :]
        + norm[2:3, :]
    ).astype(bf16)
    mid_ref[...] = mid
    pieces = []
    for op in range(OPS):
        span = slice(op * HID, (op + 1) * HID)
        joined_back = dot_on(mid, wm_ref[span, :], 1, 1)
        back = (
            (joined_back * halved[op : op + 1, :]) * slope_ref[:, span].astype(f32)
        ).astype(bf16)
        line = slice(op * LANE, (op + 1) * LANE)
        grad[line, :HID] += dot_on(window_rows(xa_ref, op), back, 1, 0)
        pieces.append(dot_on(window_ref[op], back, 1, 1))

    def write(at, value):
        part_ref[at : at + value.shape[0], :] = value.astype(bf16)

    add_windows(pieces, write)

    @pl.when(step == pl.num_programs(0) - 1)
    def _():
        means = add_up(stats_ref)[:, HID:] / all_rows
        means = jnp.where(
            lax.broadcasted_iota(jnp.int32, means.shape, 1) < WINDOW, means, 0.0
        )
        turned = means.T
        for op in range(OPS):
            start = op * LANE
            gram = gram_ref[op]
            mean, column = means[op : op + 1, :], turned[:, op : op + 1]
            sums, count = gram[WINDOW : WINDOW + 1, :], gram[WINDOW:WINDOW + 1, WINDOW : WINDOW + 1]
            gram = gram - column * (sums - count * mean) - gram[:, WINDOW : WINDOW + 1] * mean
            grad[start : start + LANE, HID:] = gram
            level = grad[start + WINDOW : start + WINDOW + 1, :HID]
            grad[start : start + LANE, :HID] = jnp.concatenate(
                [
                    grad[start : start + WINDOW, :HID] - column[:WINDOW] * level,
                    level,
                    grad_out_ref[op * SHARE : (op + 1) * SHARE, :],
                    jnp.zeros((LANE - WINDOW - 1 - SHARE, HID), f32),
                ],
                axis=0,
            )
        size = all_ref.shape[1]
        for index, block_index in enumerate(owned_order(all_ref.shape[0])):
            at = block_index * size
            all_ref[index] = grad[at : at + size, :].astype(bf16)


def branch_back_call(
    all_rows,
    devices,
    counts,
    pre,
    back,
    slope,
    features,
    mid_low,
    window,
    mid_stats,
    sums,
    stats,
    grad_out,
    gram,
    block,
):
    total = pre.shape[0]
    wide = HID + LANE
    parts = (devices, OPS * LANE // devices, wide)
    return pl.pallas_call(
        functools.partial(branch_back_body, all_rows),
        grid_spec=pltpu.PrefetchScalarGridSpec(
            num_scalar_prefetch=1,
            grid=(total // block,),
            in_specs=[
                rows_of(block, HID),
                rows_of(block, HID),
                rows_of(block, CAT),
                columns_of(VALID, block),
                fixed((CAT, HID)),
                fixed((OPS, WINDOW, HID)),
                fixed(mid_stats.shape),
                fixed(sums.shape),
                fixed(stats.shape),
                fixed((CPAD, HID)),
                fixed((OPS, LANE, LANE)),
            ],
            out_specs=[rows_of(block, HID), columns_of(VALID, block), fixed(parts)],
            scratch_shapes=[
                pltpu.VMEM((8, HID), f32),
                pltpu.VMEM((8, HID), f32),
                pltpu.VMEM((OPS * LANE, wide), f32),
                pltpu.VMEM((WIDE, block), bf16),
            ],
        ),
        out_shape=[shape((total, HID), bf16), shape((VALID, total), bf16), shape(parts, bf16)],
        compiler_params=params(),
        cost_estimate=cost(48),
        name="branch_back",
    )(counts, pre, back, slope, features, mid_low, window, mid_stats, sums, stats, grad_out, gram)


def mid_grad_body(mid_ref, joined_ref, *refs):
    step = pl.program_id(0)
    parts, grad = refs[:-1], refs[-1]

    @pl.when(step == 0)
    def _():
        grad[...] = jnp.zeros_like(grad)

    for op in range(OPS):
        span = slice(op * HID, (op + 1) * HID)
        grad[span, :] += dot_on(joined_ref[:, span], mid_ref[...], 0, 0)

    @pl.when(step == pl.num_programs(0) - 1)
    def _():
        groups = lax.axis_size("row")
        row = lax.axis_index("row")
        core, far = lax.rem(row, 2), row // (groups // 2)
        pairs, size = parts[0].shape[0], parts[0].shape[1]
        for index, part in enumerate(parts):
            which = core if index < 2 else 1 - core
            half = far if index % 2 == 0 else 1 - far
            for pair in range(pairs):
                chunk = 2 * (half * pairs + pair) + which
                part[pair] = grad[pl.ds(pl.multiple_of(chunk * size, size), size), :]


def mid_grad_call(groups, mid, joined, block):
    total = mid.shape[0]
    parted = (groups // 4, CAT // groups, HID)
    return pl.pallas_call(
        mid_grad_body,
        grid=(total // block,),
        in_specs=[rows_of(block, HID), rows_of(block, CAT)],
        out_specs=[fixed(parted)] * 4,
        out_shape=[shape(parted, f32)] * 4,
        scratch_shapes=[pltpu.VMEM((CAT, HID), f32)],
        compiler_params=params(),
        cost_estimate=cost(25),
        name="mid_grad",
    )(mid, joined)


def branch_terms(all_rows, scale, window, raw):
    level = raw[WINDOW : WINDOW + 1, :]
    inner = scale * jnp.sum(window.astype(f32) * raw[:WINDOW, :], axis=0, keepdims=True)
    return level / all_rows, scale * (inner / all_rows)


def rows_back_body(
    all_rows,
    counts,
    x_ref,
    part_ref,
    stats_ref,
    window_ref,
    *refs,
):
    out_ref, inner, base, grads = refs[4:]
    step = pl.program_id(0)
    block = x_ref.shape[1]

    @pl.when(step == 0)
    def _():
        gather_quarters(refs[:4], grads)
        stats = add_up(stats_ref)
        for op in range(OPS):
            mean, scale = branch_scale(stats, op, all_rows)
            window = window_ref[op]
            level, slant = branch_terms(
                all_rows, scale, window, grads[op * LANE : (op + 1) * LANE, :HID].astype(f32)
            )
            inner[op] = dot_on((window.astype(f32) * -slant).astype(bf16), window, 1, 1).astype(bf16)
            base[op] = jnp.sum(
                window.astype(f32) * (mean * slant - level), axis=1, keepdims=True
            )

    moved = []
    for op in range(OPS):
        rows = x_ref[op * STRIDE : op * STRIDE + WINDOW, :]
        moved.append(jnp.dot(inner[op], rows, preferred_element_type=f32) + base[op])
    column = step * block + lax.broadcasted_iota(jnp.int32, (1, block), 1)
    valid = column < own_count(counts)

    def write(at, value):
        span = slice(at, at + value.shape[0])
        value = jnp.where(valid, value + part_ref[span, :].astype(f32), 0.0)
        out_ref[span, :] = value.astype(bf16)

    add_windows(moved, write)


def rows_back_call(all_rows, counts, features, part, stats, window, quarters, block):
    total = features.shape[1]
    return pl.pallas_call(
        functools.partial(rows_back_body, all_rows),
        grid_spec=pltpu.PrefetchScalarGridSpec(
            num_scalar_prefetch=1,
            grid=(total // block,),
            in_specs=[
                columns_of(VALID, block),
                columns_of(VALID, block),
                fixed(stats.shape),
                fixed((OPS, WINDOW, HID)),
            ]
            + [fixed(part.shape) for part in quarters],
            out_specs=columns_of(VALID, block),
            scratch_shapes=[
                pltpu.VMEM((OPS, WINDOW, WINDOW), bf16),
                pltpu.VMEM((OPS, WINDOW, 1), f32),
                pltpu.VMEM((OPS * LANE, HID + LANE), bf16),
            ],
        ),
        out_shape=shape((VALID, total), bf16),
        compiler_params=params(),
        cost_estimate=cost(8),
        name="rows_back",
    )(counts, features, part, stats, window, *quarters)


def slots_of(rows, peers):
    return -(-(rows // LANE + 1) // peers)


def first_row(counts, source):
    row = lax.axis_index("row")
    begin = jnp.int32(0)
    for peer in range(counts.shape[1]):
        begin += jnp.where(peer < source, counts[row, peer], 0)
    return begin


def deal_body(counts, logits_ref, out_ref):
    peers = out_ref.shape[0]
    tiles = logits_ref.shape[1] // LANE
    begin = first_row(counts, lax.axis_index("col"))
    count = own_count(counts)
    shift = lax.rem(begin, LANE)
    chunk = begin // LANE
    lane = lax.broadcasted_iota(jnp.int32, (CPAD, LANE), 1)
    empty = jnp.zeros((CPAD, LANE), f32)
    left = empty
    for tile in range(peers * (out_ref.shape[2] // LANE)):
        right = empty
        if tile < tiles:
            piece = logits_ref[:, tile * LANE : (tile + 1) * LANE].astype(f32)
            piece = jnp.where(tile * LANE + lane < count, piece, 0.0)
            right = pltpu.roll(piece, shift, 1)
        slot = tile // peers * LANE
        peer = lax.rem(chunk + tile, peers)
        out_ref[peer, :, slot : slot + LANE] = jnp.where(lane < shift, left, right).astype(bf16)
        left = right


def deal_call(counts, logits, peers):
    total = logits.shape[1]
    dealt = (peers, CPAD, slots_of(total, peers) * LANE)
    return pl.pallas_call(
        deal_body,
        grid_spec=pltpu.PrefetchScalarGridSpec(
            num_scalar_prefetch=1,
            grid=(1,),
            in_specs=[fixed((CPAD, total))],
            out_specs=fixed(dealt),
        ),
        out_shape=shape(dealt, bf16),
        compiler_params=params(),
        cost_estimate=cost(3),
        name="deal_logits",
    )(counts, logits)


def collect_body(counts, dealt_ref, out_ref, held):
    peers, _, width = dealt_ref.shape
    member = lax.axis_index("col")
    held[...] = jnp.zeros_like(held)
    for source in range(peers):
        chunk = first_row(counts, source) // LANE
        ahead = lax.rem(member + peers - lax.rem(chunk, peers), peers)
        at = pl.ds(pl.multiple_of((chunk + ahead) // peers * LANE, LANE), width)
        held[:, at] += dealt_ref[source].astype(f32)
    share = out_ref.shape[2]
    for peer in range(peers):
        out_ref[peer] = held[:, peer * share : (peer + 1) * share].astype(bf16)


def collect_call(counts, dealt):
    peers, height, width = dealt.shape
    collected = (peers, height, AVG // peers)
    return pl.pallas_call(
        collect_body,
        grid_spec=pltpu.PrefetchScalarGridSpec(
            num_scalar_prefetch=1,
            grid=(1,),
            in_specs=[fixed(dealt.shape)],
            out_specs=fixed(collected),
            scratch_shapes=[pltpu.VMEM((height, AVG + LANE + width), f32)],
        ),
        out_shape=shape(collected, bf16),
        compiler_params=params(),
        cost_estimate=cost(3),
        name="collect_logits",
    )(counts, dealt)


def join_body(pieces_ref, out_ref):
    peers, _, share = pieces_ref.shape
    for peer in range(peers):
        for index in range(share // LANE):
            at = (index * peers + peer) * LANE
            piece = pieces_ref[peer, :, index * LANE : (index + 1) * LANE].astype(f32)
            out_ref[:, at : at + LANE] = piece[:CLS, :]


def join_call(pieces):
    return pl.pallas_call(
        join_body,
        out_shape=shape((CLS, AVG), f32),
        compiler_params=params(),
        cost_estimate=cost(2),
        name="join_logits",
    )(pieces)


def moments(turned, first, second):
    new_first = beta_first * first + (1.0 - beta_first) * turned
    new_second = beta_second * second + (1.0 - beta_second) * turned * turned
    direction = (
        new_first
        / (1.0 - beta_first**STEP)
        / (jnp.sqrt(new_second / (1.0 - beta_second**STEP)) + adam_eps)
    )
    return new_first, new_second, direction


def dot_parts(first_arg, second_arg, first_dim, second_dim):
    first_high, first_low = split_low(first_arg)
    second_high, second_low = split_low(second_arg)
    return dot_on(first_high, second_high, first_dim, second_dim) + (
        dot_on(first_high, second_low, first_dim, second_dim)
        + dot_on(first_low, second_high, first_dim, second_dim)
    )


def factor(old, grad, dim):
    low = grad.astype(bf16)
    return beta_factor * old + (1.0 - beta_factor) * dot_on(low, low, dim, dim)


def branch_update_body(all_rows, stats_ref, window_ref, *refs):
    (
        w_ref,
        left_ref,
        right_ref,
        basis_left_ref,
        basis_right_ref,
        first_ref,
        second_ref,
        new_left_ref,
        new_right_ref,
        new_first_ref,
        new_second_ref,
        new_w_ref,
        low_w_ref,
        grad_out_ref,
        grads,
    ) = refs[4:]
    step = pl.program_id(0)

    @pl.when(step == 0)
    def _():
        gather_quarters(refs[:4], grads)
        for op in range(OPS):
            at = op * LANE + WINDOW + 1
            grad_out_ref[op * SHARE : (op + 1) * SHARE, :] = grads[at : at + SHARE, :HID].astype(f32)

    for op in range(OPS):

        @pl.when(step == op)
        def _(op=op):
            mean, scale = branch_scale(add_up(stats_ref), op, all_rows)
            window = window_ref[op]
            raw = grads[op * LANE : (op + 1) * LANE, :HID].astype(f32)
            gram = grads[op * LANE : (op + 1) * LANE, HID:]
            level, slant = branch_terms(all_rows, scale, window, raw)
            normed = jnp.dot(gram, padded(window), preferred_element_type=f32)
            grad = raw[:WINDOW, :] - normed[:WINDOW, :] * slant
            shift = op * (DIN - STRIDE)
            grad = grad[shift : shift + DIN, :]
            new_left_ref[:, op, :] = factor(left_ref[:, op, :], grad, 1)
            new_right_ref[0] = factor(right_ref[0], grad, 0)
            basis_left, basis_right = basis_left_ref[:, op, :], basis_right_ref[0]
            turned = dot_parts(basis_left, grad, 0, 0)
            turned = dot_parts(turned, basis_right, 1, 0)
            new_first, new_second, direction = moments(
                turned, first_ref[:, op, :], second_ref[:, op, :]
            )
            new_first_ref[:, op, :] = new_first
            new_second_ref[:, op, :] = new_second
            back = dot_parts(basis_left, direction, 1, 0)
            back = dot_parts(back, basis_right, 1, 1)
            new_w = w_ref[:, op, :] - rate_branch * back
            new_w_ref[:, op, :] = new_w
            low_w_ref[:, op, :] = new_w.astype(bf16)


def branch_update_call(
    all_rows, stats, window, quarters, w, left, right, basis_left, basis_right, first, second
):
    small, wide = fixed((DIN, OPS, DIN)), fixed((DIN, OPS, HID))
    square = pl.BlockSpec((1, HID, HID), lambda k: (k, 0, 0))
    return pl.pallas_call(
        functools.partial(branch_update_body, all_rows),
        grid=(OPS,),
        in_specs=[fixed(stats.shape), fixed((OPS, WINDOW, HID))]
        + [fixed(part.shape) for part in quarters]
        + [wide, small, square, small, square, wide, wide],
        out_specs=[small, square, wide, wide, wide, wide, fixed((CPAD, HID))],
        out_shape=[
            shape((DIN, OPS, DIN), f32),
            shape((OPS, HID, HID), f32),
            shape((DIN, OPS, HID), f32),
            shape((DIN, OPS, HID), f32),
            shape((DIN, OPS, HID), f32),
            shape((DIN, OPS, HID), bf16),
            shape((CPAD, HID), f32),
        ],
        scratch_shapes=[pltpu.VMEM((OPS * LANE, HID + LANE), bf16)],
        compiler_params=params(VMEM_WHOLE),
        cost_estimate=cost(12),
        name="branch_update",
    )(stats, window, *quarters, w, left, right, basis_left, basis_right, first, second)


def out_update_body(
    grad_ref,
    w_ref,
    left_ref,
    right_ref,
    basis_left_ref,
    basis_right_ref,
    first_ref,
    second_ref,
    new_left_ref,
    new_right_ref,
    new_first_ref,
    new_second_ref,
    new_w_ref,
    low_w_ref,
):
    grad = grad_ref[:CLS, :]
    new_left_ref[...] = factor(left_ref[...], grad, 0)
    new_right_ref[...] = factor(right_ref[...], grad, 1)
    turned = dot_parts(grad, basis_left_ref[...], 1, 0)
    turned = dot_parts(basis_right_ref[...], turned, 0, 0)
    new_first, new_second, direction = moments(turned, first_ref[...], second_ref[...])
    new_first_ref[...] = new_first
    new_second_ref[...] = new_second
    back = dot_parts(direction, basis_left_ref[...], 1, 1)
    back = dot_parts(basis_right_ref[...], back, 1, 0)
    new_w = w_ref[...] - rate_out * back
    new_w_ref[...] = new_w
    low_w_ref[...] = new_w.astype(bf16)


def out_update_call(grad, w, left, right, basis_left, basis_right, first, second):
    return pl.pallas_call(
        out_update_body,
        out_shape=[
            shape((HID, HID), f32),
            shape((CLS, CLS), f32),
            shape((CLS, HID), f32),
            shape((CLS, HID), f32),
            shape((CLS, HID), f32),
            shape((CLS, HID), bf16),
        ],
        compiler_params=params(),
        cost_estimate=cost(4),
        name="out_update",
    )(grad, w, left, right, basis_left, basis_right, first, second)


def mid_update_body(
    grad_ref, w_ref, basis_ref, first_ref, second_ref, new_first_ref, new_second_ref, new_w_ref, low_w_ref
):
    turned = dot_parts(grad_ref[...], basis_ref[...], 1, 0)
    new_first, new_second, direction = moments(turned, first_ref[...], second_ref[...])
    new_first_ref[...] = new_first
    new_second_ref[...] = new_second
    new_w = w_ref[...] - rate_mid * dot_parts(direction, basis_ref[...], 1, 1)
    new_w_ref[...] = new_w
    low_w_ref[...] = new_w.astype(bf16)


def mid_update_call(grad, w, basis, first, second):
    rows = grad.shape[0]
    return pl.pallas_call(
        mid_update_body,
        out_shape=[shape((rows, HID), f32)] * 3 + [shape((rows, HID), bf16)],
        compiler_params=params(),
        cost_estimate=cost(3),
        name="mid_update",
    )(grad, w, basis, first, second)


def half_blocks():
    parts = HID // LANE
    return [(i, j) for i in range(parts) for j in range(i, parts)]


def mid_gram_body(rows_ref, out_ref):
    rows = rows_ref[...]
    gram = dot_on(rows, rows, 0, 0)
    for index, (i, j) in enumerate(half_blocks()):
        out_ref[index] = gram[i * LANE : (i + 1) * LANE, j * LANE : (j + 1) * LANE].astype(bf16)


def mid_gram_call(rows):
    return pl.pallas_call(
        mid_gram_body,
        out_shape=shape((len(half_blocks()), LANE, LANE), bf16),
        compiler_params=params(),
        cost_estimate=cost(2),
        name="mid_gram",
    )(rows)


def mid_factor_body(right_ref, own_ref, near_ref, out_ref):
    for index, (i, j) in enumerate(half_blocks()):
        block = (1.0 - beta_factor) * (own_ref[index] + near_ref[index])
        rows, columns = slice(i * LANE, (i + 1) * LANE), slice(j * LANE, (j + 1) * LANE)
        out_ref[rows, columns] = beta_factor * right_ref[rows, columns] + block
        if i != j:
            out_ref[columns, rows] = beta_factor * right_ref[columns, rows] + block.T


def mid_factor_call(right, own, near):
    return pl.pallas_call(
        mid_factor_body,
        out_shape=shape((HID, HID), f32),
        compiler_params=params(),
        cost_estimate=cost(2),
        name="mid_factor",
    )(right, own, near)


def after(values, *others):
    return lax.optimization_barrier((values,) + others)[0]


def swap(values, axis, distance):
    peers = lax.axis_size(axis)
    return lax.ppermute(values, axis, [(peer, peer ^ distance) for peer in range(peers)])


def swap_both(values, first, second):
    groups, peers = lax.axis_size("row"), lax.axis_size("col")
    away = {"row": 0, "col": 0}
    for axis, distance in (first, second):
        away[axis] ^= distance
    pairs = [
        (row * peers + col, (row ^ away["row"]) * peers + (col ^ away["col"]))
        for row in range(groups)
        for col in range(peers)
    ]
    return lax.ppermute(values, BOTH, pairs)


def in_order(values, other, step):
    axis, distance = step
    bit = lax.rem(lax.axis_index(axis) // distance, 2) > 0
    return jnp.where(
        bit,
        jnp.concatenate([other, values], axis=0),
        jnp.concatenate([values, other], axis=0),
    )


def gather_by_steps(values):
    steps = doubling_steps()
    while len(steps) > 3:
        first, second = steps[:2]
        steps = steps[2:]
        near, far, both = (
            swap(values, *first),
            swap(values, *second),
            swap_both(values, first, second),
        )
        values = in_order(
            in_order(values, near, first), in_order(far, both, first), second
        )
    while len(steps) > 2:
        values = in_order(values, swap(values, *steps[0]), steps[0])
        steps = steps[1:]
    first, second = steps
    return [values, swap(values, *first), swap(values, *second), swap_both(values, first, second)]


def add_all(values):
    while len(values) > 1:
        values = [values[i] + values[i + 1] for i in range(0, len(values), 2)]
    return values[0]


def exchange(values):
    return lax.all_to_all(values, "col", 0, 0, tiled=True)


def spread_out(values, dtype=f32):
    copies = jnp.broadcast_to(values[None], (lax.axis_size("col"),) + values.shape)
    return exchange(copies.astype(dtype))


def far_copies(values):
    pieces = {0: values}
    distance = lax.axis_size("row") // 2
    while distance > 1:
        pieces.update({d ^ distance: swap(v, "row", distance) for d, v in list(pieces.items())})
        distance //= 2
    return pieces


def near_copies(pieces, *others):
    held = lax.optimization_barrier((*[pieces[d] for d in sorted(pieces)], *others))
    pieces = dict(zip(sorted(pieces), held))
    pieces.update({d ^ 1: swap(v, "row", 1) for d, v in list(pieces.items())})
    return [pieces[d] for d in sorted(pieces)], held[len(held) - len(others) :]


def sum_in_row(values):
    return add_all([values] + [swap(values, "row", d) for d in range(1, lax.axis_size("row"))])


def keep_bit(values, distance):
    bit = lax.rem(lax.axis_index("row") // distance, 2)
    pairs = values.reshape((-1, 2) + values.shape[1:])
    kept = lax.dynamic_index_in_dim(pairs, bit, 1, keepdims=False)
    sent = lax.dynamic_index_in_dim(pairs, 1 - bit, 1, keepdims=False)
    return kept, sent


def finish_scatter(values, distance):
    while distance < lax.axis_size("row") // 2:
        kept, sent = keep_bit(values, distance)
        values = kept + swap(sent.astype(bf16), "row", distance).astype(f32)
        distance *= 2
    values = values.reshape((lax.axis_size("col"), -1) + values.shape[2:]).astype(bf16)
    return jnp.sum(exchange(values).astype(f32), axis=0)


def local(
    features,
    labels,
    counts,
    w_branch,
    w_mid,
    w_out,
    left_branch,
    right_branch,
    basis_left_branch,
    basis_right_branch,
    first_branch,
    second_branch,
    right_mid,
    basis_right_mid,
    first_mid,
    second_mid,
    left_out,
    right_out,
    basis_left_out,
    basis_right_out,
    first_out,
    second_out,
):
    groups, peers = lax.axis_size("row"), lax.axis_size("col")
    devices = groups * peers
    all_rows = float(AVG * devices)

    def by_input(values):
        return values.transpose(1, 0, 2)

    turned = features.T
    own_mid = spread_out(w_mid, bf16).reshape(-1, HID)
    window, gram, branch_sums = gram_call(counts, turned, by_input(w_branch), 4096)
    branch_sums = sum_in_row(branch_sums)
    own_mid = after(own_mid, branch_sums)
    pieces = far_copies(own_mid)
    branch_stats = spread_out(branch_sums)
    pieces, (branch_stats,) = near_copies(pieces, branch_stats)
    pre, joined, slope, mid_low, mid_sums = forward_call(
        all_rows, devices, counts, turned, branch_stats, window, pieces, 1024
    )
    mid_stats = lax.all_to_all(mid_sums, BOTH, 0, 0, tiled=True)
    back, logits, grad_out, back_sums = head_call(
        all_rows, counts, pre, mid_stats, w_out.T, labels.reshape(1, -1), 2048
    )
    back_stats = lax.all_to_all(back_sums, BOTH, 0, 0, tiled=True)

    dealt = deal_call(counts, logits, peers)
    back_stats, dealt = lax.optimization_barrier((back_stats, dealt))
    dealt = exchange(dealt)
    mid, part, grad_branch = branch_back_call(
        all_rows,
        devices,
        counts,
        pre,
        back,
        slope,
        turned,
        mid_low,
        window,
        mid_stats,
        back_stats,
        branch_stats,
        grad_out,
        gram,
        1024,
    )
    grad_branch, dealt = lax.optimization_barrier((grad_branch, dealt))
    grad_branch = lax.all_to_all(grad_branch, BOTH, 0, 0, tiled=True)
    parts = mid_grad_call(groups, mid, joined, 1024)
    grad_branch, *parts = lax.optimization_barrier((grad_branch, *parts))
    kept, sent = parts[:2], parts[2:]
    grad_branch = jnp.sum(grad_branch.astype(f32), axis=0).astype(bf16)
    near = [swap(part, "row", 1) for part in sent]
    away = (kept[1] + near[1]).astype(bf16)
    grad_branch, away = lax.optimization_barrier((grad_branch, away))
    quarters = [part.reshape(-1, HID + LANE) for part in gather_by_steps(grad_branch)]
    far = swap(away, "row", groups // 2)
    base = after(kept[0] + near[0], away)
    grad_mid = finish_scatter(base + far.astype(f32), 2)
    grad_features = rows_back_call(
        all_rows, counts, turned, part, branch_stats, window, quarters, 4096
    )
    collected = collect_call(counts, after(dealt, grad_features))
    grad_mid, grad_features, collected = lax.optimization_barrier(
        (grad_mid, grad_features, collected)
    )
    all_mid = spread_out(grad_mid, bf16).reshape(-1, HID)
    *branch_parts, grad_out = branch_update_call(
        all_rows,
        branch_stats,
        window,
        quarters,
        by_input(w_branch),
        by_input(left_branch),
        right_branch,
        by_input(basis_left_branch),
        basis_right_branch,
        by_input(first_branch),
        by_input(second_branch),
    )
    held = lax.optimization_barrier((all_mid, *branch_parts))
    all_mid, branch_parts = held[0], held[1:]
    collected = exchange(after(collected, all_mid))
    mid_gram = mid_gram_call(all_mid)
    distance = groups // 2
    others = swap(mid_gram, "row", distance)
    mid_parts = mid_update_call(
        after(grad_mid, mid_gram), w_mid, basis_right_mid, first_mid, second_mid
    )
    out_parts = out_update_call(
        after(grad_out, mid_gram),
        w_out.T,
        left_out,
        right_out,
        basis_left_out,
        basis_right_out,
        first_out.T,
        second_out.T,
    )
    mid_gram, others, *held = lax.optimization_barrier(
        (mid_gram, others, *mid_parts, *out_parts)
    )
    mid_parts, out_parts = held[:4], held[4:]
    mid_gram = mid_gram.astype(f32) + others.astype(f32)
    while distance > 2:
        distance //= 2
        mid_gram = mid_gram + swap(mid_gram, "row", distance)
    others = swap(mid_gram, "row", 1)
    new_logits = join_call(after(collected, mid_gram))
    others, new_logits = lax.optimization_barrier((others, new_logits))
    new_right_mid = mid_factor_call(right_mid, mid_gram, others)
    branch_parts = [
        part if index == 1 else by_input(part) for index, part in enumerate(branch_parts)
    ]
    out_parts = list(out_parts[:2]) + [part.T for part in out_parts[2:]]
    return (new_logits.T, grad_features.T, *branch_parts, new_right_mid, *mid_parts, *out_parts)


def solution(mesh):
    split, rows, whole = P(BOTH, None), P(BOTH), P()
    in_specs = (split, rows, whole, whole, split) + (whole,) * 9 + (split, split) + (whole,) * 6
    out_specs = (split, split) + (whole,) * 7 + (split,) * 4 + (whole,) * 6
    return jax.shard_map(local, mesh=mesh, in_specs=in_specs, out_specs=out_specs, check_vma=False)
```
